128 devices in a mesh: lon: 8 (over x, y_lo), sample: 16 (over y_hi, z, core).
Axes of the slice: x: 4, y: 4 (y_hi: 2, y_lo: 2; y = y_hi * 2 + y_lo), z: 4, core: 2. Of those that a mesh axis runs over, the one named last changes fastest.
Arguments:
- ocean_state: bfloat16 [16, 192, 128, 128], P('sample', None, 'lon'), may hold values from -6 to 6
- cotangent: bfloat16 [16, 192, 128, 128], P('sample', None, 'lon'), may hold values from -6 to 6
- land_sea: int32 [128, 128], P('lon'), may hold values 0 or 1
- kernel: float32 [192, 7, 7], replicated, may hold values from -0.875 to 0.875
- norm_gain: float32 [192], replicated, may hold values from 0.1 to 1.9
- in_weight: bfloat16 [192, 768], replicated, may hold values from -0.4375 to 0.4375
- out_weight: bfloat16 [768, 192], replicated, may hold values from -0.21875 to 0.21875
Outputs:
- state_out: bfloat16 [16, 192, 128, 128], P('sample', None, 'lon')
- grad_input: bfloat16 [16, 192, 128, 128], P('sample', None, 'lon')
- grad_in_weight: float32 [192, 768], P('sample')
- grad_out_weight: float32 [768, 192], P(None, 'sample')
- grad_kernel: float32 [192, 7, 7], P('sample')
- grad_gain: float32 [192], P('sample')
The draws below stay inside these ranges and needn't reach their ends.
All inputs are finite; a program needn't handle non-finite values. No bound on the sum of `land_sea` on one device may be relied on, other than what follows from the above.
Results may differ from the reference program's by a relative error of at most 0.0056.
Values may be sent and summed in bfloat16 or wider, within the bound.
A program may use at most 128 MiB of HBM per device.

```python
import math
import jax
import jax.numpy as jnp
from jax import lax

C = 192
HID = 768
LAT = 128
NS = 16
NLON = 128


def plant(values, stream_key, least, largest):
    spot = [jax.random.randint(jax.random.fold_in(stream_key, axis), (), 0, length) for axis, length in enumerate(values.shape)]
    longest = values.shape.index(max(values.shape))
    beside = spot[:longest] + [(spot[longest] + 1) % values.shape[longest]] + spot[longest + 1:]
    return values.at[tuple(spot)].set(least).at[tuple(beside)].set(largest)


def with_spikes(array, own_key, source, target, blocks, factor):
    owner, partner = [(jnp.arange(array.shape[axis_at]) // (array.shape[axis_at] // blocks)).reshape([-1 if axis == axis_at else 1 for axis in range(array.ndim)]) for axis_at in (source, target)]
    chosen = jax.random.permutation(own_key, blocks)[partner]
    strong = (owner == chosen) | (owner == (partner + blocks // 2) % blocks)
    return jnp.where(strong, factor * array, array)


def block_scale(stream_key, dims, shards, smallest, largest):
    factor_of = 1.0
    for dim, shards_of in shards:
        draws = jax.random.uniform(jax.random.fold_in(jax.random.fold_in(stream_key, 6), dim), (shards_of,), jnp.float32, smallest / len(shards), largest / len(shards))
        factor_of = factor_of * jnp.repeat(jnp.exp(draws), dims[dim] // shards_of).reshape((-1,) + (1,) * (len(dims) - 1 - dim))
    return factor_of


def bell_draw(own_key, shape, scale, bound, pieces=(), held_as=jnp.bfloat16):
    values = jax.random.normal(own_key, shape, jnp.float32) * scale
    if len(pieces) > 0:
        values = block_scale(own_key, shape, pieces, -0.22, 0.18) * values
    return jnp.clip(values, min=-bound, max=bound).astype(held_as)


def gaussian_with(own_key, shape, deviation, most, cuts, heavy, dtype=jnp.bfloat16):
    values = deviation * jax.random.normal(own_key, shape, jnp.float32)
    if cuts:
        values = values * block_scale(own_key, shape, cuts, -0.22, 0.18)
    return jnp.clip(with_spikes(values, jax.random.fold_in(own_key, 3), *heavy), -most, most).astype(dtype)


def setup_inputs(seed: int = 0) -> dict:
    keys = jax.random.split(jax.random.key(seed), 8)
    return {
        "ocean_state": bell_draw(keys[0], (NS, C, NLON, LAT), 1.0, 6.0, ((0, 16), (2, 8))),
        "cotangent": gaussian_with(keys[1], (NS, C, NLON, LAT), 1.0, 6.0, ((0, 16), (2, 8)), (0, 1, 16, 2.0)),
        "land_sea": plant((jax.random.randint(keys[2], (NLON, LAT), 0, 10) < 7).astype(jnp.int32), jax.random.fold_in(keys[2], 1), 0, 1),
        "kernel": bell_draw(keys[3], (C, 7, 7), 49 ** -0.5, 0.875, (), jnp.float32),
        "norm_gain": jnp.clip(1.0 + 0.18 * jax.random.normal(keys[4], (C,), jnp.float32), 0.1, 1.9),
        "in_weight": bell_draw(keys[5], (C, HID), C ** -0.5, 0.4375),
        "out_weight": bell_draw(keys[6], (HID, C), HID ** -0.5, 0.21875),
    }


def smooth_gate(values):
    return jax.nn.gelu(values, approximate=True)

def depthwise(padded, kernel, lon_cols, lat_rows):
    result = jnp.zeros(padded.shape[:-2] + (lon_cols, lat_rows), jnp.float32)
    for a in range(7):
        for b in range(7):
            result = result + kernel[:, a, b][:, None, None] * padded[..., a:a + lon_cols, b:b + lat_rows].astype(jnp.float32)
    return result

def transposed(padded, kernel, lon_cols, lat_rows):
    result = jnp.zeros(padded.shape[:-2] + (lon_cols, lat_rows), jnp.float32)
    for a in range(7):
        for b in range(7):
            result = result + kernel[:, a, b][:, None, None] * padded[..., 6 - a:6 - a + lon_cols, 6 - b:6 - b + lat_rows]
    return result

def kernel_grads(grad_conv, padded, lon_cols, lat_rows, sum_axes):
    rows_list = []
    for a in range(7):
        for b in range(7):
            rows_list.append(lax.optimization_barrier(jnp.sum(grad_conv * padded[..., a:a + lon_cols, b:b + lat_rows].astype(jnp.float32), axis=sum_axes)))
    return jnp.stack(rows_list, axis=1).reshape(-1, 7, 7)

def normalize(mixed_conv):
    average = lax.optimization_barrier(jnp.mean(mixed_conv, axis=-3, keepdims=True))
    centred = mixed_conv - average
    variance = lax.optimization_barrier(jnp.mean(centred * centred, axis=-3, keepdims=True))
    inv_scale = lax.rsqrt(variance + 1e-06)
    return (centred * inv_scale, inv_scale)

def norm_backward(grad_normed, scaled, inv_scale, norm_gain):
    grad_scaled = grad_normed * norm_gain[:, None, None]
    first = lax.optimization_barrier(jnp.mean(grad_scaled, axis=-3, keepdims=True))
    second = lax.optimization_barrier(jnp.mean(grad_scaled * scaled, axis=-3, keepdims=True))
    return inv_scale * (grad_scaled - first - scaled * second)

def feed_pieces(norm_block, grad_block, in_weight, out_weight):
    preact = jnp.dot(in_weight.T, norm_block, preferred_element_type=jnp.float32)
    hidden_f, pull_back = jax.vjp(smooth_gate, preact)
    hidden = hidden_f.astype(jnp.bfloat16)
    branch = jnp.dot(out_weight.T, hidden, preferred_element_type=jnp.float32)
    grad_hidden = jnp.dot(out_weight, grad_block, preferred_element_type=jnp.float32)
    grad_preact = pull_back(grad_hidden)[0].astype(jnp.bfloat16)
    out_term = jnp.dot(hidden, grad_block.T, preferred_element_type=jnp.float32)
    in_term = jnp.dot(norm_block, grad_preact.T, preferred_element_type=jnp.float32)
    grad_normed = jnp.dot(in_weight, grad_preact, preferred_element_type=jnp.float32)
    return (branch, grad_normed, in_term, out_term)

def wrap_pad(field):
    joined = jnp.concatenate([field[:, -3:], field, field[:, :3]], axis=1)
    return jnp.pad(joined, ((0, 0), (0, 0), (3, 3)))

def reference(ocean_state, cotangent, land_sea, kernel, norm_gain, in_weight, out_weight):
    ocean_mask = land_sea.astype(jnp.float32)

    def one_sample(totals, inputs):
        state, grad_out = inputs
        padded = wrap_pad(state)
        mixed_conv = depthwise(padded, kernel, NLON, LAT)
        scaled, inv_scale = normalize(mixed_conv)
        normed = (scaled * norm_gain[:, None, None]).astype(jnp.bfloat16)
        grad_branch = (grad_out.astype(jnp.float32) * ocean_mask).astype(jnp.bfloat16)
        branch, grad_normed, in_term, out_term = feed_pieces(normed.reshape(C, -1), grad_branch.reshape(C, -1), in_weight, out_weight)
        branch = branch.reshape(C, NLON, LAT)
        grad_normed = grad_normed.reshape(C, NLON, LAT)
        result_state = (ocean_mask * (state.astype(jnp.float32) + branch)).astype(jnp.bfloat16)
        gain_term = lax.optimization_barrier(jnp.sum(grad_normed * scaled, axis=(1, 2)))
        grad_conv = norm_backward(grad_normed, scaled, inv_scale, norm_gain)
        grad_pad = wrap_pad(grad_conv)
        grad_in = (grad_branch.astype(jnp.float32) + transposed(grad_pad, kernel, NLON, LAT)).astype(jnp.bfloat16)
        kernel_term = kernel_grads(grad_conv, padded, NLON, LAT, (1, 2))
        totals = (totals[0] + in_term, totals[1] + out_term, totals[2] + kernel_term, totals[3] + gain_term)
        return (totals, (result_state, grad_in))
    start = (jnp.zeros((C, HID), jnp.float32), jnp.zeros((HID, C), jnp.float32), jnp.zeros((C, 7, 7), jnp.float32), jnp.zeros((C,), jnp.float32))
    totals, outputs = lax.scan(one_sample, start, (ocean_state, cotangent))
    norm_factor = 1.0 / math.sqrt(NS * NLON * LAT)
    return (outputs[0], outputs[1], totals[0] * norm_factor, totals[1] * norm_factor, totals[2] * norm_factor, totals[3] * norm_factor)
```

```python
import functools
import math

import jax
import jax.numpy as jnp
from jax import lax
from jax.experimental import pallas as pl
from jax.experimental.pallas import tpu as pltpu
from jax.sharding import PartitionSpec as P

C = 192
HID = 768
LON = 16
LAT = 128
TAPS = 7
HALO = 3
GROUP = 4
TILE = 16
OWN = 12
PACKED = 1152
BF = jnp.bfloat16
F32 = jnp.float32
MESH = pl.DeviceIdType.MESH


def tree_sum(terms):
    while len(terms) > 1:
        paired = [terms[k] + terms[k + 1] for k in range(0, len(terms) - 1, 2)]
        if len(terms) % 2:
            paired.append(terms[-1])
        terms = paired
    return terms[0]


def matmul(left, right):
    return jnp.dot(left, right, preferred_element_type=F32)


def matmul_nt(left, right):
    return lax.dot_general(left, right, (((1,), (1,)), ((), ())), preferred_element_type=F32)


def one_hot(condition):
    return jnp.where(condition, 1.0, 0.0).astype(BF)


def column(ref, at):
    return ref[pl.ds(at, C, stride=LON), :]


def kernel_body(
    n_lon,
    n_sample,
    factor,
    state_ref,
    cot_ref,
    sea_ref,
    taps_ref,
    gain_ref,
    win_ref,
    wout_ref,
    sout_ref,
    gin_ref,
    gwin_ref,
    gwout_ref,
    gk_ref,
    gg_ref,
    x32,
    c32,
    xa,
    ga,
    xf,
    kb,
    kf,
    flat_taps,
    spread_to,
    mixed_buf,
    gainb,
    win_t,
    wout_t,
    shift_b,
    shift_g,
    pick,
    ybuf,
    gshift,
    prod,
    hid_buf,
    gp_buf,
    acc_in,
    acc_out,
    acc_gain,
    dks,
    stage,
    wsend,
    wcore,
    wmid,
    wparts,
    wslab,
    ksend,
    kcore,
    kmid,
    kparts,
    kslab,
    send,
    recv,
):
    remote = n_lon > 1
    if remote:
        lon = lax.axis_index("lon")
        sample = lax.axis_index("sample")
        core = lax.rem(sample, 2)
        owner = sample // 2
        n_own = n_sample // 2
        partner = {"sample": sample + 1 - 2 * core}
        right = {"lon": lax.rem(lon + 1, n_lon)}
        left = {"lon": lax.rem(lon + n_lon - 1, n_lon)}
        owners = [lax.rem(owner + d, n_own) for d in range(1, n_own)]
        slabs = [lax.rem(lon + d, n_lon) for d in range(1, n_lon)]
        peers = (
            [partner]
            + [{"sample": 2 * other + core} for other in owners]
            + [{"lon": other} for other in slabs]
        )
        barrier = pltpu.get_barrier_semaphore()
        for peer in peers:
            pl.semaphore_signal(barrier, inc=1, device_id=peer, device_id_type=MESH)

        def copy(src, dst, slot, peer):
            return pltpu.make_async_remote_copy(
                src_ref=src,
                dst_ref=dst,
                send_sem=send.at[slot],
                recv_sem=recv.at[slot],
                device_id=peer,
                device_id_type=MESH,
            )

    def halo_copies(ref, slot):
        return (
            copy(ref.at[pl.ds(LON, HALO)], ref.at[pl.ds(0, HALO)], slot, right),
            copy(ref.at[pl.ds(HALO, HALO)], ref.at[pl.ds(LON + HALO, HALO)], slot + 1, left),
        )

    def local_halo(ref):
        ref[0:HALO] = ref[LON : LON + HALO]
        ref[LON + HALO : LON + 2 * HALO] = ref[HALO : 2 * HALO]

    x32[...] = state_ref[...].astype(F32).reshape(C * LON, LAT)
    for i in (13, 14, 15, 0, 1, 2):
        own = column(x32, i)
        xf[HALO + i] = own
        xa[HALO + i] = own.astype(BF)
    if remote:
        pl.semaphore_wait(barrier, len(peers))
        x_halo = halo_copies(xa, 0)
        for one in x_halo:
            one.start()
    for i in range(3, 13):
        own = column(x32, i)
        xf[HALO + i] = own
        xa[HALO + i] = own.astype(BF)
    c32[...] = cot_ref[...].astype(F32).reshape(C * LON, LAT)

    taps = TAPS * TAPS
    flat_taps[...] = jnp.zeros_like(flat_taps)
    for a in range(TAPS):
        flat_taps[:, 8 * a : 8 * a + TAPS] = taps_ref[:, a, :]
    rest = flat_taps[...]
    pieces = []
    for _ in range(3):
        piece = rest.astype(BF)
        pieces.append(piece)
        rest = rest - piece.astype(F32)
    split = jnp.concatenate(pieces, axis=1)
    place = lax.broadcasted_iota(jnp.int32, (3 * LAT, LAT), 0) % LAT
    for a in range(TAPS):
        for b in range(TAPS):
            t = a * TAPS + b
            spread_to[:, t * LAT : (t + 1) * LAT] = one_hot(place == 8 * a + b)
    kf[...] = matmul(split, spread_to[...])
    for t in range(taps):
        kb[t] = kf[:, t * LAT : (t + 1) * LAT].astype(BF)
    gainb[...] = jnp.broadcast_to(gain_ref[...], (LAT, C)).T
    win_t[...] = win_ref[...].T
    wout_t[...] = wout_ref[...].T
    rows = lax.broadcasted_iota(jnp.int32, (LAT, LAT), 0)
    lanes = lax.broadcasted_iota(jnp.int32, (LAT, LAT), 1)
    for b in range(TAPS):
        backward = one_hot(rows == lanes - (b - HALO))
        shift_b[b * LAT : (b + 1) * LAT, :] = backward
        shift_g[:, b * LAT : (b + 1) * LAT] = backward
    for t in range(TAPS * TAPS + 1):
        pick[t * LAT : (t + 1) * LAT, :] = one_hot(lanes == t)

    acc_in[...] = jnp.zeros_like(acc_in)
    acc_out[...] = jnp.zeros_like(acc_out)
    acc_gain[...] = jnp.zeros_like(acc_gain)

    def filtered(field, col, flip, shifts):
        def one_tile(tile, carry):
            at = pl.multiple_of(tile * TILE, TILE)
            window = field[pl.ds(col, GROUP + 2 * HALO), pl.ds(at, TILE), :]
            for b in range(TAPS):
                terms = []
                for a in range(TAPS):
                    first = 2 * HALO - a if flip else a
                    weight = kb[a * TAPS + b, pl.ds(at, TILE), :]
                    terms.append(weight[None] * window[first : first + GROUP])
                ybuf[:, pl.ds(at, TILE), b * LAT : (b + 1) * LAT] = tree_sum(terms)
            return carry

        lax.fori_loop(0, C // TILE, one_tile, 0)
        flat = ybuf[...].reshape(GROUP * C, TAPS * LAT)
        return matmul(flat, shifts[...]).reshape(GROUP, C, LAT)

    def filtered_exact(col):
        lane = lax.broadcasted_iota(jnp.int32, (GROUP, 8, LAT), 2)

        def one_tile(tile, carry):
            at = pl.multiple_of(tile * 8, 8)
            window = xf[pl.ds(col, GROUP + 2 * HALO), pl.ds(at, 8), :]
            total = None
            for b in range(TAPS):
                terms = [
                    kf[pl.ds(at, 8), (a * TAPS + b) * LAT : (a * TAPS + b + 1) * LAT][None]
                    * window[a : a + GROUP]
                    for a in range(TAPS)
                ]
                part = tree_sum(terms)
                by = b - HALO
                if by != 0:
                    turned = pltpu.roll(part, (-by) % LAT, axis=2)
                    inside = lane < LAT - by if by > 0 else lane >= -by
                    part = jnp.where(inside, turned, 0.0)
                total = part if total is None else total + part
            mixed_buf[:, pl.ds(at, 8), :] = total
            return carry

        lax.fori_loop(0, C // 8, one_tile, 0)
        return mixed_buf[...]

    def masks(col):
        return [sea_ref[pl.ds(col + k, 1), :].astype(F32) for k in range(GROUP)]

    def side_by_side(parts):
        return jnp.concatenate([parts[k] for k in range(GROUP)], axis=1)

    def forward_group(col):
        mixed = filtered_exact(col)
        centred = mixed - jnp.mean(mixed, axis=1, keepdims=True)
        variance = jnp.mean(centred * centred, axis=1, keepdims=True)
        inv_scale = lax.rsqrt(variance + 1e-06)
        scaled = centred * inv_scale
        gain = gainb[...]
        normed = side_by_side((scaled * gain[None]).astype(BF))
        mask = masks(col)
        grad_out = side_by_side([(column(c32, col + k) * mask[k]).astype(BF) for k in range(GROUP)])
        block = 128
        for h in range(0, HID, block):
            pre = matmul(win_t[h : h + block, :], normed)
            grad_hidden = matmul(wout_ref[h : h + block, :], grad_out)
            square = pre * pre
            inner = pre * (0.7978845608028654 + 0.035677408136300125 * square)
            gate = 0.5 + 0.5 * jnp.tanh(inner)
            hidden = pre * gate
            slope = gate + hidden * (1.0 - gate) * (
                1.5957691216057308 + 0.21406444881780074 * square
            )
            hid_buf[h : h + block, :] = hidden.astype(BF)
            gp_buf[h : h + block, :] = (grad_hidden * slope).astype(BF)
        branch = matmul(wout_t[...], hid_buf[...])
        grad_normed = matmul(win_ref[...], gp_buf[...])
        acc_out[...] += matmul_nt(grad_out, hid_buf[...])
        acc_in[...] += matmul_nt(normed, gp_buf[...])
        for k in range(GROUP):
            lane = slice(k * LAT, (k + 1) * LAT)
            at = pl.ds(col + k, C, stride=LON)
            x32[at, :] = mask[k] * (x32[at, :] + branch[:, lane])
            grad = grad_normed[:, lane]
            product = grad * scaled[k]
            acc_gain[...] += product
            grad_scaled = grad * gain
            first = jnp.mean(grad_scaled, axis=0, keepdims=True)
            second = jnp.mean(product * gain, axis=0, keepdims=True)
            grad_conv = inv_scale[k] * (grad_scaled - first - scaled[k] * second)
            ga[HALO + col + k] = grad_conv.astype(BF)

    def fill_halo():
        for i in (0, 1, 2, 19, 20, 21):
            xf[i] = xa[i].astype(F32)

    def one_group(step, carry):
        if remote:

            @pl.when(step == 2)
            def _():
                for one in x_halo:
                    one.wait()
                fill_halo()

        forward_group(lax.rem(GROUP + step * GROUP, LON))
        return carry

    if not remote:
        local_halo(xa)
        fill_halo()
    lax.fori_loop(0, LON // GROUP, one_group, 0)

    if remote:
        g_halo = halo_copies(ga, 2)
        for one in g_halo:
            one.start()
    else:
        local_halo(ga)

    for o in range(16):
        at = OWN * o
        wide = HID // 2
        stage[o, 0:12, 0:HID] = acc_in[at : at + 12, :]
        stage[o, 12:16, 0:HID] = acc_out[at : at + 4, :]
        stage[o, 0:8, HID:PACKED] = acc_out[at + 4 : at + 12, 0:wide]
        stage[o, 8:16, HID:PACKED] = acc_out[at + 4 : at + 12, wide:HID]
    for o in range(16):
        wsend[o % 2, o // 2] = stage[o].astype(BF)

    def reduction(base, packed, from_core, middle, parts, slab, kind):
        def core_copy():
            return copy(packed.at[1 - core], from_core, base, partner)

        def owner_copies():
            return [
                copy(middle.at[other], parts.at[d], base + 1 + d, {"sample": 2 * other + core})
                for d, other in enumerate(owners)
            ]

        def slab_copies():
            return [
                copy(slab.at[lon], slab.at[lon], base + 1 + len(owners) + d, {"lon": other})
                for d, other in enumerate(slabs)
            ]

        def start_core():
            core_copy().start()

        def start_owners():
            core_copy().wait()
            middle[...] = (packed[core].astype(F32) + from_core[...].astype(F32)).astype(kind)
            for one in owner_copies():
                one.start()

        def start_slabs():
            for one in owner_copies():
                one.wait()
            total = middle[owner].astype(F32)
            for d in range(len(owners)):
                total = total + parts[d].astype(F32)
            slab[lon] = total.astype(kind)
            for one in slab_copies():
                one.start()

        def finish():
            for one in slab_copies():
                one.wait()
            total = slab[0].astype(F32)
            for other in range(1, n_lon):
                total = total + slab[other].astype(F32)
            return total * factor

        return start_core, start_owners, start_slabs, finish

    if remote:
        w_core, w_owners, w_slabs, w_finish = reduction(
            4, wsend, wcore, wmid, wparts, wslab, BF
        )
        k_core, k_owners, k_slabs, k_finish = reduction(
            19, ksend, kcore, kmid, kparts, kslab, F32
        )
        w_core()

    def shifted(i, carry):
        gshift[i] = matmul(ga[HALO + i], shift_g[...]).astype(BF)
        return carry

    lax.fori_loop(0, LON, shifted, 0)
    if remote:
        w_owners()

    def products(tile, carry):
        at = pl.multiple_of(tile * TILE, TILE)
        for b in range(TAPS):
            grads = gshift[:, pl.ds(at, TILE), b * LAT : (b + 1) * LAT]
            for a in range(TAPS):
                field = xa[a : a + LON, pl.ds(at, TILE), :]
                terms = grads * field
                t = a * TAPS + b
                prod[pl.ds(at, TILE), t * LAT : (t + 1) * LAT] = tree_sum(
                    [terms[k] for k in range(LON)]
                )
        return carry

    lax.fori_loop(0, C // TILE, products, 0)
    prod[:, TAPS * TAPS * LAT :] = acc_gain[...].astype(BF)
    dks[0:C, :] = matmul(prod[...], pick[...])
    dks[C : C + 16, :] = jnp.zeros((16, LAT), F32)
    for o in range(16):
        ksend[o % 2, o // 2] = dks[OWN * o : OWN * o + 16, :]
    if remote:
        k_core()

    def backward_group(col):
        spread = filtered(ga, col, True, shift_b)
        mask = masks(col)
        for k in range(GROUP):
            at = pl.ds(col + k, C, stride=LON)
            c32[at, :] = c32[at, :] * mask[k] + spread[k]

    def one_back(step, carry):
        backward_group(lax.rem(GROUP + step * GROUP, LON))
        return carry

    if remote:
        w_slabs()
    lax.fori_loop(0, 2, one_back, 0)
    if remote:
        k_owners()
        for one in g_halo:
            one.wait()
    lax.fori_loop(2, 4, one_back, 0)
    if remote:
        k_slabs()
    sout_ref[...] = x32[...].reshape(C, LON, LAT).astype(BF)
    gin_ref[...] = c32[...].reshape(C, LON, LAT).astype(BF)
    if remote:
        weights = w_finish()
        small = k_finish()
    else:
        weights = wsend[0, 0].astype(F32) * factor
        small = ksend[0, 0] * factor
    wide = HID // 2
    gwin_ref[...] = weights[0:12, 0:HID]
    stage[0, 0:4, 0:HID] = weights[12:16, 0:HID]
    stage[0, 4:12, 0:wide] = weights[0:8, HID:PACKED]
    stage[0, 4:12, wide:HID] = weights[8:16, HID:PACKED]
    gwout_ref[...] = stage[0, :, 0:HID].T[:, 0:OWN]
    for a in range(TAPS):
        gk_ref[:, a, :] = small[0:OWN, a * TAPS : (a + 1) * TAPS]
    gg_ref[...] = small.T[TAPS * TAPS : TAPS * TAPS + 1, 0:OWN]


def block(n_lon, n_sample, factor, state, cot, sea, taps, gain, win, wout):
    vmem = pl.BlockSpec(memory_space=pltpu.VMEM)
    shape = jax.ShapeDtypeStruct
    outs = (
        shape((C, LON, LAT), BF),
        shape((C, LON, LAT), BF),
        shape((OWN, HID), F32),
        shape((HID, OWN), F32),
        shape((OWN, TAPS, TAPS), F32),
        shape((1, OWN), F32),
    )
    scratch = [
        pltpu.VMEM((C * LON, LAT), F32),
        pltpu.VMEM((C * LON, LAT), F32),
        pltpu.VMEM((LON + 2 * HALO, C, LAT), BF),
        pltpu.VMEM((LON + 2 * HALO, C, LAT), BF),
        pltpu.VMEM((LON + 2 * HALO, C, LAT), F32),
        pltpu.VMEM((TAPS * TAPS, C, LAT), BF),
        pltpu.VMEM((C, TAPS * TAPS * LAT), F32),
        pltpu.VMEM((C, LAT), F32),
        pltpu.VMEM((3 * LAT, TAPS * TAPS * LAT), BF),
        pltpu.VMEM((GROUP, C, LAT), F32),
        pltpu.VMEM((C, LAT), F32),
        pltpu.VMEM((HID, C), BF),
        pltpu.VMEM((C, HID), BF),
        pltpu.VMEM((TAPS * LAT, LAT), BF),
        pltpu.VMEM((LAT, TAPS * LAT), BF),
        pltpu.VMEM(((TAPS * TAPS + 1) * LAT, LAT), BF),
        pltpu.VMEM((GROUP, C, TAPS * LAT), BF),
        pltpu.VMEM((LON, C, TAPS * LAT), BF),
        pltpu.VMEM((C, (TAPS * TAPS + 1) * LAT), BF),
        pltpu.VMEM((HID, GROUP * LAT), BF),
        pltpu.VMEM((HID, GROUP * LAT), BF),
        pltpu.VMEM((C, HID), F32),
        pltpu.VMEM((C, HID), F32),
        pltpu.VMEM((C, LAT), F32),
        pltpu.VMEM((C + 16, LAT), F32),
        pltpu.VMEM((16, 16, PACKED), F32),
        pltpu.VMEM((2, 8, 16, PACKED), BF),
        pltpu.VMEM((8, 16, PACKED), BF),
        pltpu.VMEM((8, 16, PACKED), BF),
        pltpu.VMEM((7, 16, PACKED), BF),
        pltpu.VMEM((8, 16, PACKED), BF),
        pltpu.VMEM((2, 8, 16, LAT), F32),
        pltpu.VMEM((8, 16, LAT), F32),
        pltpu.VMEM((8, 16, LAT), F32),
        pltpu.VMEM((7, 16, LAT), F32),
        pltpu.VMEM((8, 16, LAT), F32),
        pltpu.SemaphoreType.DMA((34,)),
        pltpu.SemaphoreType.DMA((34,)),
    ]
    extra = dict(collective_id=0, has_side_effects=True) if n_lon > 1 else {}
    return pl.pallas_call(
        functools.partial(kernel_body, n_lon, n_sample, factor),
        out_shape=outs,
        in_specs=[vmem] * 7,
        out_specs=(vmem,) * 6,
        scratch_shapes=scratch,
        compiler_params=pltpu.CompilerParams(vmem_limit_bytes=60 * 1024 * 1024, **extra),
    )(
        state.reshape(C, LON, LAT),
        cot.reshape(C, LON, LAT),
        sea,
        taps,
        gain.reshape(1, C),
        win,
        wout,
    )


def solution(mesh):
    n_lon, n_sample = mesh.shape["lon"], mesh.shape["sample"]
    factor = 1.0 / math.sqrt(n_sample * n_lon * LON * LAT)

    def on_device(state, cot, sea, taps, gain, win, wout):
        out = block(n_lon, n_sample, factor, state, cot, sea, taps, gain, win, wout)
        shape = state.shape
        return (
            out[0].reshape(shape),
            out[1].reshape(shape),
            out[2],
            out[3],
            out[4],
            out[5].reshape(OWN),
        )

    slab = P("sample", None, "lon", None)
    return jax.shard_map(
        on_device,
        mesh=mesh,
        in_specs=(slab, slab, P("lon", None), P(), P(), P(), P()),
        out_specs=(
            slab,
            slab,
            P("sample", None),
            P(None, "sample"),
            P("sample", None, None),
            P("sample"),
        ),
        check_vma=False,
    )
```

```python
import functools
import math

import jax
import jax.numpy as jnp
import numpy as np
from jax import lax
from jax.experimental import pallas as pl
from jax.experimental.pallas import tpu as pltpu
from jax.sharding import PartitionSpec as P

C = 192
HID = 768
LON = 16
LAT = 128
PERIOD = 131
SPEC = 256
TAPS = 7
HALO = 3
GROUP = 4
TILE = 16
OWN = 12
PACKED = 1152
BF = jnp.bfloat16
F32 = jnp.float32
MESH = pl.DeviceIdType.MESH


def tree_sum(terms):
    while len(terms) > 1:
        paired = [terms[k] + terms[k + 1] for k in range(0, len(terms) - 1, 2)]
        if len(terms) % 2:
            paired.append(terms[-1])
        terms = paired
    return terms[0]


def matmul(left, right):
    return jnp.dot(left, right, preferred_element_type=F32)


def matmul_nt(left, right):
    return lax.dot_general(left, right, (((1,), (1,)), ((), ())), preferred_element_type=F32)


def split_constant(values):
    high = values.astype(BF)
    low = (values - high.astype(np.float64)).astype(BF)
    return high, low


def spectral_constants():
    angle = 2.0 * math.pi / PERIOD
    row = np.arange(LAT)
    field_f, field_b = np.zeros((LAT, SPEC)), np.zeros((LAT, SPEC))
    back_f, back_b = np.zeros((SPEC, LAT)), np.zeros((SPEC, LAT))
    taps = np.zeros((8, SPEC))
    shift = np.arange(TAPS) - HALO
    field_f[:, 0] = field_b[:, 0] = 1.0
    back_f[0] = back_b[0] = 1.0 / PERIOD
    taps[:TAPS, 0] = 1.0
    half = PERIOD // 2
    for f in range(1, half + 1):
        one, two, three = f, half + f, 2 * half + f
        cos, sin = np.cos(angle * f * row), np.sin(angle * f * row)
        c, d = np.cos(angle * f * shift), np.sin(angle * f * shift)
        taps[:TAPS, one], taps[:TAPS, two], taps[:TAPS, three] = c, d - c, c + d
        field_f[:, one], field_f[:, two], field_f[:, three] = cos - sin, cos, -sin
        field_b[:, one], field_b[:, two], field_b[:, three] = cos + sin, cos, sin
        scale = 2.0 / PERIOD
        back_f[one], back_f[two], back_f[three] = scale * (cos - sin), -scale * sin, -scale * cos
        back_b[one], back_b[two], back_b[three] = scale * (cos + sin), scale * sin, -scale * cos

    def stacked(values):
        return np.concatenate(split_constant(values), axis=0)

    def beside(values):
        return np.concatenate(split_constant(values), axis=1)

    spread_high, spread_low = np.zeros((64, TAPS * SPEC)), np.zeros((64, TAPS * SPEC))
    high, low = split_constant(taps)
    for a in range(TAPS):
        spread_high[8 * a : 8 * a + 8, a * SPEC : (a + 1) * SPEC] = high
        spread_low[8 * a : 8 * a + 8, a * SPEC : (a + 1) * SPEC] = low
    spread = np.concatenate([spread_high, spread_high, spread_low]).astype(BF)
    gather = np.zeros((SPEC, LAT))
    gather[:, :8] = taps.T
    return (
        stacked(field_f),
        np.concatenate([stacked(back_f.T), stacked(field_b)], axis=1),
        beside(back_f),
        beside(back_b),
        spread,
        beside(gather),
    )


def column(ref, at):
    return ref[pl.ds(at, C, stride=LON), :]


def kernel_body(
    n_lon,
    n_sample,
    factor,
    state_ref,
    cot_ref,
    sea_ref,
    taps_ref,
    gain_ref,
    win_ref,
    wout_t,
    field_f,
    field_g,
    back_f,
    back_b,
    spread,
    gather,
    sout_ref,
    gin_ref,
    gwin_ref,
    gwout_ref,
    gk_ref,
    gg_ref,
    x32,
    c32,
    xa,
    ga,
    xh,
    gh,
    gw,
    kf,
    dkf,
    flat_taps,
    sum_high,
    sum_low,
    gainb,
    win_t,
    wout,
    hid_buf,
    gp_buf,
    acc_in,
    acc_out,
    acc_gain,
    dks,
    stage,
    wsend,
    wcore,
    wmid,
    wparts,
    wslab,
    ksend,
    kcore,
    kmid,
    kparts,
    kslab,
    send,
    recv,
):
    remote = n_lon > 1
    if remote:
        lon = lax.axis_index("lon")
        sample = lax.axis_index("sample")
        core = lax.rem(sample, 2)
        owner = sample // 2
        n_own = n_sample // 2
        partner = {"sample": sample + 1 - 2 * core}
        right = {"lon": lax.rem(lon + 1, n_lon)}
        left = {"lon": lax.rem(lon + n_lon - 1, n_lon)}
        owners = [lax.rem(owner + d, n_own) for d in range(1, n_own)]
        slabs = [lax.rem(lon + d, n_lon) for d in range(1, n_lon)]
        peers = (
            [partner]
            + [{"sample": 2 * other + core} for other in owners]
            + [{"lon": other} for other in slabs]
        )
        barrier = pltpu.get_barrier_semaphore()
        for peer in peers:
            pl.semaphore_signal(barrier, inc=1, device_id=peer, device_id_type=MESH)

        def copy(src, dst, slot, peer):
            return pltpu.make_async_remote_copy(
                src_ref=src,
                dst_ref=dst,
                send_sem=send.at[slot],
                recv_sem=recv.at[slot],
                device_id=peer,
                device_id_type=MESH,
            )

    def halo_copies(ref, slot):
        return (
            copy(ref.at[pl.ds(LON, HALO)], ref.at[pl.ds(0, HALO)], slot, right),
            copy(ref.at[pl.ds(HALO, HALO)], ref.at[pl.ds(LON + HALO, HALO)], slot + 1, left),
        )

    def local_halo(ref):
        ref[0:HALO] = ref[LON : LON + HALO]
        ref[LON + HALO : LON + 2 * HALO] = ref[HALO : 2 * HALO]

    x32[...] = state_ref[...].astype(F32).reshape(C * LON, LAT)
    for i in (13, 14, 15, 0, 1, 2):
        own = column(x32, i)
        xa[HALO + i] = own.astype(BF)
    if remote:
        pl.semaphore_wait(barrier, len(peers))
        x_halo = halo_copies(xa, 0)
        for one in x_halo:
            one.start()
    for i in range(3, 13):
        own = column(x32, i)
        xa[HALO + i] = own.astype(BF)
    c32[...] = cot_ref[...].astype(F32).reshape(C * LON, LAT)

    flat_taps[...] = jnp.zeros_like(flat_taps)
    for a in range(TAPS):
        flat_taps[8 * a : 8 * a + TAPS, 0:C] = taps_ref[a]
    rest = flat_taps[...].T[0:C, :]
    high = rest.astype(BF)
    low = (rest - high.astype(F32)).astype(BF)
    kf[...] = matmul(
        jnp.concatenate([high[:, 0:64], low[:, 0:64], high[:, 0:64]], axis=1), spread[...]
    )
    gainb[...] = jnp.broadcast_to(gain_ref[...], (LAT, C)).T
    win_t[...] = win_ref[...].T
    wout[...] = wout_t[...].T
    acc_in[...] = jnp.zeros_like(acc_in)
    acc_out[...] = jnp.zeros_like(acc_out)
    acc_gain[...] = jnp.zeros_like(acc_gain)

    def doubled(columns):
        flat = columns.reshape(-1, LAT)
        return jnp.concatenate([flat, flat], axis=1)

    def field_spectrum(at, count):
        spectrum = matmul(doubled(xa[at : at + count]), field_f[...])
        xh[at : at + count] = spectrum.reshape(count, C, SPEC)

    def grad_spectrum(at, count):
        spectrum = matmul(doubled(ga[at : at + count]), field_g[:, SPEC:])
        gh[at : at + count] = spectrum.reshape(count, C, SPEC)

    def filtered(field, col, flip, inverse):
        def one_tile(tile, carry):
            at = pl.multiple_of(tile * TILE, TILE)
            for half in range(0, SPEC, LAT):
                window = field[pl.ds(col, GROUP + 2 * HALO), pl.ds(at, TILE), half : half + LAT]
                terms = []
                for a in range(TAPS):
                    first = 2 * HALO - a if flip else a
                    lane = a * SPEC + half
                    weight = kf[pl.ds(at, TILE), lane : lane + LAT]
                    terms.append(weight[None] * window[first : first + GROUP])
                total = tree_sum(terms)
                high = total.astype(BF)
                sum_high[:, pl.ds(at, TILE), half : half + LAT] = high
                sum_low[:, pl.ds(at, TILE), half : half + LAT] = (
                    total - high.astype(F32)
                ).astype(BF)
            return carry

        lax.fori_loop(0, C // TILE, one_tile, 0)
        main = matmul(sum_high[...].reshape(GROUP * C, SPEC), inverse[...])
        rest = matmul(sum_low[...].reshape(GROUP * C, SPEC), inverse[:, 0:LAT])
        return (main[:, 0:LAT] + main[:, LAT:] + rest).reshape(GROUP, C, LAT)

    def masks(col):
        return [sea_ref[pl.ds(col + k, 1), :].astype(F32) for k in range(GROUP)]

    def side_by_side(parts):
        return jnp.concatenate([parts[k] for k in range(GROUP)], axis=1)

    def forward_group(col):
        mixed = filtered(xh, col, False, back_f)
        centred = mixed - jnp.mean(mixed, axis=1, keepdims=True)
        variance = jnp.mean(centred * centred, axis=1, keepdims=True)
        inv_scale = lax.rsqrt(variance + 1e-06)
        scaled = centred * inv_scale
        gain = gainb[...]
        normed = side_by_side((scaled * gain[None]).astype(BF))
        mask = masks(col)
        grad_out = side_by_side([(column(c32, col + k) * mask[k]).astype(BF) for k in range(GROUP)])
        block = 128
        for h in range(0, HID, block):
            pre = matmul(win_t[h : h + block, :], normed)
            grad_hidden = matmul(wout[h : h + block, :], grad_out)
            square = pre * pre
            inner = pre * (0.7978845608028654 + 0.035677408136300125 * square)
            gate = 0.5 + 0.5 * jnp.tanh(inner)
            hidden = pre * gate
            slope = gate + hidden * (1.0 - gate) * (
                1.5957691216057308 + 0.21406444881780074 * square
            )
            hid_buf[h : h + block, :] = hidden.astype(BF)
            gp_buf[h : h + block, :] = (grad_hidden * slope).astype(BF)
        branch = matmul(wout_t[...], hid_buf[...])
        grad_normed = matmul(win_ref[...], gp_buf[...])
        acc_out[...] += matmul_nt(grad_out, hid_buf[...])
        acc_in[...] += matmul_nt(normed, gp_buf[...])
        for k in range(GROUP):
            lane = slice(k * LAT, (k + 1) * LAT)
            at = pl.ds(col + k, C, stride=LON)
            x32[at, :] = mask[k] * (x32[at, :] + branch[:, lane])
            grad = grad_normed[:, lane]
            product = grad * scaled[k]
            acc_gain[...] += product
            grad_scaled = grad * gain
            first = jnp.mean(grad_scaled, axis=0, keepdims=True)
            second = jnp.mean(product * gain, axis=0, keepdims=True)
            grad_conv = inv_scale[k] * (grad_scaled - first - scaled[k] * second)
            grad_conv = grad_conv.astype(BF)
            ga[HALO + col + k] = grad_conv
            spectrum = matmul(doubled(grad_conv), field_g[...])
            gw[col + k] = spectrum[:, 0:SPEC]
            gh[HALO + col + k] = spectrum[:, SPEC:]

    def fill_halo():
        field_spectrum(0, HALO)
        field_spectrum(LON + HALO, HALO)

    def one_group(step, carry):
        if remote:

            @pl.when(step == 2)
            def _():
                for one in x_halo:
                    one.wait()
                fill_halo()

        forward_group(lax.rem(GROUP + step * GROUP, LON))
        return carry

    for at in range(HALO, LON + HALO, GROUP):
        field_spectrum(at, GROUP)
    if not remote:
        local_halo(xa)
        fill_halo()
    lax.fori_loop(0, LON // GROUP, one_group, 0)

    if remote:
        g_halo = halo_copies(ga, 2)
        for one in g_halo:
            one.start()
    else:
        local_halo(ga)
        grad_spectrum(0, HALO)
        grad_spectrum(LON + HALO, HALO)

    for o in range(16):
        at = OWN * o
        wide = HID // 2
        stage[o, 0:12, 0:HID] = acc_in[at : at + 12, :]
        stage[o, 12:16, 0:HID] = acc_out[at : at + 4, :]
        stage[o, 0:8, HID:PACKED] = acc_out[at + 4 : at + 12, 0:wide]
        stage[o, 8:16, HID:PACKED] = acc_out[at + 4 : at + 12, wide:HID]
    for o in range(16):
        wsend[o % 2, o // 2] = stage[o].astype(BF)

    def reduction(base, packed, from_core, middle, parts, slab, kind):
        def core_copy():
            return copy(packed.at[1 - core], from_core, base, partner)

        def owner_copies():
            return [
                copy(middle.at[other], parts.at[d], base + 1 + d, {"sample": 2 * other + core})
                for d, other in enumerate(owners)
            ]

        def slab_copies():
            return [
                copy(slab.at[lon], slab.at[lon], base + 1 + len(owners) + d, {"lon": other})
                for d, other in enumerate(slabs)
            ]

        def start_core():
            core_copy().start()

        def start_owners():
            core_copy().wait()
            middle[...] = (packed[core].astype(F32) + from_core[...].astype(F32)).astype(kind)
            for one in owner_copies():
                one.start()

        def start_slabs():
            for one in owner_copies():
                one.wait()
            total = middle[owner].astype(F32)
            for d in range(len(owners)):
                total = total + parts[d].astype(F32)
            slab[lon] = total.astype(kind)
            for one in slab_copies():
                one.start()

        def finish():
            for one in slab_copies():
                one.wait()
            total = slab[0].astype(F32)
            for other in range(1, n_lon):
                total = total + slab[other].astype(F32)
            return total * factor

        return start_core, start_owners, start_slabs, finish

    if remote:
        w_core, w_owners, w_slabs, w_finish = reduction(
            4, wsend, wcore, wmid, wparts, wslab, BF
        )
        k_core, k_owners, k_slabs, k_finish = reduction(
            19, ksend, kcore, kmid, kparts, kslab, F32
        )
        w_core()

    if remote:
        w_owners()

    def products(tile, carry):
        at = pl.multiple_of(tile * 8, 8)
        for half in range(0, SPEC, LAT):
            grads = gw[:, pl.ds(at, 8), half : half + LAT]
            for a in range(TAPS):
                terms = grads * xh[a : a + LON, pl.ds(at, 8), half : half + LAT]
                lane = a * SPEC + half
                dkf[pl.ds(at, 8), lane : lane + LAT] = jnp.sum(terms, axis=0)
        return carry

    lax.fori_loop(0, C // 8, products, 0)
    lanes = lax.broadcasted_iota(jnp.int32, (C, LAT), 1)
    total = jnp.where(lanes == TAPS * TAPS, jnp.sum(acc_gain[...], axis=1, keepdims=True), 0.0)
    for a in range(TAPS):
        part = dkf[:, a * SPEC : (a + 1) * SPEC]
        high = part.astype(BF)
        low = (part - high.astype(F32)).astype(BF)
        both = matmul(high, gather[...])
        found = both[:, 0:LAT] + both[:, LAT:] + matmul(low, gather[:, 0:LAT])
        total = total + (pltpu.roll(found, a * TAPS, axis=1) if a else found)
    dks[0:C, :] = total
    dks[C : C + 16, :] = jnp.zeros((16, LAT), F32)
    for o in range(16):
        ksend[o % 2, o // 2] = dks[OWN * o : OWN * o + 16, :]
    if remote:
        k_core()

    def backward_group(col):
        moved = filtered(gh, col, True, back_b)
        mask = masks(col)
        for k in range(GROUP):
            at = pl.ds(col + k, C, stride=LON)
            c32[at, :] = c32[at, :] * mask[k] + moved[k]

    def one_back(step, carry):
        backward_group(lax.rem(GROUP + step * GROUP, LON))
        return carry

    if remote:
        w_slabs()
    lax.fori_loop(0, 2, one_back, 0)
    if remote:
        k_owners()
        for one in g_halo:
            one.wait()
        grad_spectrum(0, HALO)
        grad_spectrum(LON + HALO, HALO)
    lax.fori_loop(2, 4, one_back, 0)
    if remote:
        k_slabs()
    sout_ref[...] = x32[...].reshape(C, LON, LAT).astype(BF)
    gin_ref[...] = c32[...].reshape(C, LON, LAT).astype(BF)
    if remote:
        weights = w_finish()
        small = k_finish()
    else:
        weights = wsend[0, 0].astype(F32) * factor
        small = ksend[0, 0] * factor
    wide = HID // 2
    gwin_ref[...] = weights[0:12, 0:HID]
    gwout_ref[0:4, :] = weights[12:16, 0:HID]
    gwout_ref[4:12, 0:wide] = weights[0:8, HID:PACKED]
    gwout_ref[4:12, wide:HID] = weights[8:16, HID:PACKED]
    small_t = small.T
    for a in range(TAPS):
        gk_ref[a] = small_t[a * TAPS : (a + 1) * TAPS, 0:OWN]
    gg_ref[...] = small_t[TAPS * TAPS : TAPS * TAPS + 1, 0:OWN]


def deliver(*refs):
    count = len(refs) // 3
    sems = refs[-1]
    sources, targets, held = refs[:count], refs[count : 2 * count], refs[2 * count : 3 * count]
    arrive = [pltpu.make_async_copy(sources[k], held[k], sems.at[0, k]) for k in range(count)]
    leave = [pltpu.make_async_copy(held[k], targets[k], sems.at[1, k]) for k in range(count)]
    for one in arrive:
        one.start()
    for k in range(count):
        arrive[k].wait()
        leave[k].start()
    for one in leave:
        one.wait()


def block(n_lon, n_sample, factor, state, cot, sea, taps, gain, win, wout):
    vmem = pl.BlockSpec(memory_space=pltpu.VMEM)
    shape = jax.ShapeDtypeStruct
    outs = (
        shape((C, LON, LAT), BF),
        shape((C, LON, LAT), BF),
        shape((OWN, HID), F32),
        shape((OWN, HID), F32),
        shape((TAPS, TAPS, OWN), F32),
        shape((1, OWN), F32),
    )
    scratch = [
        pltpu.VMEM((C * LON, LAT), F32),
        pltpu.VMEM((C * LON, LAT), F32),
        pltpu.VMEM((LON + 2 * HALO, C, LAT), BF),
        pltpu.VMEM((LON + 2 * HALO, C, LAT), BF),
        pltpu.VMEM((LON + 2 * HALO, C, SPEC), F32),
        pltpu.VMEM((LON + 2 * HALO, C, SPEC), F32),
        pltpu.VMEM((LON, C, SPEC), F32),
        pltpu.VMEM((C, TAPS * SPEC), F32),
        pltpu.VMEM((C, TAPS * SPEC), F32),
        pltpu.VMEM((LAT, 2 * LAT), F32),
        pltpu.VMEM((GROUP, C, SPEC), BF),
        pltpu.VMEM((GROUP, C, SPEC), BF),
        pltpu.VMEM((C, LAT), F32),
        pltpu.VMEM((HID, C), BF),
        pltpu.VMEM((HID, C), BF),
        pltpu.VMEM((HID, GROUP * LAT), BF),
        pltpu.VMEM((HID, GROUP * LAT), BF),
        pltpu.VMEM((C, HID), F32),
        pltpu.VMEM((C, HID), F32),
        pltpu.VMEM((C, LAT), F32),
        pltpu.VMEM((C + 16, LAT), F32),
        pltpu.VMEM((16, 16, PACKED), F32),
        pltpu.VMEM((2, 8, 16, PACKED), BF),
        pltpu.VMEM((8, 16, PACKED), BF),
        pltpu.VMEM((8, 16, PACKED), BF),
        pltpu.VMEM((7, 16, PACKED), BF),
        pltpu.VMEM((8, 16, PACKED), BF),
        pltpu.VMEM((2, 8, 16, LAT), F32),
        pltpu.VMEM((8, 16, LAT), F32),
        pltpu.VMEM((8, 16, LAT), F32),
        pltpu.VMEM((7, 16, LAT), F32),
        pltpu.VMEM((8, 16, LAT), F32),
        pltpu.SemaphoreType.DMA((34,)),
        pltpu.SemaphoreType.DMA((34,)),
    ]
    extra = dict(collective_id=0, has_side_effects=True) if n_lon > 1 else {}
    results = pl.pallas_call(
        functools.partial(kernel_body, n_lon, n_sample, factor),
        out_shape=outs,
        in_specs=[vmem] * 13,
        out_specs=(vmem,) * 6,
        scratch_shapes=scratch,
        compiler_params=pltpu.CompilerParams(vmem_limit_bytes=60 * 1024 * 1024, **extra),
    )(
        state.reshape(C, LON, LAT),
        cot.reshape(C, LON, LAT),
        sea,
        taps.transpose(1, 2, 0),
        gain.reshape(1, C),
        win,
        wout.T,
        *spectral_constants(),
    )
    anywhere = pl.BlockSpec(memory_space=pl.ANY)
    return pl.pallas_call(
        deliver,
        out_shape=outs,
        in_specs=[anywhere] * 6,
        out_specs=(anywhere,) * 6,
        scratch_shapes=[pltpu.VMEM(out.shape, out.dtype) for out in outs]
        + [pltpu.SemaphoreType.DMA((2, 6))],
    )(*results)


def solution(mesh):
    n_lon, n_sample = mesh.shape["lon"], mesh.shape["sample"]
    factor = 1.0 / math.sqrt(n_sample * n_lon * LON * LAT)

    def on_device(state, cot, sea, taps, gain, win, wout):
        out = block(n_lon, n_sample, factor, state, cot, sea, taps, gain, win, wout)
        shape = state.shape
        return (
            out[0].reshape(shape),
            out[1].reshape(shape),
            out[2],
            out[3].T,
            out[4].transpose(2, 0, 1),
            out[5].reshape(OWN),
        )

    slab = P("sample", None, "lon", None)
    return jax.shard_map(
        on_device,
        mesh=mesh,
        in_specs=(slab, slab, P("lon", None), P(), P(), P(), P()),
        out_specs=(
            slab,
            slab,
            P("sample", None),
            P(None, "sample"),
            P("sample", None, None),
            P("sample"),
        ),
        check_vma=False,
    )
```

```python
import functools
import math

import jax
import jax.numpy as jnp
import numpy as np
from jax import lax
from jax.experimental import pallas as pl
from jax.experimental.pallas import tpu as pltpu
from jax.sharding import PartitionSpec as P

C = 192
HID = 768
LON = 16
LAT = 128
PERIOD = 131
SPEC = 256
TAPS = 7
HALO = 3
GROUP = 4
HID_BLOCK = 128
CELL_BLOCK = 512
TILE = 16
OWN = 12
PACKED = 1152
PIECES = PACKED // LAT
BF = jnp.bfloat16
F32 = jnp.float32
MESH = pl.DeviceIdType.MESH


def tree_sum(terms):
    while len(terms) > 1:
        paired = [terms[k] + terms[k + 1] for k in range(0, len(terms) - 1, 2)]
        if len(terms) % 2:
            paired.append(terms[-1])
        terms = paired
    return terms[0]


def matmul(left, right):
    return jnp.dot(left, right, preferred_element_type=F32)


def matmul_nt(left, right):
    return lax.dot_general(left, right, (((1,), (1,)), ((), ())), preferred_element_type=F32)


def split_constant(values):
    high = values.astype(BF)
    low = (values - high.astype(np.float64)).astype(BF)
    return high, low


def spectral_constants():
    angle = 2.0 * math.pi / PERIOD
    row = np.arange(LAT)
    field_f, field_b = np.zeros((LAT, SPEC)), np.zeros((LAT, SPEC))
    back_f, back_b = np.zeros((SPEC, LAT)), np.zeros((SPEC, LAT))
    taps = np.zeros((8, SPEC))
    shift = np.arange(TAPS) - HALO
    field_f[:, 0] = field_b[:, 0] = 1.0
    back_f[0] = back_b[0] = 1.0 / PERIOD
    taps[:TAPS, 0] = 1.0
    half = PERIOD // 2
    for f in range(1, half + 1):
        one, two, three = f, half + f, 2 * half + f
        cos, sin = np.cos(angle * f * row), np.sin(angle * f * row)
        c, d = np.cos(angle * f * shift), np.sin(angle * f * shift)
        taps[:TAPS, one], taps[:TAPS, two], taps[:TAPS, three] = c, d - c, c + d
        field_f[:, one], field_f[:, two], field_f[:, three] = cos - sin, cos, -sin
        field_b[:, one], field_b[:, two], field_b[:, three] = cos + sin, cos, sin
        scale = 2.0 / PERIOD
        back_f[one], back_f[two], back_f[three] = scale * (cos - sin), -scale * sin, -scale * cos
        back_b[one], back_b[two], back_b[three] = scale * (cos + sin), scale * sin, -scale * cos

    def stacked(values):
        return np.concatenate(split_constant(values), axis=0)

    def beside(values):
        return np.concatenate(split_constant(values), axis=1)

    spread_high, spread_low = np.zeros((64, TAPS * SPEC)), np.zeros((64, TAPS * SPEC))
    high, low = split_constant(taps)
    for a in range(TAPS):
        spread_high[8 * a : 8 * a + 8, a * SPEC : (a + 1) * SPEC] = high
        spread_low[8 * a : 8 * a + 8, a * SPEC : (a + 1) * SPEC] = low
    spread = np.concatenate([spread_high, spread_high, spread_low]).astype(BF)
    gather = np.zeros((SPEC, LAT))
    gather[:, :8] = taps.T
    return (
        stacked(field_f),
        np.concatenate([stacked(back_f.T), stacked(field_b)], axis=1),
        beside(back_f),
        beside(back_b),
        spread,
        beside(gather),
    )


def column(ref, at):
    return ref[pl.ds(at, C, stride=LON), :]


def kernel_body(
    n_lon,
    n_sample,
    factor,
    state_ref,
    cot_ref,
    sea_ref,
    taps_ref,
    gain_ref,
    win_ref,
    wout_t,
    field_f,
    field_g,
    back_f,
    back_b,
    spread,
    gather,
    sout_ref,
    gin_ref,
    gwin_ref,
    gwout_ref,
    gk_ref,
    gg_ref,
    x32,
    c32,
    xa,
    ga,
    xh,
    gh,
    gw,
    kf,
    dkf,
    flat_taps,
    sum_high,
    sum_low,
    gainb,
    win_t,
    wout,
    norm_all,
    cot_all,
    hid_all,
    gp_all,
    scaled_all,
    inv_all,
    acc_in,
    acc_out,
    acc_gain,
    dks,
    stage,
    wsend,
    wcore,
    wmid,
    wparts,
    bsend,
    bparts,
    wslab,
    ksend,
    kcore,
    kmid,
    kparts,
    kslab,
    send,
    recv,
):
    remote = n_lon > 1
    if remote:
        lon = lax.axis_index("lon")
        sample = lax.axis_index("sample")
        core = lax.rem(sample, 2)
        owner = sample // 2
        n_own = n_sample // 2
        partner = {"sample": sample + 1 - 2 * core}
        right = {"lon": lax.rem(lon + 1, n_lon)}
        left = {"lon": lax.rem(lon + n_lon - 1, n_lon)}
        owners = [lax.rem(owner + d, n_own) for d in range(1, n_own)]
        slabs = [lax.rem(lon + d, n_lon) for d in range(1, n_lon)]
        peers = (
            [partner]
            + [{"sample": 2 * other + core} for other in owners]
            + [{"lon": other} for other in slabs]
        )
        barrier = pltpu.get_barrier_semaphore()
        for peer in peers:
            pl.semaphore_signal(barrier, inc=1, device_id=peer, device_id_type=MESH)

        def copy(src, dst, slot, peer):
            return pltpu.make_async_remote_copy(
                src_ref=src,
                dst_ref=dst,
                send_sem=send.at[slot],
                recv_sem=recv.at[slot],
                device_id=peer,
                device_id_type=MESH,
            )

    def halo_copies(ref, slot):
        return (
            copy(ref.at[pl.ds(LON, HALO)], ref.at[pl.ds(0, HALO)], slot, right),
            copy(ref.at[pl.ds(HALO, HALO)], ref.at[pl.ds(LON + HALO, HALO)], slot + 1, left),
        )

    def local_halo(ref):
        ref[0:HALO] = ref[LON : LON + HALO]
        ref[LON + HALO : LON + 2 * HALO] = ref[HALO : 2 * HALO]

    x32[...] = state_ref[...].astype(F32).reshape(C * LON, LAT)
    for i in (13, 14, 15, 0, 1, 2):
        own = column(x32, i)
        xa[HALO + i] = own.astype(BF)
    if remote:
        pl.semaphore_wait(barrier, len(peers))
        x_halo = halo_copies(xa, 0)
        for one in x_halo:
            one.start()
    for i in range(3, 13):
        own = column(x32, i)
        xa[HALO + i] = own.astype(BF)
    c32[...] = cot_ref[...].astype(F32).reshape(C * LON, LAT)

    flat_taps[...] = jnp.zeros_like(flat_taps)
    for a in range(TAPS):
        flat_taps[8 * a : 8 * a + TAPS, 0:C] = taps_ref[a]
    rest = flat_taps[...].T[0:C, :]
    high = rest.astype(BF)
    low = (rest - high.astype(F32)).astype(BF)
    kf[...] = matmul(
        jnp.concatenate([high[:, 0:64], low[:, 0:64], high[:, 0:64]], axis=1), spread[...]
    )
    gainb[...] = jnp.broadcast_to(gain_ref[...], (LAT, C)).T
    win_t[...] = win_ref[...].T
    wout[...] = wout_t[...].T
    acc_gain[...] = jnp.zeros_like(acc_gain)

    def doubled(columns):
        flat = columns.reshape(-1, LAT)
        return jnp.concatenate([flat, flat], axis=1)

    def field_spectrum(at, count):
        spectrum = matmul(doubled(xa[at : at + count]), field_f[...])
        xh[at : at + count] = spectrum.reshape(count, C, SPEC)

    def grad_spectrum(at, count):
        spectrum = matmul(doubled(ga[at : at + count]), field_g[:, SPEC:])
        gh[at : at + count] = spectrum.reshape(count, C, SPEC)

    def filtered(field, col, flip, inverse):
        def one_tile(tile, carry):
            at = pl.multiple_of(tile * TILE, TILE)
            for half in range(0, SPEC, LAT):
                window = field[pl.ds(col, GROUP + 2 * HALO), pl.ds(at, TILE), half : half + LAT]
                terms = []
                for a in range(TAPS):
                    first = 2 * HALO - a if flip else a
                    lane = a * SPEC + half
                    weight = kf[pl.ds(at, TILE), lane : lane + LAT]
                    terms.append(weight[None] * window[first : first + GROUP])
                total = tree_sum(terms)
                high = total.astype(BF)
                sum_high[:, pl.ds(at, TILE), half : half + LAT] = high
                sum_low[:, pl.ds(at, TILE), half : half + LAT] = (
                    total - high.astype(F32)
                ).astype(BF)
            return carry

        lax.fori_loop(0, C // TILE, one_tile, 0)
        main = matmul(sum_high[...].reshape(GROUP * C, SPEC), inverse[...])
        rest = matmul(sum_low[...].reshape(GROUP * C, SPEC), inverse[:, 0:LAT])
        return (main[:, 0:LAT] + main[:, LAT:] + rest).reshape(GROUP, C, LAT)

    def masks(col):
        return [sea_ref[pl.ds(col + k, 1), :].astype(F32) for k in range(GROUP)]

    def side_by_side(parts):
        return jnp.concatenate([parts[k] for k in range(GROUP)], axis=1)

    def lanes_of(col):
        return pl.ds(pl.multiple_of(col * LAT, GROUP * LAT), GROUP * LAT)

    def forward_group(col):
        mixed = filtered(xh, col, False, back_f)
        centred = mixed - jnp.mean(mixed, axis=1, keepdims=True)
        variance = jnp.mean(centred * centred, axis=1, keepdims=True)
        inv_scale = lax.rsqrt(variance + 1e-06)
        scaled = centred * inv_scale
        scaled_all[pl.ds(col, GROUP)] = scaled
        inv_all[pl.ds(col, GROUP), :] = inv_scale.reshape(GROUP, LAT)
        normed = side_by_side((scaled * gainb[...][None]).astype(BF))
        mask = masks(col)
        grad_out = side_by_side([(column(c32, col + k) * mask[k]).astype(BF) for k in range(GROUP)])
        where = lanes_of(col)
        norm_all[:, where] = normed
        cot_all[:, where] = grad_out
        for h in range(0, HID, HID_BLOCK):
            for n in range(0, GROUP * LAT, CELL_BLOCK):
                pre = matmul(win_t[h : h + HID_BLOCK, :], normed[:, n : n + CELL_BLOCK])
                grad_hidden = matmul(wout[h : h + HID_BLOCK, :], grad_out[:, n : n + CELL_BLOCK])
                square = pre * pre
                inner = pre * (0.7978845608028654 + 0.035677408136300125 * square)
                gate = 0.5 + 0.5 * jnp.tanh(inner)
                hidden = pre * gate
                slope = gate + hidden * (1.0 - gate) * (
                    1.5957691216057308 + 0.21406444881780074 * square
                )
                at = pl.ds(pl.multiple_of(col * LAT + n, CELL_BLOCK), CELL_BLOCK)
                hid_all[h : h + HID_BLOCK, at] = hidden.astype(BF)
                gp_all[h : h + HID_BLOCK, at] = (grad_hidden * slope).astype(BF)

    def backward_mlp(col):
        where = lanes_of(col)
        gain = gainb[...]
        mask = masks(col)
        branch = matmul(wout_t[...], hid_all[:, where])
        for k in range(GROUP):
            lane = slice(k * LAT, (k + 1) * LAT)
            at = pl.ds(col + k, C, stride=LON)
            x32[at, :] = mask[k] * (x32[at, :] + branch[:, lane])
        grad_normed = matmul(win_ref[...], gp_all[:, where])
        for k in range(GROUP):
            lane = slice(k * LAT, (k + 1) * LAT)
            scaled = scaled_all[col + k]
            grad = grad_normed[:, lane]
            product = grad * scaled
            acc_gain[...] += product
            grad_scaled = grad * gain
            first = jnp.mean(grad_scaled, axis=0, keepdims=True)
            second = jnp.mean(product * gain, axis=0, keepdims=True)
            inv_scale = inv_all[pl.ds(col + k, 1), :]
            grad_conv = (inv_scale * (grad_scaled - first - scaled * second)).astype(BF)
            ga[HALO + col + k] = grad_conv
            spectrum = matmul(doubled(grad_conv), field_g[...])
            gw[col + k] = spectrum[:, 0:SPEC]
            gh[HALO + col + k] = spectrum[:, SPEC:]

    def fill_halo():
        field_spectrum(0, HALO)
        field_spectrum(LON + HALO, HALO)

    def in_groups(first, last, work):
        def one_group(step, carry):
            work(lax.rem(GROUP + step * GROUP, LON))
            return carry

        lax.fori_loop(first, last, one_group, 0)

    def start(copies):
        for one in copies:
            one.start()

    def wait(copies):
        for one in copies:
            one.wait()

    for at in range(HALO, LON + HALO, GROUP):
        field_spectrum(at, GROUP)
    in_groups(0, 2, forward_group)
    if remote:
        wait(x_halo)
    else:
        local_halo(xa)
    fill_halo()
    in_groups(2, 4, forward_group)

    acc_out[...] = matmul_nt(cot_all[...], hid_all[...])
    acc_in[...] = matmul_nt(norm_all[...], gp_all[...])
    wide = HID // 2
    for o in range(16):
        at = OWN * o
        stage[o, 0:12, 0:HID] = acc_in[at : at + 12, :]
        stage[o, 12:16, 0:HID] = acc_out[at : at + 4, :]
        stage[o, 0:8, HID:PACKED] = acc_out[at + 4 : at + 12, 0:wide]
        stage[o, 8:16, HID:PACKED] = acc_out[at + 4 : at + 12, wide:HID]
    for o in range(16):
        q = o // 2
        for t in range(PIECES):
            slot = q if t < 8 else 8
            piece = stage[o, :, t * LAT : (t + 1) * LAT].astype(BF)
            wsend[o % 2, (q + t) % 8, slot] = piece

    if remote:

        def to_slabs(source, target, base):
            return [
                copy(source(other), target(d), base + d, {"lon": other})
                for d, other in enumerate(slabs)
            ]

        def to_owners(source, target, base):
            return [
                copy(source.at[other], target.at[d], base + d, {"sample": 2 * other + core})
                for d, other in enumerate(owners)
            ]

        def w_core():
            return [copy(wsend.at[1 - core], wcore, 4, partner)]

        def w_lon():
            return to_slabs(lambda other: wmid.at[other], lambda d: wparts.at[d], 5)

        def w_own():
            return to_owners(bsend, bparts, 12)

        def w_all():
            return to_slabs(lambda other: wslab.at[lon], lambda d: wslab.at[lon], 19)

        def k_core():
            return [copy(ksend.at[1 - core], kcore, 26, partner)]

        def k_own():
            return to_owners(kmid, kparts, 27)

        def k_all():
            return to_slabs(lambda other: kslab.at[lon], lambda d: kslab.at[lon], 34)

        start(w_core())
    in_groups(2, 4, backward_mlp)
    if remote:
        g_halo = halo_copies(ga, 2)
        start(g_halo)
        wait(w_core())
        wmid[...] = (wsend[core].astype(F32) + wcore[...].astype(F32)).astype(BF)
        start(w_lon())
    in_groups(0, 2, backward_mlp)

    def products(tile, carry):
        at = pl.multiple_of(tile * 8, 8)
        for half in range(0, SPEC, LAT):
            grads = gw[:, pl.ds(at, 8), half : half + LAT]
            for a in range(TAPS):
                terms = grads * xh[a : a + LON, pl.ds(at, 8), half : half + LAT]
                lane = a * SPEC + half
                dkf[pl.ds(at, 8), lane : lane + LAT] = jnp.sum(terms, axis=0)
        return carry

    lax.fori_loop(0, C // 8, products, 0)
    lanes = lax.broadcasted_iota(jnp.int32, (C, LAT), 1)
    total = jnp.where(lanes == TAPS * TAPS, jnp.sum(acc_gain[...], axis=1, keepdims=True), 0.0)
    for a in range(TAPS):
        part = dkf[:, a * SPEC : (a + 1) * SPEC]
        high = part.astype(BF)
        low = (part - high.astype(F32)).astype(BF)
        both = matmul(high, gather[...])
        found = both[:, 0:LAT] + both[:, LAT:] + matmul(low, gather[:, 0:LAT])
        total = total + (pltpu.roll(found, a * TAPS, axis=1) if a else found)
    dks[0:C, :] = total
    dks[C : C + 16, :] = jnp.zeros((16, LAT), F32)
    for o in range(16):
        ksend[o % 2, o // 2] = dks[OWN * o : OWN * o + 16, :]
    if remote:
        start(k_core())

    def backward_group(col):
        moved = filtered(gh, col, True, back_b)
        mask = masks(col)
        for k in range(GROUP):
            at = pl.ds(col + k, C, stride=LON)
            c32[at, :] = c32[at, :] * mask[k] + moved[k]

    if remote:
        wait(w_lon())
        total = wmid[lon].astype(F32)
        for d in range(len(slabs)):
            total = total + wparts[d].astype(F32)
        for q in range(8):
            bsend[q, 0] = total[q].astype(BF)
            bsend[q, 1] = total[8].astype(BF)
        start(w_own())
    in_groups(0, 1, backward_group)
    if remote:
        wait(k_core())
        kmid[...] = ksend[core] + kcore[...]
        start(k_own())
    in_groups(1, 2, backward_group)
    if remote:
        wait(w_own())
        held = bsend[owner].astype(F32)
        for d in range(len(owners)):
            held = held + bparts[d].astype(F32)
        wslab[lon] = held
        start(w_all())
        wait(g_halo)
    else:
        local_halo(ga)
    grad_spectrum(0, HALO)
    grad_spectrum(LON + HALO, HALO)
    in_groups(2, 3, backward_group)
    if remote:
        wait(k_own())
        held = kmid[owner]
        for d in range(len(owners)):
            held = held + kparts[d]
        kslab[lon] = held
        start(k_all())
    in_groups(3, 4, backward_group)
    sout_ref[...] = x32[...].reshape(C, LON, LAT).astype(BF)
    gin_ref[...] = c32[...].reshape(C, LON, LAT).astype(BF)
    if remote:
        wait(w_all())
        tiles = [wslab[lax.rem(owner + t, 8), 0] for t in range(8)] + [wslab[owner, 1]]
        wait(k_all())
        small = kslab[0]
        for other in range(1, n_lon):
            small = small + kslab[other]
    else:
        tiles = [wsend[0, t % 8, 0 if t < 8 else 8].astype(F32) for t in range(PIECES)]
        small = ksend[0, 0]
    weights = jnp.concatenate(tiles, axis=1) * factor
    small = small * factor
    gwin_ref[...] = weights[0:12, 0:HID]
    gwout_ref[0:4, :] = weights[12:16, 0:HID]
    gwout_ref[4:12, 0:wide] = weights[0:8, HID:PACKED]
    gwout_ref[4:12, wide:HID] = weights[8:16, HID:PACKED]
    small_t = small.T
    for a in range(TAPS):
        gk_ref[a] = small_t[a * TAPS : (a + 1) * TAPS, 0:OWN]
    gg_ref[...] = small_t[TAPS * TAPS : TAPS * TAPS + 1, 0:OWN]


def deliver(*refs):
    count = len(refs) // 3
    sems = refs[-1]
    sources, targets, held = refs[:count], refs[count : 2 * count], refs[2 * count : 3 * count]
    arrive = [pltpu.make_async_copy(sources[k], held[k], sems.at[0, k]) for k in range(count)]
    leave = [pltpu.make_async_copy(held[k], targets[k], sems.at[1, k]) for k in range(count)]
    for one in arrive:
        one.start()
    for k in range(count):
        arrive[k].wait()
        leave[k].start()
    for one in leave:
        one.wait()


def block(n_lon, n_sample, factor, state, cot, sea, taps, gain, win, wout):
    vmem = pl.BlockSpec(memory_space=pltpu.VMEM)
    shape = jax.ShapeDtypeStruct
    outs = (
        shape((C, LON, LAT), BF),
        shape((C, LON, LAT), BF),
        shape((OWN, HID), F32),
        shape((OWN, HID), F32),
        shape((TAPS, TAPS, OWN), F32),
        shape((1, OWN), F32),
    )
    scratch = [
        pltpu.VMEM((C * LON, LAT), F32),
        pltpu.VMEM((C * LON, LAT), F32),
        pltpu.VMEM((LON + 2 * HALO, C, LAT), BF),
        pltpu.VMEM((LON + 2 * HALO, C, LAT), BF),
        pltpu.VMEM((LON + 2 * HALO, C, SPEC), F32),
        pltpu.VMEM((LON + 2 * HALO, C, SPEC), F32),
        pltpu.VMEM((LON, C, SPEC), F32),
        pltpu.VMEM((C, TAPS * SPEC), F32),
        pltpu.VMEM((C, TAPS * SPEC), F32),
        pltpu.VMEM((LAT, 2 * LAT), F32),
        pltpu.VMEM((GROUP, C, SPEC), BF),
        pltpu.VMEM((GROUP, C, SPEC), BF),
        pltpu.VMEM((C, LAT), F32),
        pltpu.VMEM((HID, C), BF),
        pltpu.VMEM((HID, C), BF),
        pltpu.VMEM((C, LON * LAT), BF),
        pltpu.VMEM((C, LON * LAT), BF),
        pltpu.VMEM((HID, LON * LAT), BF),
        pltpu.VMEM((HID, LON * LAT), BF),
        pltpu.VMEM((LON, C, LAT), F32),
        pltpu.VMEM((LON, LAT), F32),
        pltpu.VMEM((C, HID), F32),
        pltpu.VMEM((C, HID), F32),
        pltpu.VMEM((C, LAT), F32),
        pltpu.VMEM((C + 16, LAT), F32),
        pltpu.VMEM((16, 16, PACKED), F32),
        pltpu.VMEM((2, 8, PIECES, 16, LAT), BF),
        pltpu.VMEM((8, PIECES, 16, LAT), BF),
        pltpu.VMEM((8, PIECES, 16, LAT), BF),
        pltpu.VMEM((7, PIECES, 16, LAT), BF),
        pltpu.VMEM((8, 2, 16, LAT), BF),
        pltpu.VMEM((7, 2, 16, LAT), BF),
        pltpu.VMEM((8, 2, 16, LAT), F32),
        pltpu.VMEM((2, 8, 16, LAT), F32),
        pltpu.VMEM((8, 16, LAT), F32),
        pltpu.VMEM((8, 16, LAT), F32),
        pltpu.VMEM((7, 16, LAT), F32),
        pltpu.VMEM((8, 16, LAT), F32),
        pltpu.SemaphoreType.DMA((41,)),
        pltpu.SemaphoreType.DMA((41,)),
    ]
    extra = dict(collective_id=0, has_side_effects=True) if n_lon > 1 else {}
    results = pl.pallas_call(
        functools.partial(kernel_body, n_lon, n_sample, factor),
        out_shape=outs,
        in_specs=[vmem] * 13,
        out_specs=(vmem,) * 6,
        scratch_shapes=scratch,
        compiler_params=pltpu.CompilerParams(vmem_limit_bytes=60 * 1024 * 1024, **extra),
    )(
        state.reshape(C, LON, LAT),
        cot.reshape(C, LON, LAT),
        sea,
        taps.transpose(1, 2, 0),
        gain.reshape(1, C),
        win,
        wout.T,
        *spectral_constants(),
    )
    anywhere = pl.BlockSpec(memory_space=pl.ANY)
    return pl.pallas_call(
        deliver,
        out_shape=outs,
        in_specs=[anywhere] * 6,
        out_specs=(anywhere,) * 6,
        scratch_shapes=[pltpu.VMEM(out.shape, out.dtype) for out in outs]
        + [pltpu.SemaphoreType.DMA((2, 6))],
    )(*results)


def solution(mesh):
    n_lon, n_sample = mesh.shape["lon"], mesh.shape["sample"]
    factor = 1.0 / math.sqrt(n_sample * n_lon * LON * LAT)

    def on_device(state, cot, sea, taps, gain, win, wout):
        out = block(n_lon, n_sample, factor, state, cot, sea, taps, gain, win, wout)
        shape = state.shape
        return (
            out[0].reshape(shape),
            out[1].reshape(shape),
            out[2],
            out[3].T,
            out[4].transpose(2, 0, 1),
            out[5].reshape(OWN),
        )

    slab = P("sample", None, "lon", None)
    return jax.shard_map(
        on_device,
        mesh=mesh,
        in_specs=(slab, slab, P("lon", None), P(), P(), P(), P()),
        out_specs=(
            slab,
            slab,
            P("sample", None),
            P(None, "sample"),
            P("sample", None, None),
            P("sample"),
        ),
        check_vma=False,
    )
```

```python
import functools
import math

import jax
import jax.numpy as jnp
import numpy as np
from jax import lax
from jax.experimental import pallas as pl
from jax.experimental.pallas import tpu as pltpu
from jax.sharding import PartitionSpec as P

C = 192
HID = 768
LON = 16
LAT = 128
PERIOD = 131
SPEC = 256
TAPS = 7
HALO = 3
GROUP = 4
HID_BLOCK = 256
CELL_BLOCK = 256
TILE = 16
OWN = 12
PACKED = 1152
BF = jnp.bfloat16
F32 = jnp.float32
MESH = pl.DeviceIdType.MESH


def tree_sum(terms):
    while len(terms) > 1:
        paired = [terms[k] + terms[k + 1] for k in range(0, len(terms) - 1, 2)]
        if len(terms) % 2:
            paired.append(terms[-1])
        terms = paired
    return terms[0]


def matmul(left, right):
    return jnp.dot(left, right, preferred_element_type=F32)


def matmul_nt(left, right):
    return lax.dot_general(left, right, (((1,), (1,)), ((), ())), preferred_element_type=F32)


def split_constant(values):
    high = values.astype(BF)
    low = (values - high.astype(np.float64)).astype(BF)
    return high, low


def spectral_constants():
    angle = 2.0 * math.pi / PERIOD
    row = np.arange(LAT)
    field_f, field_b = np.zeros((LAT, SPEC)), np.zeros((LAT, SPEC))
    back_f, back_b = np.zeros((SPEC, LAT)), np.zeros((SPEC, LAT))
    taps = np.zeros((8, SPEC))
    shift = np.arange(TAPS) - HALO
    field_f[:, 0] = field_b[:, 0] = 1.0
    back_f[0] = back_b[0] = 1.0 / PERIOD
    taps[:TAPS, 0] = 1.0
    half = PERIOD // 2
    for f in range(1, half + 1):
        one, two, three = f, half + f, 2 * half + f
        cos, sin = np.cos(angle * f * row), np.sin(angle * f * row)
        c, d = np.cos(angle * f * shift), np.sin(angle * f * shift)
        taps[:TAPS, one], taps[:TAPS, two], taps[:TAPS, three] = c, d - c, c + d
        field_f[:, one], field_f[:, two], field_f[:, three] = cos - sin, cos, -sin
        field_b[:, one], field_b[:, two], field_b[:, three] = cos + sin, cos, sin
        scale = 2.0 / PERIOD
        back_f[one], back_f[two], back_f[three] = scale * (cos - sin), -scale * sin, -scale * cos
        back_b[one], back_b[two], back_b[three] = scale * (cos + sin), scale * sin, -scale * cos

    def stacked(values):
        return np.concatenate(split_constant(values), axis=0)

    def beside(values):
        return np.concatenate(split_constant(values), axis=1)

    spread_high, spread_low = np.zeros((64, TAPS * SPEC)), np.zeros((64, TAPS * SPEC))
    high, low = split_constant(taps)
    for a in range(TAPS):
        spread_high[8 * a : 8 * a + 8, a * SPEC : (a + 1) * SPEC] = high
        spread_low[8 * a : 8 * a + 8, a * SPEC : (a + 1) * SPEC] = low
    spread = np.concatenate([spread_high, spread_high, spread_low]).astype(BF)
    gather = np.zeros((SPEC, LAT))
    gather[:, :8] = taps.T
    return (
        stacked(field_f),
        np.concatenate([stacked(back_f.T), stacked(field_b)], axis=1),
        beside(back_f),
        beside(back_b),
        spread,
        beside(gather),
    )


def column(ref, at):
    return ref[pl.ds(at, C, stride=LON), :]


def kernel_body(
    n_lon,
    n_sample,
    factor,
    state_ref,
    cot_ref,
    sea_ref,
    taps_ref,
    gain_ref,
    win_ref,
    wout_t,
    field_f,
    field_g,
    back_f,
    back_b,
    spread,
    gather,
    sout_ref,
    gin_ref,
    gwin_ref,
    gwout_ref,
    gk_ref,
    gg_ref,
    x32,
    c32,
    xa,
    ga,
    xh,
    gh,
    gw,
    kf,
    dkf,
    flat_taps,
    sum_high,
    sum_low,
    gainb,
    win_t,
    wout,
    norm_all,
    cot_all,
    hid_all,
    gp_all,
    scaled_all,
    inv_all,
    acc_in,
    acc_out,
    acc_gain,
    dks,
    stage,
    wsend,
    wcore,
    wmid,
    wparts,
    wslab,
    ksend,
    kcore,
    kmid,
    kparts,
    kslab,
    send,
    recv,
):
    remote = n_lon > 1
    if remote:
        lon = lax.axis_index("lon")
        sample = lax.axis_index("sample")
        core = lax.rem(sample, 2)
        owner = sample // 2
        n_own = n_sample // 2
        partner = {"sample": sample + 1 - 2 * core}
        right = {"lon": lax.rem(lon + 1, n_lon)}
        left = {"lon": lax.rem(lon + n_lon - 1, n_lon)}
        owners = [lax.rem(owner + d, n_own) for d in range(1, n_own)]
        slabs = [lax.rem(lon + d, n_lon) for d in range(1, n_lon)]
        peers = (
            [partner]
            + [{"sample": 2 * other + core} for other in owners]
            + [{"lon": other} for other in slabs]
        )
        barrier = pltpu.get_barrier_semaphore()
        for peer in peers:
            pl.semaphore_signal(barrier, inc=1, device_id=peer, device_id_type=MESH)

        def copy(src, dst, slot, peer):
            return pltpu.make_async_remote_copy(
                src_ref=src,
                dst_ref=dst,
                send_sem=send.at[slot],
                recv_sem=recv.at[slot],
                device_id=peer,
                device_id_type=MESH,
            )

    def halo_copies(ref, slot):
        return (
            copy(ref.at[pl.ds(LON, HALO)], ref.at[pl.ds(0, HALO)], slot, right),
            copy(ref.at[pl.ds(HALO, HALO)], ref.at[pl.ds(LON + HALO, HALO)], slot + 1, left),
        )

    def local_halo(ref):
        ref[0:HALO] = ref[LON : LON + HALO]
        ref[LON + HALO : LON + 2 * HALO] = ref[HALO : 2 * HALO]

    x32[...] = state_ref[...].astype(F32).reshape(C * LON, LAT)
    for i in (13, 14, 15, 0, 1, 2):
        own = column(x32, i)
        xa[HALO + i] = own.astype(BF)
    if remote:
        pl.semaphore_wait(barrier, len(peers))
        x_halo = halo_copies(xa, 0)
        for one in x_halo:
            one.start()
    for i in range(3, 13):
        own = column(x32, i)
        xa[HALO + i] = own.astype(BF)
    c32[...] = cot_ref[...].astype(F32).reshape(C * LON, LAT)

    flat_taps[...] = jnp.zeros_like(flat_taps)
    for a in range(TAPS):
        flat_taps[8 * a : 8 * a + TAPS, 0:C] = taps_ref[a]
    rest = flat_taps[...].T[0:C, :]
    high = rest.astype(BF)
    low = (rest - high.astype(F32)).astype(BF)
    kf[...] = matmul(
        jnp.concatenate([high[:, 0:64], low[:, 0:64], high[:, 0:64]], axis=1), spread[...]
    )
    gainb[...] = jnp.broadcast_to(gain_ref[...], (LAT, C)).T
    win_t[...] = (0.5 * win_ref[...].astype(F32)).astype(BF).T
    wout[...] = (0.5 * wout_t[...].astype(F32)).astype(BF).T
    acc_gain[...] = jnp.zeros_like(acc_gain)

    def doubled(columns):
        flat = columns.reshape(-1, LAT)
        return jnp.concatenate([flat, flat], axis=1)

    def field_spectrum(at, count):
        spectrum = matmul(doubled(xa[at : at + count]), field_f[...])
        xh[at : at + count] = spectrum.reshape(count, C, SPEC)

    def grad_spectrum(at, count):
        spectrum = matmul(doubled(ga[at : at + count]), field_g[:, SPEC:])
        gh[at : at + count] = spectrum.reshape(count, C, SPEC)

    def filtered(field, col, flip, inverse):
        def one_tile(tile, carry):
            at = pl.multiple_of(tile * TILE, TILE)
            for half in range(0, SPEC, LAT):
                window = field[pl.ds(col, GROUP + 2 * HALO), pl.ds(at, TILE), half : half + LAT]
                terms = []
                for a in range(TAPS):
                    first = 2 * HALO - a if flip else a
                    lane = a * SPEC + half
                    weight = kf[pl.ds(at, TILE), lane : lane + LAT]
                    terms.append(weight[None] * window[first : first + GROUP])
                total = tree_sum(terms)
                high = total.astype(BF)
                sum_high[:, pl.ds(at, TILE), half : half + LAT] = high
                sum_low[:, pl.ds(at, TILE), half : half + LAT] = (
                    total - high.astype(F32)
                ).astype(BF)
            return carry

        lax.fori_loop(0, C // TILE, one_tile, 0)
        main = matmul(sum_high[...].reshape(GROUP * C, SPEC), inverse[...])
        rest = matmul(sum_low[...].reshape(GROUP * C, SPEC), inverse[:, 0:LAT])
        return (main[:, 0:LAT] + main[:, LAT:] + rest).reshape(GROUP, C, LAT)

    def masks(col):
        return [sea_ref[pl.ds(col + k, 1), :].astype(F32) for k in range(GROUP)]

    def side_by_side(parts):
        return jnp.concatenate([parts[k] for k in range(GROUP)], axis=1)

    def lanes_of(col):
        return pl.ds(pl.multiple_of(col * LAT, GROUP * LAT), GROUP * LAT)

    def forward_group(col):
        mixed = filtered(xh, col, False, back_f)
        centred = mixed - jnp.mean(mixed, axis=1, keepdims=True)
        variance = jnp.mean(centred * centred, axis=1, keepdims=True)
        inv_scale = lax.rsqrt(variance + 1e-06)
        scaled = centred * inv_scale
        scaled_all[pl.ds(col, GROUP)] = scaled
        inv_all[pl.ds(col, GROUP), :] = inv_scale.reshape(GROUP, LAT)
        normed = side_by_side((scaled * gainb[...][None]).astype(BF))
        mask = masks(col)
        grad_out = side_by_side([(column(c32, col + k) * mask[k]).astype(BF) for k in range(GROUP)])
        where = lanes_of(col)
        norm_all[:, where] = normed
        cot_all[:, where] = grad_out
        for h in range(0, HID, HID_BLOCK):
            for n in range(0, GROUP * LAT, CELL_BLOCK):
                half = matmul(win_t[h : h + HID_BLOCK, :], normed[:, n : n + CELL_BLOCK])
                grad_half = matmul(wout[h : h + HID_BLOCK, :], grad_out[:, n : n + CELL_BLOCK])
                square = half * half
                bent = jnp.tanh(half * (1.5957691216057308 + 0.28541926509040104 * square))
                gate = 1.0 + bent
                hidden = half * gate
                slope = gate + hidden * (1.0 - bent) * (
                    1.5957691216057308 + 0.8562577952712031 * square
                )
                at = pl.ds(pl.multiple_of(col * LAT + n, CELL_BLOCK), CELL_BLOCK)
                hid_all[h : h + HID_BLOCK, at] = hidden.astype(BF)
                gp_all[h : h + HID_BLOCK, at] = (grad_half * slope).astype(BF)

    def finish_state(col):
        mask = masks(col)
        branch = matmul(wout_t[...], hid_all[:, lanes_of(col)])
        for k in range(GROUP):
            lane = slice(k * LAT, (k + 1) * LAT)
            at = pl.ds(col + k, C, stride=LON)
            x32[at, :] = mask[k] * (x32[at, :] + branch[:, lane])

    def backward_mlp(col):
        where = lanes_of(col)
        gain = gainb[...]
        grad_normed = matmul(win_ref[...], gp_all[:, where])
        for k in range(GROUP):
            lane = slice(k * LAT, (k + 1) * LAT)
            scaled = scaled_all[col + k]
            grad = grad_normed[:, lane]
            product = grad * scaled
            acc_gain[...] += product
            grad_scaled = grad * gain
            first = jnp.mean(grad_scaled, axis=0, keepdims=True)
            second = jnp.mean(product * gain, axis=0, keepdims=True)
            inv_scale = inv_all[pl.ds(col + k, 1), :]
            grad_conv = (inv_scale * (grad_scaled - first - scaled * second)).astype(BF)
            ga[HALO + col + k] = grad_conv
            spectrum = matmul(doubled(grad_conv), field_g[...])
            gw[col + k] = spectrum[:, 0:SPEC]
            gh[HALO + col + k] = spectrum[:, SPEC:]

    def fill_halo():
        field_spectrum(0, HALO)
        field_spectrum(LON + HALO, HALO)

    def in_groups(first, last, work):
        def one_group(step, carry):
            work(lax.rem(GROUP + step * GROUP, LON))
            return carry

        lax.fori_loop(first, last, one_group, 0)

    def start(copies):
        for one in copies:
            one.start()

    def wait(copies):
        for one in copies:
            one.wait()

    for at in range(HALO, LON + HALO, GROUP):
        field_spectrum(at, GROUP)
    def filter_grads(parts, fresh):
        def one_tile(tile, carry):
            at = pl.multiple_of(tile * 8, 8)
            for half in range(0, SPEC, LAT):
                lanes = slice(half, half + LAT)
                for a in range(TAPS):
                    spot = slice(a * SPEC + half, a * SPEC + half + LAT)
                    total = 0.0 if fresh else dkf[pl.ds(at, 8), spot]
                    for col, count in parts:
                        grads = gw[col : col + count, pl.ds(at, 8), lanes]
                        field = xh[col + a : col + a + count, pl.ds(at, 8), lanes]
                        total = total + jnp.sum(grads * field, axis=0)
                    dkf[pl.ds(at, 8), spot] = total
            return carry

        lax.fori_loop(0, C // 8, one_tile, 0)

    in_groups(0, 2, forward_group)
    in_groups(0, 2, backward_mlp)
    filter_grads([(GROUP, 2 * GROUP)], True)
    cells = slice(GROUP * LAT, 3 * GROUP * LAT)
    acc_out[...] = matmul_nt(cot_all[:, cells], hid_all[:, cells])
    acc_in[...] = matmul_nt(norm_all[:, cells], gp_all[:, cells])
    if remote:
        wait(x_halo)
    else:
        local_halo(xa)
    fill_halo()
    in_groups(2, 4, forward_group)

    for cells in (slice(0, GROUP * LAT), slice(3 * GROUP * LAT, LON * LAT)):
        acc_out[...] += matmul_nt(cot_all[:, cells], hid_all[:, cells])
        acc_in[...] += matmul_nt(norm_all[:, cells], gp_all[:, cells])
    wide = HID // 2
    for o in range(16):
        at = OWN * o
        stage[o, 0:12, 0:HID] = acc_in[at : at + 12, :]
        stage[o, 12:16, 0:HID] = acc_out[at : at + 4, :]
        stage[o, 0:8, HID:PACKED] = acc_out[at + 4 : at + 12, 0:wide]
        stage[o, 8:16, HID:PACKED] = acc_out[at + 4 : at + 12, wide:HID]
    for o in range(16):
        wsend[o % 2, o // 2] = stage[o].astype(BF)

    if remote:

        def to_slabs(slab, base):
            return [
                copy(slab.at[lon], slab.at[lon], base + d, {"lon": other})
                for d, other in enumerate(slabs)
            ]

        def to_owners(source, target, base):
            return [
                copy(source.at[other], target.at[d], base + d, {"sample": 2 * other + core})
                for d, other in enumerate(owners)
            ]

        def w_core():
            return [copy(wsend.at[1 - core], wcore, 4, partner)]

        def w_own():
            return to_owners(wmid, wparts, 5)

        def w_all():
            return to_slabs(wslab, 12)

        def k_core():
            return [copy(ksend.at[1 - core], kcore, 19, partner)]

        def k_own():
            return to_owners(kmid, kparts, 20)

        def k_all():
            return to_slabs(kslab, 27)

        start(w_core())
    in_groups(2, 4, backward_mlp)
    if remote:
        g_halo = halo_copies(ga, 2)
        start(g_halo)
        wait(w_core())
        wmid[...] = (wsend[core].astype(F32) + wcore[...].astype(F32)).astype(BF)
        start(w_own())
    filter_grads([(0, GROUP), (3 * GROUP, GROUP)], False)

    lanes = lax.broadcasted_iota(jnp.int32, (C, LAT), 1)
    total = jnp.where(lanes == TAPS * TAPS, jnp.sum(acc_gain[...], axis=1, keepdims=True), 0.0)
    for a in range(TAPS):
        part = dkf[:, a * SPEC : (a + 1) * SPEC]
        high = part.astype(BF)
        low = (part - high.astype(F32)).astype(BF)
        both = matmul(high, gather[...])
        found = both[:, 0:LAT] + both[:, LAT:] + matmul(low, gather[:, 0:LAT])
        total = total + (pltpu.roll(found, a * TAPS, axis=1) if a else found)
    dks[0:C, :] = total
    dks[C : C + 16, :] = jnp.zeros((16, LAT), F32)
    for o in range(16):
        ksend[o % 2, o // 2] = dks[OWN * o : OWN * o + 16, :]
    if remote:
        start(k_core())
    in_groups(0, 4, finish_state)
    if remote:
        wait(k_core())
        kmid[...] = ksend[core] + kcore[...]
        start(k_own())

    def backward_group(col):
        moved = filtered(gh, col, True, back_b)
        mask = masks(col)
        for k in range(GROUP):
            at = pl.ds(col + k, C, stride=LON)
            c32[at, :] = c32[at, :] * mask[k] + moved[k]

    in_groups(0, 2, backward_group)
    if remote:
        wait(w_own())
        held = wmid[owner].astype(F32)
        for d in range(len(owners)):
            held = held + wparts[d].astype(F32)
        wslab[lon] = held.astype(BF)
        start(w_all())
        wait(g_halo)
    else:
        local_halo(ga)
    grad_spectrum(0, HALO)
    grad_spectrum(LON + HALO, HALO)
    in_groups(2, 3, backward_group)
    if remote:
        wait(k_own())
        held = kmid[owner]
        for d in range(len(owners)):
            held = held + kparts[d]
        kslab[lon] = held
        start(k_all())
    in_groups(3, 4, backward_group)
    sout_ref[...] = x32[...].reshape(C, LON, LAT).astype(BF)
    gin_ref[...] = c32[...].reshape(C, LON, LAT).astype(BF)
    if remote:
        wait(w_all())
        weights = wslab[0].astype(F32)
        for other in range(1, n_lon):
            weights = weights + wslab[other].astype(F32)
        wait(k_all())
        small = kslab[0]
        for other in range(1, n_lon):
            small = small + kslab[other]
    else:
        weights = wsend[0, 0].astype(F32)
        small = ksend[0, 0]
    weights = weights * factor
    small = small * factor
    gwin_ref[...] = weights[0:12, 0:HID]
    gwout_ref[0:4, :] = weights[12:16, 0:HID]
    gwout_ref[4:12, 0:wide] = weights[0:8, HID:PACKED]
    gwout_ref[4:12, wide:HID] = weights[8:16, HID:PACKED]
    small_t = small.T
    for a in range(TAPS):
        gk_ref[a] = small_t[a * TAPS : (a + 1) * TAPS, 0:OWN]
    gg_ref[...] = small_t[TAPS * TAPS : TAPS * TAPS + 1, 0:OWN]


def deliver(*refs):
    count = len(refs) // 3
    sems = refs[-1]
    sources, targets, held = refs[:count], refs[count : 2 * count], refs[2 * count : 3 * count]
    arrive = [pltpu.make_async_copy(sources[k], held[k], sems.at[0, k]) for k in range(count)]
    leave = [pltpu.make_async_copy(held[k], targets[k], sems.at[1, k]) for k in range(count)]
    for one in arrive:
        one.start()
    for k in range(count):
        arrive[k].wait()
        leave[k].start()
    for one in leave:
        one.wait()


def block(n_lon, n_sample, factor, state, cot, sea, taps, gain, win, wout):
    vmem = pl.BlockSpec(memory_space=pltpu.VMEM)
    shape = jax.ShapeDtypeStruct
    outs = (
        shape((C, LON, LAT), BF),
        shape((C, LON, LAT), BF),
        shape((OWN, HID), F32),
        shape((OWN, HID), F32),
        shape((TAPS, TAPS, OWN), F32),
        shape((1, OWN), F32),
    )
    scratch = [
        pltpu.VMEM((C * LON, LAT), F32),
        pltpu.VMEM((C * LON, LAT), F32),
        pltpu.VMEM((LON + 2 * HALO, C, LAT), BF),
        pltpu.VMEM((LON + 2 * HALO, C, LAT), BF),
        pltpu.VMEM((LON + 2 * HALO, C, SPEC), F32),
        pltpu.VMEM((LON + 2 * HALO, C, SPEC), F32),
        pltpu.VMEM((LON, C, SPEC), F32),
        pltpu.VMEM((C, TAPS * SPEC), F32),
        pltpu.VMEM((C, TAPS * SPEC), F32),
        pltpu.VMEM((LAT, 2 * LAT), F32),
        pltpu.VMEM((GROUP, C, SPEC), BF),
        pltpu.VMEM((GROUP, C, SPEC), BF),
        pltpu.VMEM((C, LAT), F32),
        pltpu.VMEM((HID, C), BF),
        pltpu.VMEM((HID, C), BF),
        pltpu.VMEM((C, LON * LAT), BF),
        pltpu.VMEM((C, LON * LAT), BF),
        pltpu.VMEM((HID, LON * LAT), BF),
        pltpu.VMEM((HID, LON * LAT), BF),
        pltpu.VMEM((LON, C, LAT), F32),
        pltpu.VMEM((LON, LAT), F32),
        pltpu.VMEM((C, HID), F32),
        pltpu.VMEM((C, HID), F32),
        pltpu.VMEM((C, LAT), F32),
        pltpu.VMEM((C + 16, LAT), F32),
        pltpu.VMEM((16, 16, PACKED), F32),
        pltpu.VMEM((2, 8, 16, PACKED), BF),
        pltpu.VMEM((8, 16, PACKED), BF),
        pltpu.VMEM((8, 16, PACKED), BF),
        pltpu.VMEM((7, 16, PACKED), BF),
        pltpu.VMEM((8, 16, PACKED), BF),
        pltpu.VMEM((2, 8, 16, LAT), F32),
        pltpu.VMEM((8, 16, LAT), F32),
        pltpu.VMEM((8, 16, LAT), F32),
        pltpu.VMEM((7, 16, LAT), F32),
        pltpu.VMEM((8, 16, LAT), F32),
        pltpu.SemaphoreType.DMA((34,)),
        pltpu.SemaphoreType.DMA((34,)),
    ]
    extra = dict(collective_id=0, has_side_effects=True) if n_lon > 1 else {}
    results = pl.pallas_call(
        functools.partial(kernel_body, n_lon, n_sample, factor),
        out_shape=outs,
        in_specs=[vmem] * 13,
        out_specs=(vmem,) * 6,
        scratch_shapes=scratch,
        compiler_params=pltpu.CompilerParams(vmem_limit_bytes=60 * 1024 * 1024, **extra),
    )(
        state.reshape(C, LON, LAT),
        cot.reshape(C, LON, LAT),
        sea,
        taps.transpose(1, 2, 0),
        gain.reshape(1, C),
        win,
        wout.T,
        *spectral_constants(),
    )
    anywhere = pl.BlockSpec(memory_space=pl.ANY)
    return pl.pallas_call(
        deliver,
        out_shape=outs,
        in_specs=[anywhere] * 6,
        out_specs=(anywhere,) * 6,
        scratch_shapes=[pltpu.VMEM(out.shape, out.dtype) for out in outs]
        + [pltpu.SemaphoreType.DMA((2, 6))],
    )(*results)


def solution(mesh):
    n_lon, n_sample = mesh.shape["lon"], mesh.shape["sample"]
    factor = 1.0 / math.sqrt(n_sample * n_lon * LON * LAT)

    def on_device(state, cot, sea, taps, gain, win, wout):
        out = block(n_lon, n_sample, factor, state, cot, sea, taps, gain, win, wout)
        shape = state.shape
        return (
            out[0].reshape(shape),
            out[1].reshape(shape),
            out[2],
            out[3].T,
            out[4].transpose(2, 0, 1),
            out[5].reshape(OWN),
        )

    slab = P("sample", None, "lon", None)
    return jax.shard_map(
        on_device,
        mesh=mesh,
        in_specs=(slab, slab, P("lon", None), P(), P(), P(), P()),
        out_specs=(
            slab,
            slab,
            P("sample", None),
            P(None, "sample"),
            P("sample", None, None),
            P("sample"),
        ),
        check_vma=False,
    )
```

```python
import functools
import math

import jax
import jax.numpy as jnp
import numpy as np
from jax import lax
from jax.experimental import pallas as pl
from jax.experimental.pallas import tpu as pltpu
from jax.sharding import PartitionSpec as P

C = 192
HID = 768
LON = 16
LAT = 128
PERIOD = 131
SPEC = 256
TAPS = 7
HALO = 3
GROUP = 4
HID_BLOCK = 256
CELL_BLOCK = 256
TILE = 16
OWN = 12
PACKED = 1152
BF = jnp.bfloat16
F32 = jnp.float32
MESH = pl.DeviceIdType.MESH


def tree_sum(terms):
    while len(terms) > 1:
        paired = [terms[k] + terms[k + 1] for k in range(0, len(terms) - 1, 2)]
        if len(terms) % 2:
            paired.append(terms[-1])
        terms = paired
    return terms[0]


def matmul(left, right):
    return jnp.dot(left, right, preferred_element_type=F32)


def matmul_nt(left, right):
    return lax.dot_general(left, right, (((1,), (1,)), ((), ())), preferred_element_type=F32)


def split_constant(values):
    high = values.astype(BF)
    low = (values - high.astype(np.float64)).astype(BF)
    return high, low


def spectral_constants():
    angle = 2.0 * math.pi / PERIOD
    row = np.arange(LAT)
    field_f, field_b = np.zeros((LAT, SPEC)), np.zeros((LAT, SPEC))
    back_f, back_b = np.zeros((SPEC, LAT)), np.zeros((SPEC, LAT))
    taps = np.zeros((8, SPEC))
    shift = np.arange(TAPS) - HALO
    field_f[:, 0] = field_b[:, 0] = 1.0
    back_f[0] = back_b[0] = 1.0 / PERIOD
    taps[:TAPS, 0] = 1.0
    half = PERIOD // 2
    for f in range(1, half + 1):
        one, two, three = f, half + f, 2 * half + f
        cos, sin = np.cos(angle * f * row), np.sin(angle * f * row)
        c, d = np.cos(angle * f * shift), np.sin(angle * f * shift)
        taps[:TAPS, one], taps[:TAPS, two], taps[:TAPS, three] = c, d - c, c + d
        field_f[:, one], field_f[:, two], field_f[:, three] = cos - sin, cos, -sin
        field_b[:, one], field_b[:, two], field_b[:, three] = cos + sin, cos, sin
        scale = 2.0 / PERIOD
        back_f[one], back_f[two], back_f[three] = scale * (cos - sin), -scale * sin, -scale * cos
        back_b[one], back_b[two], back_b[three] = scale * (cos + sin), scale * sin, -scale * cos

    def stacked(values):
        return np.concatenate(split_constant(values), axis=0)

    def beside(values):
        return np.concatenate(split_constant(values), axis=1)

    spread_high, spread_low = np.zeros((64, TAPS * SPEC)), np.zeros((64, TAPS * SPEC))
    high, low = split_constant(taps)
    for a in range(TAPS):
        spread_high[8 * a : 8 * a + 8, a * SPEC : (a + 1) * SPEC] = high
        spread_low[8 * a : 8 * a + 8, a * SPEC : (a + 1) * SPEC] = low
    spread = np.concatenate([spread_high, spread_high, spread_low]).astype(BF)
    gather = np.zeros((SPEC, LAT))
    gather[:, :8] = taps.T
    return (
        spread,
        stacked(field_f),
        beside(back_f),
        np.concatenate([stacked(back_f.T), stacked(field_b)], axis=1),
        beside(back_b),
        beside(gather),
    )


def column(ref, at):
    return ref[pl.ds(at, C, stride=LON), :]


def kernel_body(
    n_lon,
    n_sample,
    factor,
    state_ref,
    sea_ref,
    taps_ref,
    gain_ref,
    cot_far,
    win_far,
    wout_far,
    spread_far,
    field_f_far,
    back_f_far,
    field_g_far,
    back_b_far,
    gather_far,
    sout_ref,
    gin_ref,
    gwin_ref,
    gwout_ref,
    gk_ref,
    gg_ref,
    cot_ref,
    win_ref,
    wout_t,
    spread,
    field_f,
    back_f,
    field_g,
    back_b,
    gather,
    x32,
    c32,
    xa,
    ga,
    xh,
    gh,
    gw,
    kf,
    dkf,
    flat_taps,
    sum_high,
    sum_low,
    gainb,
    win_t,
    wout,
    norm_all,
    cot_all,
    hid_all,
    gp_all,
    scaled_all,
    inv_all,
    acc_in,
    acc_out,
    acc_gain,
    dks,
    stage,
    wsend,
    wcore,
    wmid,
    wparts,
    wslab,
    ksend,
    kcore,
    kmid,
    kparts,
    kslab,
    kout,
    send,
    recv,
    near,
):
    fetches = [
        pltpu.make_async_copy(far, here, near.at[k])
        for k, (far, here) in enumerate(
            (
                (spread_far, spread),
                (field_f_far, field_f),
                (back_f_far, back_f),
                (win_far, win_ref),
                (wout_far, wout_t),
                (cot_far, cot_ref),
                (field_g_far, field_g),
                (back_b_far, back_b),
                (gather_far, gather),
            )
        )
    ]
    for fetch in fetches:
        fetch.start()
    remote = n_lon > 1
    if remote:
        lon = lax.axis_index("lon")
        sample = lax.axis_index("sample")
        core = lax.rem(sample, 2)
        owner = sample // 2
        n_own = n_sample // 2
        partner = {"sample": sample + 1 - 2 * core}
        right = {"lon": lax.rem(lon + 1, n_lon)}
        left = {"lon": lax.rem(lon + n_lon - 1, n_lon)}
        owners = [lax.rem(owner + d, n_own) for d in range(1, n_own)]
        slabs = [lax.rem(lon + d, n_lon) for d in range(1, n_lon)]
        peers = (
            [partner]
            + [{"sample": 2 * other + core} for other in owners]
            + [{"lon": other} for other in slabs]
        )
        barrier = pltpu.get_barrier_semaphore()
        for peer in peers:
            pl.semaphore_signal(barrier, inc=1, device_id=peer, device_id_type=MESH)

        def copy(src, dst, slot, peer):
            return pltpu.make_async_remote_copy(
                src_ref=src,
                dst_ref=dst,
                send_sem=send.at[slot],
                recv_sem=recv.at[slot],
                device_id=peer,
                device_id_type=MESH,
            )

    def halo_copies(ref, slot):
        return (
            copy(ref.at[pl.ds(LON, HALO)], ref.at[pl.ds(0, HALO)], slot, right),
            copy(ref.at[pl.ds(HALO, HALO)], ref.at[pl.ds(LON + HALO, HALO)], slot + 1, left),
        )

    def local_halo(ref):
        ref[0:HALO] = ref[LON : LON + HALO]
        ref[LON + HALO : LON + 2 * HALO] = ref[HALO : 2 * HALO]

    x32[...] = state_ref[...].astype(F32).reshape(C * LON, LAT)
    for i in (0, 1, 2, 13, 14, 15):
        xa[HALO + i] = column(x32, i).astype(BF)
    if remote:
        pl.semaphore_wait(barrier, len(peers))
        x_right, x_left = halo_copies(xa, 0)
        x_left.start()
        x_right.start()
    for i in range(3, 13):
        xa[HALO + i] = column(x32, i).astype(BF)
    for fetch in fetches:
        fetch.wait()
    c32[...] = cot_ref[...].astype(F32).reshape(C * LON, LAT)

    flat_taps[...] = jnp.zeros_like(flat_taps)
    for a in range(TAPS):
        flat_taps[8 * a : 8 * a + TAPS, 0:C] = taps_ref[a]
    rest = flat_taps[...].T[0:C, :]
    high = rest.astype(BF)
    low = (rest - high.astype(F32)).astype(BF)
    kf[...] = matmul(
        jnp.concatenate([high[:, 0:64], low[:, 0:64], high[:, 0:64]], axis=1), spread[...]
    )
    gainb[...] = jnp.broadcast_to(gain_ref[...], (LAT, C)).T
    win_t[...] = (0.5 * win_ref[...].astype(F32)).astype(BF).T
    wout[...] = (0.5 * wout_t[...].astype(F32)).astype(BF).T
    acc_gain[...] = jnp.zeros_like(acc_gain)

    def doubled(columns):
        flat = columns.reshape(-1, LAT)
        return jnp.concatenate([flat, flat], axis=1)

    def field_spectrum(at, count):
        spectrum = matmul(doubled(xa[at : at + count]), field_f[...])
        xh[at : at + count] = spectrum.reshape(count, C, SPEC)

    def grad_spectrum(at, count):
        spectrum = matmul(doubled(ga[at : at + count]), field_g[:, SPEC:])
        gh[at : at + count] = spectrum.reshape(count, C, SPEC)

    def filtered(field, col, flip, inverse):
        def one_tile(tile, carry):
            at = pl.multiple_of(tile * TILE, TILE)
            for half in range(0, SPEC, LAT):
                window = field[pl.ds(col, GROUP + 2 * HALO), pl.ds(at, TILE), half : half + LAT]
                terms = []
                for a in range(TAPS):
                    first = 2 * HALO - a if flip else a
                    lane = a * SPEC + half
                    weight = kf[pl.ds(at, TILE), lane : lane + LAT]
                    terms.append(weight[None] * window[first : first + GROUP])
                total = tree_sum(terms)
                high = total.astype(BF)
                sum_high[:, pl.ds(at, TILE), half : half + LAT] = high
                sum_low[:, pl.ds(at, TILE), half : half + LAT] = (
                    total - high.astype(F32)
                ).astype(BF)
            return carry

        lax.fori_loop(0, C // TILE, one_tile, 0, unroll=2)
        main = matmul(sum_high[...].reshape(GROUP * C, SPEC), inverse[...])
        rest = matmul(sum_low[...].reshape(GROUP * C, SPEC), inverse[:, 0:LAT])
        return (main[:, 0:LAT] + main[:, LAT:] + rest).reshape(GROUP, C, LAT)

    def masks(col):
        return [sea_ref[pl.ds(col + k, 1), :].astype(F32) for k in range(GROUP)]

    def side_by_side(parts):
        return jnp.concatenate([parts[k] for k in range(GROUP)], axis=1)

    def lanes_of(col):
        return pl.ds(pl.multiple_of(col * LAT, GROUP * LAT), GROUP * LAT)

    def forward_group(col):
        mixed = filtered(xh, col, False, back_f)
        centred = mixed - jnp.mean(mixed, axis=1, keepdims=True)
        variance = jnp.mean(centred * centred, axis=1, keepdims=True)
        inv_scale = lax.rsqrt(variance + 1e-06)
        scaled = centred * inv_scale
        scaled_all[pl.ds(col, GROUP)] = scaled
        inv_all[pl.ds(col, GROUP), :] = inv_scale.reshape(GROUP, LAT)
        normed = side_by_side((scaled * gainb[...][None]).astype(BF))
        mask = masks(col)
        grad_out = side_by_side([(column(c32, col + k) * mask[k]).astype(BF) for k in range(GROUP)])
        where = lanes_of(col)
        norm_all[:, where] = normed
        cot_all[:, where] = grad_out
        for h in range(0, HID, HID_BLOCK):
            for n in range(0, GROUP * LAT, CELL_BLOCK):
                half = matmul(win_t[h : h + HID_BLOCK, :], normed[:, n : n + CELL_BLOCK])
                grad_half = matmul(wout[h : h + HID_BLOCK, :], grad_out[:, n : n + CELL_BLOCK])
                square = half * half
                bent = jnp.tanh(half * (1.5957691216057308 + 0.28541926509040104 * square))
                gate = 1.0 + bent
                hidden = half * gate
                slope = gate + hidden * (1.0 - bent) * (
                    1.5957691216057308 + 0.8562577952712031 * square
                )
                at = pl.ds(pl.multiple_of(col * LAT + n, CELL_BLOCK), CELL_BLOCK)
                hid_all[h : h + HID_BLOCK, at] = hidden.astype(BF)
                gp_all[h : h + HID_BLOCK, at] = (grad_half * slope).astype(BF)

    def finish_state(col):
        mask = masks(col)
        branch = matmul(wout_t[...], hid_all[:, lanes_of(col)])
        for k in range(GROUP):
            lane = slice(k * LAT, (k + 1) * LAT)
            at = pl.ds(col + k, C, stride=LON)
            x32[at, :] = mask[k] * (x32[at, :] + branch[:, lane])

    def backward_mlp(col):
        where = lanes_of(col)
        gain = gainb[...]
        grad_normed = matmul(win_ref[...], gp_all[:, where])
        for k in range(GROUP):
            lane = slice(k * LAT, (k + 1) * LAT)
            scaled = scaled_all[col + k]
            grad = grad_normed[:, lane]
            product = grad * scaled
            acc_gain[...] += product
            grad_scaled = grad * gain
            first = jnp.mean(grad_scaled, axis=0, keepdims=True)
            second = jnp.mean(product * gain, axis=0, keepdims=True)
            inv_scale = inv_all[pl.ds(col + k, 1), :]
            grad_conv = (inv_scale * (grad_scaled - first - scaled * second)).astype(BF)
            ga[HALO + col + k] = grad_conv
            spectrum = matmul(doubled(grad_conv), field_g[...])
            gw[col + k] = spectrum[:, 0:SPEC]
            gh[HALO + col + k] = spectrum[:, SPEC:]

    def in_groups(first, last, work):
        def one_group(step, carry):
            work(lax.rem(GROUP + step * GROUP, LON))
            return carry

        lax.fori_loop(first, last, one_group, 0)

    def start(copies):
        for one in copies:
            one.start()

    def wait(copies):
        for one in copies:
            one.wait()

    for at in range(HALO, LON + HALO, GROUP):
        field_spectrum(at, GROUP)
    def filter_grads(parts, fresh):
        def one_tile(tile, carry):
            at = pl.multiple_of(tile * 8, 8)
            for half in range(0, SPEC, LAT):
                lanes = slice(half, half + LAT)
                for a in range(TAPS):
                    spot = slice(a * SPEC + half, a * SPEC + half + LAT)
                    total = 0.0 if fresh else dkf[pl.ds(at, 8), spot]
                    for col, count in parts:
                        grads = gw[col : col + count, pl.ds(at, 8), lanes]
                        field = xh[col + a : col + a + count, pl.ds(at, 8), lanes]
                        total = total + jnp.sum(grads * field, axis=0)
                    dkf[pl.ds(at, 8), spot] = total
            return carry

        lax.fori_loop(0, C // 8, one_tile, 0, unroll=2)

    in_groups(0, 2, forward_group)
    in_groups(0, 2, backward_mlp)
    filter_grads([(GROUP, 2 * GROUP)], True)
    cells = slice(GROUP * LAT, 3 * GROUP * LAT)
    acc_out[...] = matmul_nt(cot_all[:, cells], hid_all[:, cells])
    acc_in[...] = matmul_nt(norm_all[:, cells], gp_all[:, cells])
    if remote:
        g_right, g_left = halo_copies(ga, 2)
        x_left.wait()
    else:
        local_halo(xa)
    field_spectrum(LON + HALO, HALO)
    forward_group(LON - GROUP)
    backward_mlp(LON - GROUP)
    if remote:
        g_right.start()
        x_right.wait()
    field_spectrum(0, HALO)
    forward_group(0)
    backward_mlp(0)
    if remote:
        g_left.start()

    for cells in (slice(0, GROUP * LAT), slice(3 * GROUP * LAT, LON * LAT)):
        acc_out[...] += matmul_nt(cot_all[:, cells], hid_all[:, cells])
        acc_in[...] += matmul_nt(norm_all[:, cells], gp_all[:, cells])
    wide = HID // 2
    for o in range(16):
        at = OWN * o
        stage[o, 0:12, 0:HID] = acc_in[at : at + 12, :]
        stage[o, 12:16, 0:HID] = acc_out[at : at + 4, :]
        stage[o, 0:8, HID:PACKED] = acc_out[at + 4 : at + 12, 0:wide]
        stage[o, 8:16, HID:PACKED] = acc_out[at + 4 : at + 12, wide:HID]
    for o in range(16):
        wsend[o % 2, o // 2] = stage[o].astype(BF)

    if remote:

        def to_slabs(slab, base):
            return [
                copy(slab.at[lon], slab.at[lon], base + d, {"lon": other})
                for d, other in enumerate(slabs)
            ]

        def to_owners(source, target, base):
            return [
                copy(source.at[other], target.at[d], base + d, {"sample": 2 * other + core})
                for d, other in enumerate(owners)
            ]

        def w_core():
            return [copy(wsend.at[1 - core], wcore, 4, partner)]

        def w_own():
            return to_owners(wmid, wparts, 5)

        def w_all():
            return to_slabs(wslab, 12)

        def k_core():
            return [copy(ksend.at[1 - core], kcore, 19, partner)]

        def k_own():
            return to_owners(kmid, kparts, 20)

        def k_all():
            return to_slabs(kslab, 27)

        start(w_core())
    filter_grads([(0, GROUP), (3 * GROUP, GROUP)], False)
    if remote:
        wait(w_core())
        wmid[...] = (wsend[core].astype(F32) + wcore[...].astype(F32)).astype(BF)
        start(w_own())

    lanes = lax.broadcasted_iota(jnp.int32, (C, LAT), 1)
    total = jnp.where(lanes == TAPS * TAPS, jnp.sum(acc_gain[...], axis=1, keepdims=True), 0.0)
    for a in range(TAPS):
        part = dkf[:, a * SPEC : (a + 1) * SPEC]
        high = part.astype(BF)
        low = (part - high.astype(F32)).astype(BF)
        both = matmul(high, gather[...])
        found = both[:, 0:LAT] + both[:, LAT:] + matmul(low, gather[:, 0:LAT])
        total = total + (pltpu.roll(found, a * TAPS, axis=1) if a else found)
    dks[0, 0:C, :] = total
    dks[1, 0:C, :] = pltpu.roll(total, LAT // 2, axis=1)
    for side in range(2):
        dks[side, C : C + 16, :] = jnp.zeros((16, LAT), F32)
    for o in range(16):
        at = OWN * o
        ksend[o % 2, o // 2] = dks[0, at : at + 8, :] + dks[1, at + 6 : at + 14, :]
    if remote:
        start(k_core())
    in_groups(0, 4, finish_state)
    if remote:
        wait(k_core())
        kmid[...] = ksend[core] + kcore[...]
        start(k_own())

    def backward_group(col):
        moved = filtered(gh, col, True, back_b)
        mask = masks(col)
        for k in range(GROUP):
            at = pl.ds(col + k, C, stride=LON)
            c32[at, :] = c32[at, :] * mask[k] + moved[k]

    in_groups(0, 2, backward_group)
    if remote:
        g_right.wait()
    else:
        local_halo(ga)
    grad_spectrum(0, HALO)
    backward_group(0)
    if remote:
        wait(w_own())
        held = wmid[owner].astype(F32)
        for d in range(len(owners)):
            held = held + wparts[d].astype(F32)
        wslab[lon] = held.astype(BF)
        start(w_all())
        wait(k_own())
        held = kmid[owner]
        for d in range(len(owners)):
            held = held + kparts[d]
        kslab[lon] = held
        start(k_all())
        g_left.wait()
    grad_spectrum(LON + HALO, HALO)
    backward_group(LON - GROUP)
    sout_ref[...] = x32[...].reshape(C, LON, LAT).astype(BF)
    gin_ref[...] = c32[...].reshape(C, LON, LAT).astype(BF)
    if remote:
        wait(w_all())
        weights = wslab[0].astype(F32)
        for other in range(1, n_lon):
            weights = weights + wslab[other].astype(F32)
        wait(k_all())
        small = kslab[0]
        for other in range(1, n_lon):
            small = small + kslab[other]
    else:
        weights = wsend[0, 0].astype(F32)
        small = ksend[0, 0]
    weights = weights * factor
    small = small * factor
    gwin_ref[...] = weights[0:12, 0:HID]
    gwout_ref[0:4, :] = weights[12:16, 0:HID]
    gwout_ref[4:12, 0:wide] = weights[0:8, HID:PACKED]
    gwout_ref[4:12, wide:HID] = weights[8:16, HID:PACKED]
    kout[0:6, :] = small[0:6, :]
    kout[6:12, :] = pltpu.roll(small, LAT // 2, axis=1)[0:6, :]
    small_t = kout[...].T
    for a in range(TAPS):
        gk_ref[a] = small_t[a * TAPS : (a + 1) * TAPS, 0:OWN]
    gg_ref[...] = small_t[TAPS * TAPS : TAPS * TAPS + 1, 0:OWN]


def deliver(*refs):
    count = len(refs) // 3
    sems = refs[-1]
    sources, targets, held = refs[:count], refs[count : 2 * count], refs[2 * count : 3 * count]
    arrive = [pltpu.make_async_copy(sources[k], held[k], sems.at[0, k]) for k in range(count)]
    leave = [pltpu.make_async_copy(held[k], targets[k], sems.at[1, k]) for k in range(count)]
    for one in arrive:
        one.start()
    for k in range(count):
        arrive[k].wait()
        leave[k].start()
    for one in leave:
        one.wait()


def block(n_lon, n_sample, factor, state, cot, sea, taps, gain, win, wout):
    vmem = pl.BlockSpec(memory_space=pltpu.VMEM)
    far = pl.BlockSpec(memory_space=pltpu.HBM)
    shape = jax.ShapeDtypeStruct
    outs = (
        shape((C, LON, LAT), BF),
        shape((C, LON, LAT), BF),
        shape((OWN, HID), F32),
        shape((OWN, HID), F32),
        shape((TAPS, TAPS, OWN), F32),
        shape((1, OWN), F32),
    )
    scratch = [
        pltpu.VMEM((C, LON, LAT), BF),
        pltpu.VMEM((C, HID), BF),
        pltpu.VMEM((C, HID), BF),
        pltpu.VMEM((3 * 64, TAPS * SPEC), BF),
        pltpu.VMEM((2 * LAT, SPEC), BF),
        pltpu.VMEM((SPEC, 2 * LAT), BF),
        pltpu.VMEM((2 * LAT, 2 * SPEC), BF),
        pltpu.VMEM((SPEC, 2 * LAT), BF),
        pltpu.VMEM((SPEC, 2 * LAT), BF),
        pltpu.VMEM((C * LON, LAT), F32),
        pltpu.VMEM((C * LON, LAT), F32),
        pltpu.VMEM((LON + 2 * HALO, C, LAT), BF),
        pltpu.VMEM((LON + 2 * HALO, C, LAT), BF),
        pltpu.VMEM((LON + 2 * HALO, C, SPEC), F32),
        pltpu.VMEM((LON + 2 * HALO, C, SPEC), F32),
        pltpu.VMEM((LON, C, SPEC), F32),
        pltpu.VMEM((C, TAPS * SPEC), F32),
        pltpu.VMEM((C, TAPS * SPEC), F32),
        pltpu.VMEM((LAT, 2 * LAT), F32),
        pltpu.VMEM((GROUP, C, SPEC), BF),
        pltpu.VMEM((GROUP, C, SPEC), BF),
        pltpu.VMEM((C, LAT), F32),
        pltpu.VMEM((HID, C), BF),
        pltpu.VMEM((HID, C), BF),
        pltpu.VMEM((C, LON * LAT), BF),
        pltpu.VMEM((C, LON * LAT), BF),
        pltpu.VMEM((HID, LON * LAT), BF),
        pltpu.VMEM((HID, LON * LAT), BF),
        pltpu.VMEM((LON, C, LAT), F32),
        pltpu.VMEM((LON, LAT), F32),
        pltpu.VMEM((C, HID), F32),
        pltpu.VMEM((C, HID), F32),
        pltpu.VMEM((C, LAT), F32),
        pltpu.VMEM((2, C + 16, LAT), F32),
        pltpu.VMEM((16, 16, PACKED), F32),
        pltpu.VMEM((2, 8, 16, PACKED), BF),
        pltpu.VMEM((8, 16, PACKED), BF),
        pltpu.VMEM((8, 16, PACKED), BF),
        pltpu.VMEM((7, 16, PACKED), BF),
        pltpu.VMEM((8, 16, PACKED), BF),
        pltpu.VMEM((2, 8, 8, LAT), F32),
        pltpu.VMEM((8, 8, LAT), F32),
        pltpu.VMEM((8, 8, LAT), F32),
        pltpu.VMEM((7, 8, LAT), F32),
        pltpu.VMEM((8, 8, LAT), F32),
        pltpu.VMEM((16, LAT), F32),
        pltpu.SemaphoreType.DMA((34,)),
        pltpu.SemaphoreType.DMA((34,)),
        pltpu.SemaphoreType.DMA((9,)),
    ]
    extra = dict(collective_id=0, has_side_effects=True) if n_lon > 1 else {}
    results = pl.pallas_call(
        functools.partial(kernel_body, n_lon, n_sample, factor),
        out_shape=outs,
        in_specs=[vmem] * 4 + [far] * 9,
        out_specs=(vmem,) * 6,
        scratch_shapes=scratch,
        compiler_params=pltpu.CompilerParams(vmem_limit_bytes=62 * 1024 * 1024, **extra),
    )(
        state.reshape(C, LON, LAT),
        sea,
        taps.transpose(1, 2, 0),
        gain.reshape(1, C),
        cot.reshape(C, LON, LAT),
        win,
        wout.T,
        *spectral_constants(),
    )
    anywhere = pl.BlockSpec(memory_space=pl.ANY)
    return pl.pallas_call(
        deliver,
        out_shape=outs,
        in_specs=[anywhere] * 6,
        out_specs=(anywhere,) * 6,
        scratch_shapes=[pltpu.VMEM(out.shape, out.dtype) for out in outs]
        + [pltpu.SemaphoreType.DMA((2, 6))],
    )(*results)


def solution(mesh):
    n_lon, n_sample = mesh.shape["lon"], mesh.shape["sample"]
    factor = 1.0 / math.sqrt(n_sample * n_lon * LON * LAT)

    def on_device(state, cot, sea, taps, gain, win, wout):
        out = block(n_lon, n_sample, factor, state, cot, sea, taps, gain, win, wout)
        shape = state.shape
        return (
            out[0].reshape(shape),
            out[1].reshape(shape),
            out[2],
            out[3].T,
            out[4].transpose(2, 0, 1),
            out[5].reshape(OWN),
        )

    slab = P("sample", None, "lon", None)
    return jax.shard_map(
        on_device,
        mesh=mesh,
        in_specs=(slab, slab, P("lon", None), P(), P(), P(), P()),
        out_specs=(
            slab,
            slab,
            P("sample", None),
            P(None, "sample"),
            P("sample", None, None),
            P("sample"),
        ),
        check_vma=False,
    )
```

```python
import functools
import math

import jax
import jax.numpy as jnp
import numpy as np
from jax import lax
from jax.experimental import pallas as pl
from jax.experimental.pallas import tpu as pltpu
from jax.sharding import PartitionSpec as P

C = 192
HID = 768
LON = 16
LAT = 128
PERIOD = 131
SPEC = 256
TAPS = 7
HALO = 3
GROUP = 4
HID_BLOCK = 256
CELL_BLOCK = 256
TILE = 16
OWN = 12
PACKED = 1152
PIECES = PACKED // LAT
BF = jnp.bfloat16
F32 = jnp.float32
MESH = pl.DeviceIdType.MESH


def tree_sum(terms):
    while len(terms) > 1:
        paired = [terms[k] + terms[k + 1] for k in range(0, len(terms) - 1, 2)]
        if len(terms) % 2:
            paired.append(terms[-1])
        terms = paired
    return terms[0]


def matmul(left, right):
    return jnp.dot(left, right, preferred_element_type=F32)


def matmul_nt(left, right):
    return lax.dot_general(left, right, (((1,), (1,)), ((), ())), preferred_element_type=F32)


def split_constant(values):
    high = values.astype(BF)
    low = (values - high.astype(np.float64)).astype(BF)
    return high, low


def spectral_constants():
    angle = 2.0 * math.pi / PERIOD
    row = np.arange(LAT)
    field_f, field_b = np.zeros((LAT, SPEC)), np.zeros((LAT, SPEC))
    back_f, back_b = np.zeros((SPEC, LAT)), np.zeros((SPEC, LAT))
    taps = np.zeros((8, SPEC))
    shift = np.arange(TAPS) - HALO
    field_f[:, 0] = field_b[:, 0] = 1.0
    back_f[0] = back_b[0] = 1.0 / PERIOD
    taps[:TAPS, 0] = 1.0
    half = PERIOD // 2
    for f in range(1, half + 1):
        one, two, three = f, half + f, 2 * half + f
        cos, sin = np.cos(angle * f * row), np.sin(angle * f * row)
        c, d = np.cos(angle * f * shift), np.sin(angle * f * shift)
        taps[:TAPS, one], taps[:TAPS, two], taps[:TAPS, three] = c, d - c, c + d
        field_f[:, one], field_f[:, two], field_f[:, three] = cos - sin, cos, -sin
        field_b[:, one], field_b[:, two], field_b[:, three] = cos + sin, cos, sin
        scale = 2.0 / PERIOD
        back_f[one], back_f[two], back_f[three] = scale * (cos - sin), -scale * sin, -scale * cos
        back_b[one], back_b[two], back_b[three] = scale * (cos + sin), scale * sin, -scale * cos

    def stacked(values):
        return np.concatenate(split_constant(values), axis=0)

    def beside(values):
        return np.concatenate(split_constant(values), axis=1)

    spread_high, spread_low = np.zeros((64, TAPS * SPEC)), np.zeros((64, TAPS * SPEC))
    high, low = split_constant(taps)
    for a in range(TAPS):
        spread_high[8 * a : 8 * a + 8, a * SPEC : (a + 1) * SPEC] = high
        spread_low[8 * a : 8 * a + 8, a * SPEC : (a + 1) * SPEC] = low
    spread = np.concatenate([spread_high, spread_high, spread_low]).astype(BF)
    gather = np.zeros((SPEC, LAT))
    gather[:, :8] = taps.T
    return (
        spread,
        stacked(field_f),
        beside(back_f),
        np.concatenate([stacked(back_f.T), stacked(field_b)], axis=1),
        beside(back_b),
        beside(gather),
    )


def column(ref, at):
    return ref[pl.ds(at, C, stride=LON), :]


def kernel_body(
    n_lon,
    n_sample,
    factor,
    state_ref,
    sea_ref,
    taps_ref,
    gain_ref,
    cot_far,
    win_far,
    wout_far,
    spread_far,
    field_f_far,
    back_f_far,
    field_g_far,
    back_b_far,
    gather_far,
    sout_ref,
    gin_ref,
    gwin_ref,
    gwout_ref,
    gk_ref,
    gg_ref,
    cot_ref,
    win_ref,
    wout_t,
    spread,
    field_f,
    back_f,
    field_g,
    back_b,
    gather,
    x32,
    c32,
    xa,
    ga,
    xh,
    gh,
    gw,
    kf,
    dkf,
    flat_taps,
    sum_high,
    sum_low,
    gainb,
    win_t,
    wout,
    norm_all,
    cot_all,
    hid_all,
    gp_all,
    scaled_all,
    inv_all,
    acc_in,
    acc_out,
    acc_gain,
    dks,
    stage,
    wsend,
    wcore,
    wmid,
    wparts,
    bsend,
    bparts,
    wslab,
    ksend,
    kcore,
    kmid,
    kparts,
    kslab,
    kout,
    send,
    recv,
    near,
):
    fetches = [
        pltpu.make_async_copy(far, here, near.at[k])
        for k, (far, here) in enumerate(
            (
                (spread_far, spread),
                (field_f_far, field_f),
                (back_f_far, back_f),
                (win_far, win_ref),
                (wout_far, wout_t),
                (cot_far, cot_ref),
                (field_g_far, field_g),
                (back_b_far, back_b),
                (gather_far, gather),
            )
        )
    ]
    remote = n_lon > 1
    if remote:
        lon = lax.axis_index("lon")
        sample = lax.axis_index("sample")
        core = lax.rem(sample, 2)
        owner = sample // 2
        n_own = n_sample // 2
        partner = {"sample": sample + 1 - 2 * core}
        right = {"lon": lax.rem(lon + 1, n_lon)}
        left = {"lon": lax.rem(lon + n_lon - 1, n_lon)}
        owners = [lax.rem(owner + d, n_own) for d in range(1, n_own)]
        slabs = [lax.rem(lon + d, n_lon) for d in range(1, n_lon)]
        peers = (
            [partner]
            + [{"sample": 2 * other + core} for other in owners]
            + [{"lon": other} for other in slabs]
        )
        barrier = pltpu.get_barrier_semaphore()
        for peer in peers:
            pl.semaphore_signal(barrier, inc=1, device_id=peer, device_id_type=MESH)

        def copy(src, dst, slot, peer):
            return pltpu.make_async_remote_copy(
                src_ref=src,
                dst_ref=dst,
                send_sem=send.at[slot],
                recv_sem=recv.at[slot],
                device_id=peer,
                device_id_type=MESH,
            )

    def halo_copies(ref, slot):
        return (
            copy(ref.at[pl.ds(LON, HALO)], ref.at[pl.ds(0, HALO)], slot, right),
            copy(ref.at[pl.ds(HALO, HALO)], ref.at[pl.ds(LON + HALO, HALO)], slot + 1, left),
        )

    def local_halo(ref):
        ref[0:HALO] = ref[LON : LON + HALO]
        ref[LON + HALO : LON + 2 * HALO] = ref[HALO : 2 * HALO]

    x32[...] = state_ref[...].astype(F32).reshape(C * LON, LAT)
    for i in (0, 1, 2, 13, 14, 15):
        xa[HALO + i] = column(x32, i).astype(BF)
    if remote:
        pl.semaphore_wait(barrier, len(peers))
        x_right, x_left = halo_copies(xa, 0)
        x_left.start()
        x_right.start()
    for fetch in fetches:
        fetch.start()
    for i in range(3, 13):
        xa[HALO + i] = column(x32, i).astype(BF)
    for fetch in fetches:
        fetch.wait()
    c32[...] = cot_ref[...].astype(F32).reshape(C * LON, LAT)

    flat_taps[...] = jnp.zeros_like(flat_taps)
    for a in range(TAPS):
        flat_taps[8 * a : 8 * a + TAPS, 0:C] = taps_ref[a]
    rest = flat_taps[...].T[0:C, :]
    high = rest.astype(BF)
    low = (rest - high.astype(F32)).astype(BF)
    kf[...] = matmul(
        jnp.concatenate([high[:, 0:64], low[:, 0:64], high[:, 0:64]], axis=1), spread[...]
    )
    gainb[...] = jnp.broadcast_to(gain_ref[...], (LAT, C)).T
    win_t[...] = (0.5 * win_ref[...].astype(F32)).astype(BF).T
    wout[...] = (0.5 * wout_t[...].astype(F32)).astype(BF).T
    acc_gain[...] = jnp.zeros_like(acc_gain)

    def doubled(columns):
        flat = columns.reshape(-1, LAT)
        return jnp.concatenate([flat, flat], axis=1)

    def field_spectrum(at, count):
        spectrum = matmul(doubled(xa[at : at + count]), field_f[...])
        xh[at : at + count] = spectrum.reshape(count, C, SPEC)

    def grad_spectrum(at, count):
        spectrum = matmul(doubled(ga[at : at + count]), field_g[:, SPEC:])
        gh[at : at + count] = spectrum.reshape(count, C, SPEC)

    def filtered(field, col, flip, inverse):
        def one_tile(tile, carry):
            at = pl.multiple_of(tile * TILE, TILE)
            for half in range(0, SPEC, LAT):
                window = field[pl.ds(col, GROUP + 2 * HALO), pl.ds(at, TILE), half : half + LAT]
                terms = []
                for a in range(TAPS):
                    first = 2 * HALO - a if flip else a
                    lane = a * SPEC + half
                    weight = kf[pl.ds(at, TILE), lane : lane + LAT]
                    terms.append(weight[None] * window[first : first + GROUP])
                total = tree_sum(terms)
                high = total.astype(BF)
                sum_high[:, pl.ds(at, TILE), half : half + LAT] = high
                sum_low[:, pl.ds(at, TILE), half : half + LAT] = (
                    total - high.astype(F32)
                ).astype(BF)
            return carry

        lax.fori_loop(0, C // TILE, one_tile, 0, unroll=2)
        main = matmul(sum_high[...].reshape(GROUP * C, SPEC), inverse[...])
        rest = matmul(sum_low[...].reshape(GROUP * C, SPEC), inverse[:, 0:LAT])
        return (main[:, 0:LAT] + main[:, LAT:] + rest).reshape(GROUP, C, LAT)

    def masks(col):
        return [sea_ref[pl.ds(col + k, 1), :].astype(F32) for k in range(GROUP)]

    def side_by_side(parts):
        return jnp.concatenate([parts[k] for k in range(GROUP)], axis=1)

    def lanes_of(col):
        return pl.ds(pl.multiple_of(col * LAT, GROUP * LAT), GROUP * LAT)

    def forward_group(col):
        mixed = filtered(xh, col, False, back_f)
        centred = mixed - jnp.mean(mixed, axis=1, keepdims=True)
        variance = jnp.mean(centred * centred, axis=1, keepdims=True)
        inv_scale = lax.rsqrt(variance + 1e-06)
        scaled = centred * inv_scale
        scaled_all[pl.ds(col, GROUP)] = scaled
        inv_all[pl.ds(col, GROUP), :] = inv_scale.reshape(GROUP, LAT)
        normed = side_by_side((scaled * gainb[...][None]).astype(BF))
        mask = masks(col)
        grad_out = side_by_side([(column(c32, col + k) * mask[k]).astype(BF) for k in range(GROUP)])
        where = lanes_of(col)
        norm_all[:, where] = normed
        cot_all[:, where] = grad_out
        for h in range(0, HID, HID_BLOCK):
            for n in range(0, GROUP * LAT, CELL_BLOCK):
                half = matmul(win_t[h : h + HID_BLOCK, :], normed[:, n : n + CELL_BLOCK])
                grad_half = matmul(wout[h : h + HID_BLOCK, :], grad_out[:, n : n + CELL_BLOCK])
                square = half * half
                bent = jnp.tanh(half * (1.5957691216057308 + 0.28541926509040104 * square))
                gate = 1.0 + bent
                hidden = half * gate
                slope = gate + hidden * (1.0 - bent) * (
                    1.5957691216057308 + 0.8562577952712031 * square
                )
                at = pl.ds(pl.multiple_of(col * LAT + n, CELL_BLOCK), CELL_BLOCK)
                hid_all[h : h + HID_BLOCK, at] = hidden.astype(BF)
                gp_all[h : h + HID_BLOCK, at] = (grad_half * slope).astype(BF)

    def finish_state(col):
        mask = masks(col)
        branch = matmul(wout_t[...], hid_all[:, lanes_of(col)])
        for k in range(GROUP):
            lane = slice(k * LAT, (k + 1) * LAT)
            at = pl.ds(col + k, C, stride=LON)
            x32[at, :] = mask[k] * (x32[at, :] + branch[:, lane])

    def backward_mlp(col):
        where = lanes_of(col)
        gain = gainb[...]
        grad_normed = matmul(win_ref[...], gp_all[:, where])
        for k in range(GROUP):
            lane = slice(k * LAT, (k + 1) * LAT)
            scaled = scaled_all[col + k]
            grad = grad_normed[:, lane]
            product = grad * scaled
            acc_gain[...] += product
            grad_scaled = grad * gain
            first = jnp.mean(grad_scaled, axis=0, keepdims=True)
            second = jnp.mean(product * gain, axis=0, keepdims=True)
            inv_scale = inv_all[pl.ds(col + k, 1), :]
            grad_conv = (inv_scale * (grad_scaled - first - scaled * second)).astype(BF)
            ga[HALO + col + k] = grad_conv
            spectrum = matmul(doubled(grad_conv), field_g[...])
            gw[col + k] = spectrum[:, 0:SPEC]
            gh[HALO + col + k] = spectrum[:, SPEC:]

    def in_groups(first, last, work):
        def one_group(step, carry):
            work(lax.rem(GROUP + step * GROUP, LON))
            return carry

        lax.fori_loop(first, last, one_group, 0)

    def start(copies):
        for one in copies:
            one.start()

    def wait(copies):
        for one in copies:
            one.wait()

    for at in range(HALO, LON + HALO, GROUP):
        field_spectrum(at, GROUP)
    def filter_grads(parts, fresh):
        def one_tile(tile, carry):
            at = pl.multiple_of(tile * 8, 8)
            for half in range(0, SPEC, LAT):
                lanes = slice(half, half + LAT)
                for a in range(TAPS):
                    spot = slice(a * SPEC + half, a * SPEC + half + LAT)
                    total = 0.0 if fresh else dkf[pl.ds(at, 8), spot]
                    for col, count in parts:
                        grads = gw[col : col + count, pl.ds(at, 8), lanes]
                        field = xh[col + a : col + a + count, pl.ds(at, 8), lanes]
                        total = total + jnp.sum(grads * field, axis=0)
                    dkf[pl.ds(at, 8), spot] = total
            return carry

        lax.fori_loop(0, C // 8, one_tile, 0, unroll=2)

    in_groups(0, 2, forward_group)
    in_groups(0, 2, backward_mlp)
    filter_grads([(GROUP, 2 * GROUP)], True)
    cells = slice(GROUP * LAT, 3 * GROUP * LAT)
    acc_out[...] = matmul_nt(cot_all[:, cells], hid_all[:, cells])
    acc_in[...] = matmul_nt(norm_all[:, cells], gp_all[:, cells])
    if remote:
        g_right, g_left = halo_copies(ga, 2)
        x_left.wait()
    else:
        local_halo(xa)
    field_spectrum(LON + HALO, HALO)
    forward_group(LON - GROUP)
    if remote:
        x_right.wait()
    field_spectrum(0, HALO)
    forward_group(0)

    for cells in (slice(0, GROUP * LAT), slice(3 * GROUP * LAT, LON * LAT)):
        acc_out[...] += matmul_nt(cot_all[:, cells], hid_all[:, cells])
        acc_in[...] += matmul_nt(norm_all[:, cells], gp_all[:, cells])
    wide = HID // 2
    for o in range(16):
        at = OWN * o
        stage[o, 0:12, 0:HID] = acc_in[at : at + 12, :]
        stage[o, 12:16, 0:HID] = acc_out[at : at + 4, :]
        stage[o, 0:8, HID:PACKED] = acc_out[at + 4 : at + 12, 0:wide]
        stage[o, 8:16, HID:PACKED] = acc_out[at + 4 : at + 12, wide:HID]
    for o in range(16):
        q = o // 2
        for t in range(PIECES):
            slot = q if t < 8 else 8
            wsend[o % 2, (q + t) % 8, slot] = stage[o, :, t * LAT : (t + 1) * LAT].astype(BF)

    if remote:

        def to_slabs(slab, base):
            return [
                copy(slab.at[lon], slab.at[lon], base + d, {"lon": other})
                for d, other in enumerate(slabs)
            ]

        def to_owners(source, target, base):
            return [
                copy(source.at[other], target.at[d], base + d, {"sample": 2 * other + core})
                for d, other in enumerate(owners)
            ]

        def w_core():
            return [copy(wsend.at[1 - core], wcore, 4, partner)]

        def w_lon():
            return [
                copy(wmid.at[other], wparts.at[d], 5 + d, {"lon": other})
                for d, other in enumerate(slabs)
            ]

        def w_own():
            return to_owners(bsend, bparts, 12)

        def w_all():
            return to_slabs(wslab, 19)

        def k_core():
            return [copy(ksend.at[1 - core], kcore, 26, partner)]

        def k_own():
            return to_owners(kmid, kparts, 27)

        def k_all():
            return to_slabs(kslab, 34)

        start(w_core())
    backward_mlp(LON - GROUP)
    if remote:
        g_right.start()
    backward_mlp(0)
    if remote:
        wait(w_core())
        wmid[...] = (wsend[core].astype(F32) + wcore[...].astype(F32)).astype(BF)
        start(w_lon())
        g_left.start()
    filter_grads([(0, GROUP), (3 * GROUP, GROUP)], False)

    lanes = lax.broadcasted_iota(jnp.int32, (C, LAT), 1)
    total = jnp.where(lanes == TAPS * TAPS, jnp.sum(acc_gain[...], axis=1, keepdims=True), 0.0)
    for a in range(TAPS):
        part = dkf[:, a * SPEC : (a + 1) * SPEC]
        high = part.astype(BF)
        low = (part - high.astype(F32)).astype(BF)
        both = matmul(high, gather[...])
        found = both[:, 0:LAT] + both[:, LAT:] + matmul(low, gather[:, 0:LAT])
        total = total + (pltpu.roll(found, a * TAPS, axis=1) if a else found)
    dks[0, 0:C, :] = total
    dks[1, 0:C, :] = pltpu.roll(total, LAT // 2, axis=1)
    for side in range(2):
        dks[side, C : C + 16, :] = jnp.zeros((16, LAT), F32)
    for o in range(16):
        at = OWN * o
        ksend[o % 2, o // 2] = dks[0, at : at + 8, :] + dks[1, at + 6 : at + 14, :]
    if remote:
        start(k_core())
    in_groups(0, 2, finish_state)
    if remote:
        wait(k_core())
        kmid[...] = ksend[core] + kcore[...]
        start(k_own())
    in_groups(2, 4, finish_state)

    def backward_group(col):
        moved = filtered(gh, col, True, back_b)
        mask = masks(col)
        for k in range(GROUP):
            at = pl.ds(col + k, C, stride=LON)
            c32[at, :] = c32[at, :] * mask[k] + moved[k]

    in_groups(0, 1, backward_group)
    if remote:
        wait(w_lon())
        total = wmid[lon].astype(F32)
        for d in range(len(slabs)):
            total = total + wparts[d].astype(F32)
        total = total.astype(BF)
        for q in range(8):
            bsend[q, 0] = total[q]
            bsend[q, 1] = total[8]
        start(w_own())
    in_groups(1, 2, backward_group)
    if remote:
        g_right.wait()
    else:
        local_halo(ga)
    grad_spectrum(0, HALO)
    backward_group(0)
    if remote:
        wait(k_own())
        held = kmid[owner]
        for d in range(len(owners)):
            held = held + kparts[d]
        kslab[lon] = held
        start(k_all())
        g_left.wait()
    grad_spectrum(LON + HALO, HALO)
    backward_group(LON - GROUP)
    if remote:
        wait(w_own())
        held = bsend[owner].astype(F32)
        for d in range(len(owners)):
            held = held + bparts[d].astype(F32)
        wslab[lon] = held.astype(BF)
        start(w_all())
    sout_ref[...] = x32[...].reshape(C, LON, LAT).astype(BF)
    gin_ref[...] = c32[...].reshape(C, LON, LAT).astype(BF)
    if remote:
        wait(k_all())
        small = kslab[0]
        for other in range(1, n_lon):
            small = small + kslab[other]
        wait(w_all())
        tiles = [wslab[lax.rem(owner + t, 8), 0] for t in range(8)] + [wslab[owner, 1]]
    else:
        tiles = [wsend[0, t % 8, 0 if t < 8 else 8] for t in range(PIECES)]
        small = ksend[0, 0]
    weights = jnp.concatenate(tiles, axis=1).astype(F32)
    weights = weights * factor
    small = small * factor
    gwin_ref[...] = weights[0:12, 0:HID]
    gwout_ref[0:4, :] = weights[12:16, 0:HID]
    gwout_ref[4:12, 0:wide] = weights[0:8, HID:PACKED]
    gwout_ref[4:12, wide:HID] = weights[8:16, HID:PACKED]
    kout[0:6, :] = small[0:6, :]
    kout[6:12, :] = pltpu.roll(small, LAT // 2, axis=1)[0:6, :]
    small_t = kout[...].T
    for a in range(TAPS):
        gk_ref[a] = small_t[a * TAPS : (a + 1) * TAPS, 0:OWN]
    gg_ref[...] = small_t[TAPS * TAPS : TAPS * TAPS + 1, 0:OWN]


def deliver(*refs):
    count = len(refs) // 3
    sems = refs[-1]
    sources, targets, held = refs[:count], refs[count : 2 * count], refs[2 * count : 3 * count]
    arrive = [pltpu.make_async_copy(sources[k], held[k], sems.at[0, k]) for k in range(count)]
    leave = [pltpu.make_async_copy(held[k], targets[k], sems.at[1, k]) for k in range(count)]
    for one in arrive:
        one.start()
    for k in range(count):
        arrive[k].wait()
        leave[k].start()
    for one in leave:
        one.wait()


def block(n_lon, n_sample, factor, state, cot, sea, taps, gain, win, wout):
    vmem = pl.BlockSpec(memory_space=pltpu.VMEM)
    far = pl.BlockSpec(memory_space=pltpu.HBM)
    shape = jax.ShapeDtypeStruct
    outs = (
        shape((C, LON, LAT), BF),
        shape((C, LON, LAT), BF),
        shape((OWN, HID), F32),
        shape((OWN, HID), F32),
        shape((TAPS, TAPS, OWN), F32),
        shape((1, OWN), F32),
    )
    scratch = [
        pltpu.VMEM((C, LON, LAT), BF),
        pltpu.VMEM((C, HID), BF),
        pltpu.VMEM((C, HID), BF),
        pltpu.VMEM((3 * 64, TAPS * SPEC), BF),
        pltpu.VMEM((2 * LAT, SPEC), BF),
        pltpu.VMEM((SPEC, 2 * LAT), BF),
        pltpu.VMEM((2 * LAT, 2 * SPEC), BF),
        pltpu.VMEM((SPEC, 2 * LAT), BF),
        pltpu.VMEM((SPEC, 2 * LAT), BF),
        pltpu.VMEM((C * LON, LAT), F32),
        pltpu.VMEM((C * LON, LAT), F32),
        pltpu.VMEM((LON + 2 * HALO, C, LAT), BF),
        pltpu.VMEM((LON + 2 * HALO, C, LAT), BF),
        pltpu.VMEM((LON + 2 * HALO, C, SPEC), F32),
        pltpu.VMEM((LON + 2 * HALO, C, SPEC), F32),
        pltpu.VMEM((LON, C, SPEC), F32),
        pltpu.VMEM((C, TAPS * SPEC), F32),
        pltpu.VMEM((C, TAPS * SPEC), F32),
        pltpu.VMEM((LAT, 2 * LAT), F32),
        pltpu.VMEM((GROUP, C, SPEC), BF),
        pltpu.VMEM((GROUP, C, SPEC), BF),
        pltpu.VMEM((C, LAT), F32),
        pltpu.VMEM((HID, C), BF),
        pltpu.VMEM((HID, C), BF),
        pltpu.VMEM((C, LON * LAT), BF),
        pltpu.VMEM((C, LON * LAT), BF),
        pltpu.VMEM((HID, LON * LAT), BF),
        pltpu.VMEM((HID, LON * LAT), BF),
        pltpu.VMEM((LON, C, LAT), F32),
        pltpu.VMEM((LON, LAT), F32),
        pltpu.VMEM((C, HID), F32),
        pltpu.VMEM((C, HID), F32),
        pltpu.VMEM((C, LAT), F32),
        pltpu.VMEM((2, C + 16, LAT), F32),
        pltpu.VMEM((16, 16, PACKED), F32),
        pltpu.VMEM((2, 8, PIECES, 16, LAT), BF),
        pltpu.VMEM((8, PIECES, 16, LAT), BF),
        pltpu.VMEM((8, PIECES, 16, LAT), BF),
        pltpu.VMEM((7, PIECES, 16, LAT), BF),
        pltpu.VMEM((8, 2, 16, LAT), BF),
        pltpu.VMEM((7, 2, 16, LAT), BF),
        pltpu.VMEM((8, 2, 16, LAT), BF),
        pltpu.VMEM((2, 8, 8, LAT), F32),
        pltpu.VMEM((8, 8, LAT), F32),
        pltpu.VMEM((8, 8, LAT), F32),
        pltpu.VMEM((7, 8, LAT), F32),
        pltpu.VMEM((8, 8, LAT), F32),
        pltpu.VMEM((16, LAT), F32),
        pltpu.SemaphoreType.DMA((41,)),
        pltpu.SemaphoreType.DMA((41,)),
        pltpu.SemaphoreType.DMA((9,)),
    ]
    extra = dict(collective_id=0, has_side_effects=True) if n_lon > 1 else {}
    results = pl.pallas_call(
        functools.partial(kernel_body, n_lon, n_sample, factor),
        out_shape=outs,
        in_specs=[vmem] * 4 + [far] * 9,
        out_specs=(vmem,) * 6,
        scratch_shapes=scratch,
        compiler_params=pltpu.CompilerParams(vmem_limit_bytes=62 * 1024 * 1024, **extra),
    )(
        state.reshape(C, LON, LAT),
        sea,
        taps.transpose(1, 2, 0),
        gain.reshape(1, C),
        cot.reshape(C, LON, LAT),
        win,
        wout.T,
        *spectral_constants(),
    )
    anywhere = pl.BlockSpec(memory_space=pl.ANY)
    return pl.pallas_call(
        deliver,
        out_shape=outs,
        in_specs=[anywhere] * 6,
        out_specs=(anywhere,) * 6,
        scratch_shapes=[pltpu.VMEM(out.shape, out.dtype) for out in outs]
        + [pltpu.SemaphoreType.DMA((2, 6))],
    )(*results)


def solution(mesh):
    n_lon, n_sample = mesh.shape["lon"], mesh.shape["sample"]
    factor = 1.0 / math.sqrt(n_sample * n_lon * LON * LAT)

    def on_device(state, cot, sea, taps, gain, win, wout):
        out = block(n_lon, n_sample, factor, state, cot, sea, taps, gain, win, wout)
        shape = state.shape
        return (
            out[0].reshape(shape),
            out[1].reshape(shape),
            out[2],
            out[3].T,
            out[4].transpose(2, 0, 1),
            out[5].reshape(OWN),
        )

    slab = P("sample", None, "lon", None)
    return jax.shard_map(
        on_device,
        mesh=mesh,
        in_specs=(slab, slab, P("lon", None), P(), P(), P(), P()),
        out_specs=(
            slab,
            slab,
            P("sample", None),
            P(None, "sample"),
            P("sample", None, None),
            P("sample"),
        ),
        check_vma=False,
    )
```

```python
import functools
import math

import jax
import jax.numpy as jnp
import numpy as np
from jax import lax
from jax.experimental import pallas as pl
from jax.experimental.pallas import tpu as pltpu
from jax.sharding import PartitionSpec as P

C = 192
HID = 768
LON = 16
LAT = 128
PERIOD = 131
SPEC = 256
TAPS = 7
HALO = 3
GROUP = 4
HID_BLOCK = 256
CUTS = 4
CELL_BLOCK = 256
TILE = 16
OWN = 12
PACKED = 1152
BF = jnp.bfloat16
F32 = jnp.float32
MESH = pl.DeviceIdType.MESH


def tree_sum(terms):
    while len(terms) > 1:
        paired = [terms[k] + terms[k + 1] for k in range(0, len(terms) - 1, 2)]
        if len(terms) % 2:
            paired.append(terms[-1])
        terms = paired
    return terms[0]


def matmul(left, right):
    return jnp.dot(left, right, preferred_element_type=F32)


def matmul_nt(left, right):
    return lax.dot_general(left, right, (((1,), (1,)), ((), ())), preferred_element_type=F32)


def split_constant(values):
    high = values.astype(BF)
    low = (values - high.astype(np.float64)).astype(BF)
    return high, low


def spectral_constants():
    angle = 2.0 * math.pi / PERIOD
    row = np.arange(LAT)
    field_f, field_b = np.zeros((LAT, SPEC)), np.zeros((LAT, SPEC))
    back_f, back_b = np.zeros((SPEC, LAT)), np.zeros((SPEC, LAT))
    taps = np.zeros((8, SPEC))
    shift = np.arange(TAPS) - HALO
    field_f[:, 0] = field_b[:, 0] = 1.0
    back_f[0] = back_b[0] = 1.0 / PERIOD
    taps[:TAPS, 0] = 1.0
    half = PERIOD // 2
    for f in range(1, half + 1):
        one, two, three = f, half + f, 2 * half + f
        cos, sin = np.cos(angle * f * row), np.sin(angle * f * row)
        c, d = np.cos(angle * f * shift), np.sin(angle * f * shift)
        taps[:TAPS, one], taps[:TAPS, two], taps[:TAPS, three] = c, d - c, c + d
        field_f[:, one], field_f[:, two], field_f[:, three] = cos - sin, cos, -sin
        field_b[:, one], field_b[:, two], field_b[:, three] = cos + sin, cos, sin
        scale = 2.0 / PERIOD
        back_f[one], back_f[two], back_f[three] = scale * (cos - sin), -scale * sin, -scale * cos
        back_b[one], back_b[two], back_b[three] = scale * (cos + sin), scale * sin, -scale * cos

    def stacked(values):
        return np.concatenate(split_constant(values), axis=0)

    def beside(values):
        return np.concatenate(split_constant(values), axis=1)

    spread_high, spread_low = np.zeros((64, TAPS * SPEC)), np.zeros((64, TAPS * SPEC))
    high, low = split_constant(taps)
    for a in range(TAPS):
        spread_high[8 * a : 8 * a + 8, a * SPEC : (a + 1) * SPEC] = high
        spread_low[8 * a : 8 * a + 8, a * SPEC : (a + 1) * SPEC] = low
    spread = np.concatenate([spread_high, spread_high, spread_low]).astype(BF)
    gather = np.zeros((SPEC, LAT))
    gather[:, :8] = taps.T
    return (
        spread,
        stacked(field_f),
        beside(back_f),
        np.concatenate([stacked(back_f.T), stacked(field_b)], axis=1),
        beside(back_b),
        beside(gather),
    )


def column(ref, at):
    return ref[pl.ds(at, C, stride=LON), :]


def kernel_body(
    n_lon,
    n_sample,
    factor,
    state_ref,
    sea_ref,
    taps_ref,
    gain_ref,
    cot_far,
    win_far,
    wout_far,
    spread_far,
    field_f_far,
    back_f_far,
    field_g_far,
    back_b_far,
    gather_far,
    sout_ref,
    gin_ref,
    gwin_ref,
    gwout_ref,
    gk_ref,
    gg_ref,
    cot_ref,
    win_ref,
    wout_t,
    spread,
    field_f,
    back_f,
    field_g,
    back_b,
    gather,
    x32,
    c32,
    xa,
    ga,
    xh,
    gh,
    gw,
    kf,
    dkf,
    flat_taps,
    sum_high,
    sum_low,
    gainb,
    win_t,
    wout,
    norm_all,
    cot_all,
    hid_all,
    gp_all,
    scaled_all,
    inv_all,
    acc_in,
    acc_out,
    acc_gain,
    dks,
    stage,
    wsend,
    wcore,
    wmid,
    wparts,
    wslab,
    vsend,
    vcore,
    vmid,
    vparts,
    vslab,
    sout_buf,
    gin_buf,
    ksend,
    kparts,
    kslab,
    kout,
    send,
    recv,
    near,
):
    fetches = [
        pltpu.make_async_copy(far, here, near.at[k])
        for k, (far, here) in enumerate(
            (
                (spread_far, spread),
                (field_f_far, field_f),
                (back_f_far, back_f),
                (win_far, win_ref),
                (wout_far, wout_t),
                (cot_far, cot_ref),
                (field_g_far, field_g),
                (back_b_far, back_b),
                (gather_far, gather),
            )
        )
    ]
    remote = n_lon > 1
    if remote:
        lon = lax.axis_index("lon")
        sample = lax.axis_index("sample")
        core = lax.rem(sample, 2)
        owner = sample // 2
        n_own = n_sample // 2
        partner = {"sample": sample + 1 - 2 * core}
        right = {"lon": lax.rem(lon + 1, n_lon)}
        left = {"lon": lax.rem(lon + n_lon - 1, n_lon)}
        owners = [lax.rem(owner + d, n_own) for d in range(1, n_own)]
        slabs = [lax.rem(lon + d, n_lon) for d in range(1, n_lon)]
        samples = [lax.rem(sample + d, n_sample) for d in range(1, n_sample)]
        peers = (
            [partner]
            + [{"sample": 2 * other + core} for other in owners]
            + [{"sample": 2 * other + 1 - core} for other in owners]
            + [{"lon": other} for other in slabs]
        )
        barrier = pltpu.get_barrier_semaphore()
        for peer in peers:
            pl.semaphore_signal(barrier, inc=1, device_id=peer, device_id_type=MESH)

        def copy(src, dst, slot, peer):
            return pltpu.make_async_remote_copy(
                src_ref=src,
                dst_ref=dst,
                send_sem=send.at[slot],
                recv_sem=recv.at[slot],
                device_id=peer,
                device_id_type=MESH,
            )

    def halo_copies(ref, slot):
        return (
            copy(ref.at[pl.ds(LON, HALO)], ref.at[pl.ds(0, HALO)], slot, right),
            copy(ref.at[pl.ds(HALO, HALO)], ref.at[pl.ds(LON + HALO, HALO)], slot + 1, left),
        )

    def local_halo(ref):
        ref[0:HALO] = ref[LON : LON + HALO]
        ref[LON + HALO : LON + 2 * HALO] = ref[HALO : 2 * HALO]

    x32[...] = state_ref[...].astype(F32).reshape(C * LON, LAT)
    for i in (0, 1, 2, 13, 14, 15):
        xa[HALO + i] = column(x32, i).astype(BF)
    if remote:
        pl.semaphore_wait(barrier, len(peers))
        x_right, x_left = halo_copies(xa, 0)
        x_left.start()
        x_right.start()
    for fetch in fetches:
        fetch.start()
    for i in range(3, 13):
        xa[HALO + i] = column(x32, i).astype(BF)
    for fetch in fetches:
        fetch.wait()
    c32[...] = cot_ref[...].astype(F32).reshape(C * LON, LAT)

    flat_taps[...] = jnp.zeros_like(flat_taps)
    for a in range(TAPS):
        flat_taps[8 * a : 8 * a + TAPS, 0:C] = taps_ref[a]
    rest = flat_taps[...].T[0:C, :]
    high = rest.astype(BF)
    low = (rest - high.astype(F32)).astype(BF)
    kf[...] = matmul(
        jnp.concatenate([high[:, 0:64], low[:, 0:64], high[:, 0:64]], axis=1), spread[...]
    )
    gainb[...] = jnp.broadcast_to(gain_ref[...], (LAT, C)).T
    win_t[...] = (0.5 * win_ref[...].astype(F32)).astype(BF).T
    wout[...] = (0.5 * wout_t[...].astype(F32)).astype(BF).T
    acc_gain[...] = jnp.zeros_like(acc_gain)

    def doubled(columns):
        flat = columns.reshape(-1, LAT)
        return jnp.concatenate([flat, flat], axis=1)

    def field_spectrum(at, count):
        spectrum = matmul(doubled(xa[at : at + count]), field_f[...])
        xh[at : at + count] = spectrum.reshape(count, C, SPEC)

    def grad_spectrum(at, count):
        spectrum = matmul(doubled(ga[at : at + count]), field_g[:, SPEC:])
        gh[at : at + count] = spectrum.reshape(count, C, SPEC)

    def filtered(field, col, flip, inverse):
        def one_tile(tile, carry):
            at = pl.multiple_of(tile * TILE, TILE)
            for half in range(0, SPEC, LAT):
                window = field[pl.ds(col, GROUP + 2 * HALO), pl.ds(at, TILE), half : half + LAT]
                terms = []
                for a in range(TAPS):
                    first = 2 * HALO - a if flip else a
                    lane = a * SPEC + half
                    weight = kf[pl.ds(at, TILE), lane : lane + LAT]
                    terms.append(weight[None] * window[first : first + GROUP])
                total = tree_sum(terms)
                high = total.astype(BF)
                sum_high[:, pl.ds(at, TILE), half : half + LAT] = high
                sum_low[:, pl.ds(at, TILE), half : half + LAT] = (
                    total - high.astype(F32)
                ).astype(BF)
            return carry

        lax.fori_loop(0, C // TILE, one_tile, 0, unroll=2)
        main = matmul(sum_high[...].reshape(GROUP * C, SPEC), inverse[...])
        rest = matmul(sum_low[...].reshape(GROUP * C, SPEC), inverse[:, 0:LAT])
        return (main[:, 0:LAT] + main[:, LAT:] + rest).reshape(GROUP, C, LAT)

    def masks(col):
        return [sea_ref[pl.ds(col + k, 1), :].astype(F32) for k in range(GROUP)]

    def side_by_side(parts):
        return jnp.concatenate([parts[k] for k in range(GROUP)], axis=1)

    def lanes_of(col):
        return pl.ds(pl.multiple_of(col * LAT, GROUP * LAT), GROUP * LAT)

    def forward_group(col):
        mixed = filtered(xh, col, False, back_f)
        centred = mixed - jnp.mean(mixed, axis=1, keepdims=True)
        variance = jnp.mean(centred * centred, axis=1, keepdims=True)
        inv_scale = lax.rsqrt(variance + 1e-06)
        scaled = centred * inv_scale
        scaled_all[pl.ds(col, GROUP)] = scaled
        inv_all[pl.ds(col, GROUP), :] = inv_scale.reshape(GROUP, LAT)
        normed = side_by_side((scaled * gainb[...][None]).astype(BF))
        mask = masks(col)
        grad_out = side_by_side([(column(c32, col + k) * mask[k]).astype(BF) for k in range(GROUP)])
        where = lanes_of(col)
        norm_all[:, where] = normed
        cot_all[:, where] = grad_out
        for h in range(0, HID, HID_BLOCK):
            for n in range(0, GROUP * LAT, CELL_BLOCK):
                half = matmul(win_t[h : h + HID_BLOCK, :], normed[:, n : n + CELL_BLOCK])
                grad_half = matmul(wout[h : h + HID_BLOCK, :], grad_out[:, n : n + CELL_BLOCK])
                square = half * half
                bent = jnp.tanh(half * (1.5957691216057308 + 0.28541926509040104 * square))
                gate = 1.0 + bent
                hidden = half * gate
                slope = gate + hidden * (1.0 - bent) * (
                    1.5957691216057308 + 0.8562577952712031 * square
                )
                at = pl.ds(pl.multiple_of(col * LAT + n, CELL_BLOCK), CELL_BLOCK)
                hid_all[h : h + HID_BLOCK, at] = hidden.astype(BF)
                gp_all[h : h + HID_BLOCK, at] = (grad_half * slope).astype(BF)

    def finish_state(col):
        mask = masks(col)
        branch = matmul(wout_t[...], hid_all[:, lanes_of(col)])
        for k in range(GROUP):
            lane = slice(k * LAT, (k + 1) * LAT)
            at = pl.ds(col + k, C, stride=LON)
            x32[at, :] = mask[k] * (x32[at, :] + branch[:, lane])

    def backward_mlp(col):
        where = lanes_of(col)
        gain = gainb[...]
        grad_normed = matmul(win_ref[...], gp_all[:, where])
        for k in range(GROUP):
            lane = slice(k * LAT, (k + 1) * LAT)
            scaled = scaled_all[col + k]
            grad = grad_normed[:, lane]
            product = grad * scaled
            acc_gain[...] += product
            grad_scaled = grad * gain
            first = jnp.mean(grad_scaled, axis=0, keepdims=True)
            second = jnp.mean(product * gain, axis=0, keepdims=True)
            inv_scale = inv_all[pl.ds(col + k, 1), :]
            grad_conv = (inv_scale * (grad_scaled - first - scaled * second)).astype(BF)
            ga[HALO + col + k] = grad_conv
            spectrum = matmul(doubled(grad_conv), field_g[...])
            gw[col + k] = spectrum[:, 0:SPEC]
            gh[HALO + col + k] = spectrum[:, SPEC:]

    def in_groups(first, last, work):
        def one_group(step, carry):
            work(lax.rem(GROUP + step * GROUP, LON))
            return carry

        lax.fori_loop(first, last, one_group, 0)

    def start(copies):
        for one in copies:
            one.start()

    def wait(copies):
        for one in copies:
            one.wait()

    for at in range(HALO, LON + HALO, GROUP):
        field_spectrum(at, GROUP)
    def filter_grads(parts, fresh):
        def one_tile(tile, carry):
            at = pl.multiple_of(tile * 8, 8)
            for half in range(0, SPEC, LAT):
                lanes = slice(half, half + LAT)
                for a in range(TAPS):
                    spot = slice(a * SPEC + half, a * SPEC + half + LAT)
                    total = 0.0 if fresh else dkf[pl.ds(at, 8), spot]
                    for col, count in parts:
                        grads = gw[col : col + count, pl.ds(at, 8), lanes]
                        field = xh[col + a : col + a + count, pl.ds(at, 8), lanes]
                        total = total + jnp.sum(grads * field, axis=0)
                    dkf[pl.ds(at, 8), spot] = total
            return carry

        lax.fori_loop(0, C // 8, one_tile, 0, unroll=2)

    in_groups(0, 2, forward_group)
    in_groups(0, 2, backward_mlp)
    filter_grads([(GROUP, 2 * GROUP)], True)
    cells = slice(GROUP * LAT, 3 * GROUP * LAT)
    acc_out[...] = matmul_nt(cot_all[:, cells], hid_all[:, cells])
    acc_in[...] = matmul_nt(norm_all[:, cells], gp_all[:, cells])
    if remote:
        g_right, g_left = halo_copies(ga, 2)
        x_left.wait()
    else:
        local_halo(xa)
    field_spectrum(LON + HALO, HALO)
    forward_group(LON - GROUP)
    backward_mlp(LON - GROUP)
    if remote:
        g_right.start()
        x_right.wait()
    field_spectrum(0, HALO)
    forward_group(0)
    backward_mlp(0)
    if remote:
        g_left.start()

    for cells in (slice(0, GROUP * LAT), slice(3 * GROUP * LAT, LON * LAT)):
        acc_out[...] += matmul_nt(cot_all[:, cells], hid_all[:, cells])
        acc_in[...] += matmul_nt(norm_all[:, cells], gp_all[:, cells])
    wide = HID // 2
    for o in range(16):
        at = OWN * o
        stage[o, 0:12, 0:HID] = acc_in[at : at + 12, :]
        stage[o, 12:16, 0:HID] = acc_out[at : at + 4, :]
        stage[o, 0:8, HID:PACKED] = acc_out[at + 4 : at + 12, 0:wide]
        stage[o, 8:16, HID:PACKED] = acc_out[at + 4 : at + 12, wide:HID]
    for o in range(16):
        wsend[o % 2, o // 2] = stage[o, :, 0:HID].astype(BF)
        vsend[o % 2, o // 2] = stage[o, :, HID:PACKED].astype(BF)

    if remote:

        def to_slabs(slab, base):
            return [
                copy(slab.at[lon], slab.at[lon], base + d, {"lon": other})
                for d, other in enumerate(slabs)
            ]

        def to_core(packed, from_core, base):
            return [copy(packed.at[1 - core], from_core, base, partner)]

        def to_owners(source, target, base):
            return [
                copy(source.at[other], target.at[d], base + d, {"sample": 2 * other + core})
                for d, other in enumerate(owners)
            ]

        def k_own():
            return [
                copy(ksend.at[other], kparts.at[d], 34 + d, {"sample": other})
                for d, other in enumerate(samples)
            ]

        def k_all():
            return to_slabs(kslab, 49)

        halves = ((wsend, wcore, wmid, wparts, wslab, 4), (vsend, vcore, vmid, vparts, vslab, 19))
        for packed, from_core, _, _, _, base in halves:
            start(to_core(packed, from_core, base))
    filter_grads([(0, GROUP), (3 * GROUP, GROUP)], False)
    if remote:
        for packed, from_core, middle, parts, _, base in halves:
            wait(to_core(packed, from_core, base))
            middle[...] = (packed[core].astype(F32) + from_core[...].astype(F32)).astype(BF)
            start(to_owners(middle, parts, base + 1))

    lanes = lax.broadcasted_iota(jnp.int32, (C, LAT), 1)
    total = jnp.where(lanes == TAPS * TAPS, jnp.sum(acc_gain[...], axis=1, keepdims=True), 0.0)
    for a in range(TAPS):
        part = dkf[:, a * SPEC : (a + 1) * SPEC]
        high = part.astype(BF)
        low = (part - high.astype(F32)).astype(BF)
        both = matmul(high, gather[...])
        found = both[:, 0:LAT] + both[:, LAT:] + matmul(low, gather[:, 0:LAT])
        total = total + (pltpu.roll(found, a * TAPS, axis=1) if a else found)
    dks[0, 0:C, :] = total
    dks[1, 0:C, :] = pltpu.roll(total, LAT // 2, axis=1)
    for side in range(2):
        dks[side, C : C + 16, :] = jnp.zeros((16, LAT), F32)
    for o in range(16):
        at = OWN * o
        ksend[o] = dks[0, at : at + 8, :] + dks[1, at + 6 : at + 14, :]
    if remote:
        start(k_own())
    in_groups(0, 4, finish_state)

    def backward_group(col):
        moved = filtered(gh, col, True, back_b)
        mask = masks(col)
        for k in range(GROUP):
            at = pl.ds(col + k, C, stride=LON)
            c32[at, :] = c32[at, :] * mask[k] + moved[k]

    in_groups(0, 2, backward_group)
    if remote:
        g_right.wait()
    else:
        local_halo(ga)
    grad_spectrum(0, HALO)
    backward_group(0)
    sout_buf[...] = x32[...].reshape(C, LON, LAT).astype(BF)
    leave = [
        pltpu.make_async_copy(sout_buf, sout_ref, near.at[9]),
        pltpu.make_async_copy(gin_buf, gin_ref, near.at[10]),
    ]
    leave[0].start()
    if remote:
        g_left.wait()
    grad_spectrum(LON + HALO, HALO)
    backward_group(LON - GROUP)
    if remote:
        wait(k_own())
        held = ksend[sample]
        for d in range(len(samples)):
            held = held + kparts[d]
        kslab[lon] = held
        start(k_all())
    gin_buf[...] = c32[...].reshape(C, LON, LAT).astype(BF)
    leave[1].start()
    if remote:
        for _, _, middle, parts, slab, base in halves:
            wait(to_owners(middle, parts, base + 1))
            held = middle[owner].astype(F32)
            for d in range(len(owners)):
                held = held + parts[d].astype(F32)
            slab[lon] = held.astype(BF)
            start(to_slabs(slab, base + 8))
        wait(k_all())
        small = kslab[0]
        for other in range(1, n_lon):
            small = small + kslab[other]
        sums = []
        for _, _, _, _, slab, base in halves:
            wait(to_slabs(slab, base + 8))
            held = slab[0].astype(F32)
            for other in range(1, n_lon):
                held = held + slab[other].astype(F32)
            sums.append(held)
        weights = jnp.concatenate(sums, axis=1)
    else:
        weights = jnp.concatenate([wsend[0, 0], vsend[0, 0]], axis=1).astype(F32)
        small = ksend[0]
    weights = weights * factor
    small = small * factor
    gwin_ref[...] = weights[0:12, 0:HID]
    gwout_ref[0:4, :] = weights[12:16, 0:HID]
    gwout_ref[4:12, 0:wide] = weights[0:8, HID:PACKED]
    gwout_ref[4:12, wide:HID] = weights[8:16, HID:PACKED]
    kout[0:6, :] = small[0:6, :]
    kout[6:12, :] = pltpu.roll(small, LAT // 2, axis=1)[0:6, :]
    small_t = kout[...].T
    for a in range(TAPS):
        gk_ref[a] = small_t[a * TAPS : (a + 1) * TAPS, 0:OWN]
    gg_ref[...] = small_t[TAPS * TAPS : TAPS * TAPS + 1, 0:OWN]
    for one in leave:
        one.wait()


def deliver(*refs):
    count = len(refs) // 3
    sems = refs[-1]
    arrive, leave = [], []
    for k in range(count):
        source, target, held = refs[k], refs[count + k], refs[2 * count + k]
        pieces = CUTS if k < 2 else 1
        length = source.shape[0] // pieces
        for p in range(pieces):
            part = pl.ds(p * length, length)
            at = len(arrive)
            arrive.append(pltpu.make_async_copy(source.at[part], held.at[part], sems.at[0, at]))
            leave.append(pltpu.make_async_copy(held.at[part], target.at[part], sems.at[1, at]))
    for one in arrive:
        one.start()
    for one, other in zip(arrive, leave):
        one.wait()
        other.start()
    for one in leave:
        one.wait()


def block(n_lon, n_sample, factor, state, cot, sea, taps, gain, win, wout):
    vmem = pl.BlockSpec(memory_space=pltpu.VMEM)
    far = pl.BlockSpec(memory_space=pltpu.HBM)
    shape = jax.ShapeDtypeStruct
    outs = (
        shape((C, LON, LAT), BF),
        shape((C, LON, LAT), BF),
        shape((OWN, HID), F32),
        shape((OWN, HID), F32),
        shape((TAPS, TAPS, OWN), F32),
        shape((1, OWN), F32),
    )
    scratch = [
        pltpu.VMEM((C, LON, LAT), BF),
        pltpu.VMEM((C, HID), BF),
        pltpu.VMEM((C, HID), BF),
        pltpu.VMEM((3 * 64, TAPS * SPEC), BF),
        pltpu.VMEM((2 * LAT, SPEC), BF),
        pltpu.VMEM((SPEC, 2 * LAT), BF),
        pltpu.VMEM((2 * LAT, 2 * SPEC), BF),
        pltpu.VMEM((SPEC, 2 * LAT), BF),
        pltpu.VMEM((SPEC, 2 * LAT), BF),
        pltpu.VMEM((C * LON, LAT), F32),
        pltpu.VMEM((C * LON, LAT), F32),
        pltpu.VMEM((LON + 2 * HALO, C, LAT), BF),
        pltpu.VMEM((LON + 2 * HALO, C, LAT), BF),
        pltpu.VMEM((LON + 2 * HALO, C, SPEC), F32),
        pltpu.VMEM((LON + 2 * HALO, C, SPEC), F32),
        pltpu.VMEM((LON, C, SPEC), F32),
        pltpu.VMEM((C, TAPS * SPEC), F32),
        pltpu.VMEM((C, TAPS * SPEC), F32),
        pltpu.VMEM((LAT, 2 * LAT), F32),
        pltpu.VMEM((GROUP, C, SPEC), BF),
        pltpu.VMEM((GROUP, C, SPEC), BF),
        pltpu.VMEM((C, LAT), F32),
        pltpu.VMEM((HID, C), BF),
        pltpu.VMEM((HID, C), BF),
        pltpu.VMEM((C, LON * LAT), BF),
        pltpu.VMEM((C, LON * LAT), BF),
        pltpu.VMEM((HID, LON * LAT), BF),
        pltpu.VMEM((HID, LON * LAT), BF),
        pltpu.VMEM((LON, C, LAT), F32),
        pltpu.VMEM((LON, LAT), F32),
        pltpu.VMEM((C, HID), F32),
        pltpu.VMEM((C, HID), F32),
        pltpu.VMEM((C, LAT), F32),
        pltpu.VMEM((2, C + 16, LAT), F32),
        pltpu.VMEM((16, 16, PACKED), F32),
        pltpu.VMEM((2, 8, 16, HID), BF),
        pltpu.VMEM((8, 16, HID), BF),
        pltpu.VMEM((8, 16, HID), BF),
        pltpu.VMEM((7, 16, HID), BF),
        pltpu.VMEM((8, 16, HID), BF),
        pltpu.VMEM((2, 8, 16, HID // 2), BF),
        pltpu.VMEM((8, 16, HID // 2), BF),
        pltpu.VMEM((8, 16, HID // 2), BF),
        pltpu.VMEM((7, 16, HID // 2), BF),
        pltpu.VMEM((8, 16, HID // 2), BF),
        pltpu.VMEM((C, LON, LAT), BF),
        pltpu.VMEM((C, LON, LAT), BF),
        pltpu.VMEM((16, 8, LAT), F32),
        pltpu.VMEM((15, 8, LAT), F32),
        pltpu.VMEM((8, 8, LAT), F32),
        pltpu.VMEM((16, LAT), F32),
        pltpu.SemaphoreType.DMA((56,)),
        pltpu.SemaphoreType.DMA((56,)),
        pltpu.SemaphoreType.DMA((11,)),
    ]
    extra = dict(collective_id=0, has_side_effects=True) if n_lon > 1 else {}
    results = pl.pallas_call(
        functools.partial(kernel_body, n_lon, n_sample, factor),
        out_shape=outs,
        in_specs=[vmem] * 4 + [far] * 9,
        out_specs=(far, far) + (vmem,) * 4,
        scratch_shapes=scratch,
        compiler_params=pltpu.CompilerParams(vmem_limit_bytes=62 * 1024 * 1024, **extra),
    )(
        state.reshape(C, LON, LAT),
        sea,
        taps.transpose(1, 2, 0),
        gain.reshape(1, C),
        cot.reshape(C, LON, LAT),
        win,
        wout.T,
        *spectral_constants(),
    )
    anywhere = pl.BlockSpec(memory_space=pl.ANY)
    return pl.pallas_call(
        deliver,
        out_shape=outs,
        in_specs=[anywhere] * 6,
        out_specs=(anywhere,) * 6,
        scratch_shapes=[pltpu.VMEM(out.shape, out.dtype) for out in outs]
        + [pltpu.SemaphoreType.DMA((2, 2 * CUTS + 4))],
    )(*results)


def solution(mesh):
    n_lon, n_sample = mesh.shape["lon"], mesh.shape["sample"]
    factor = 1.0 / math.sqrt(n_sample * n_lon * LON * LAT)

    def on_device(state, cot, sea, taps, gain, win, wout):
        out = block(n_lon, n_sample, factor, state, cot, sea, taps, gain, win, wout)
        shape = state.shape
        return (
            out[0].reshape(shape),
            out[1].reshape(shape),
            out[2],
            out[3].T,
            out[4].transpose(2, 0, 1),
            out[5].reshape(OWN),
        )

    slab = P("sample", None, "lon", None)
    return jax.shard_map(
        on_device,
        mesh=mesh,
        in_specs=(slab, slab, P("lon", None), P(), P(), P(), P()),
        out_specs=(
            slab,
            slab,
            P("sample", None),
            P(None, "sample"),
            P("sample", None, None),
            P("sample"),
        ),
        check_vma=False,
    )
```

```python
import functools
import math

import jax
import jax.numpy as jnp
import numpy as np
from jax import lax
from jax.experimental import pallas as pl
from jax.experimental.pallas import tpu as pltpu
from jax.sharding import PartitionSpec as P

C = 192
HID = 768
LON = 16
LAT = 128
PERIOD = 131
SPEC = 256
TAPS = 7
HALO = 3
GROUP = 4
HID_BLOCK = 256
CELL_BLOCK = 256
TILE = 16
OWN = 12
PACKED = 1152
BF = jnp.bfloat16
F32 = jnp.float32
MESH = pl.DeviceIdType.MESH


def tree_sum(terms):
    while len(terms) > 1:
        paired = [terms[k] + terms[k + 1] for k in range(0, len(terms) - 1, 2)]
        if len(terms) % 2:
            paired.append(terms[-1])
        terms = paired
    return terms[0]


def matmul(left, right):
    return jnp.dot(left, right, preferred_element_type=F32)


def matmul_nt(left, right):
    return lax.dot_general(left, right, (((1,), (1,)), ((), ())), preferred_element_type=F32)


def split_constant(values):
    high = values.astype(BF)
    low = (values - high.astype(np.float64)).astype(BF)
    return high, low


def spectral_constants():
    angle = 2.0 * math.pi / PERIOD
    row = np.arange(LAT)
    field_f, field_b = np.zeros((LAT, SPEC)), np.zeros((LAT, SPEC))
    back_f, back_b = np.zeros((SPEC, LAT)), np.zeros((SPEC, LAT))
    taps = np.zeros((8, SPEC))
    shift = np.arange(TAPS) - HALO
    field_f[:, 0] = field_b[:, 0] = 1.0
    back_f[0] = back_b[0] = 1.0 / PERIOD
    taps[:TAPS, 0] = 1.0
    half = PERIOD // 2
    for f in range(1, half + 1):
        one, two, three = f, half + f, 2 * half + f
        cos, sin = np.cos(angle * f * row), np.sin(angle * f * row)
        c, d = np.cos(angle * f * shift), np.sin(angle * f * shift)
        taps[:TAPS, one], taps[:TAPS, two], taps[:TAPS, three] = c, d - c, c + d
        field_f[:, one], field_f[:, two], field_f[:, three] = cos - sin, cos, -sin
        field_b[:, one], field_b[:, two], field_b[:, three] = cos + sin, cos, sin
        scale = 2.0 / PERIOD
        back_f[one], back_f[two], back_f[three] = scale * (cos - sin), -scale * sin, -scale * cos
        back_b[one], back_b[two], back_b[three] = scale * (cos + sin), scale * sin, -scale * cos

    def stacked(values):
        return np.concatenate(split_constant(values), axis=0)

    def beside(values):
        return np.concatenate(split_constant(values), axis=1)

    spread_high, spread_low = np.zeros((64, TAPS * SPEC)), np.zeros((64, TAPS * SPEC))
    high, low = split_constant(taps)
    for a in range(TAPS):
        spread_high[8 * a : 8 * a + 8, a * SPEC : (a + 1) * SPEC] = high
        spread_low[8 * a : 8 * a + 8, a * SPEC : (a + 1) * SPEC] = low
    spread = np.concatenate([spread_high, spread_high, spread_low]).astype(BF)
    gather = np.zeros((SPEC, LAT))
    gather[:, :8] = taps.T
    return (
        spread,
        stacked(field_f),
        beside(back_f),
        np.concatenate([stacked(back_f.T), stacked(field_b)], axis=1),
        beside(back_b),
        beside(gather),
    )


def column(ref, at):
    return ref[pl.ds(at, C, stride=LON), :]


def kernel_body(
    n_lon,
    n_sample,
    factor,
    state_ref,
    sea_ref,
    taps_ref,
    gain_ref,
    cot_far,
    win_far,
    wout_far,
    spread_far,
    field_f_far,
    back_f_far,
    field_g_far,
    back_b_far,
    gather_far,
    sout_ref,
    gin_ref,
    gwin_ref,
    gwout_ref,
    gk_ref,
    gg_ref,
    cot_ref,
    win_ref,
    wout_t,
    spread,
    field_f,
    back_f,
    field_g,
    back_b,
    gather,
    x32,
    c32,
    xa,
    ga,
    xh,
    gh,
    gw,
    kf,
    dkf,
    flat_taps,
    sum_high,
    sum_low,
    gainb,
    win_t,
    wout,
    norm_all,
    cot_all,
    hid_all,
    gp_all,
    scaled_all,
    inv_all,
    acc_in,
    acc_out,
    acc_gain,
    dks,
    stage,
    wsend,
    wcore,
    wmid,
    wparts,
    wslab,
    ksend,
    kcore,
    kmid,
    kparts,
    kslab,
    kout,
    sout_buf,
    gin_buf,
    send,
    recv,
    near,
):
    fetches = [
        pltpu.make_async_copy(far, here, near.at[k])
        for k, (far, here) in enumerate(
            (
                (spread_far, spread),
                (field_f_far, field_f),
                (back_f_far, back_f),
                (win_far, win_ref),
                (wout_far, wout_t),
                (cot_far, cot_ref),
                (field_g_far, field_g),
                (back_b_far, back_b),
                (gather_far, gather),
            )
        )
    ]
    for fetch in fetches:
        fetch.start()
    remote = n_lon > 1
    if remote:
        lon = lax.axis_index("lon")
        sample = lax.axis_index("sample")
        core = lax.rem(sample, 2)
        owner = sample // 2
        n_own = n_sample // 2
        partner = {"sample": sample + 1 - 2 * core}
        right = {"lon": lax.rem(lon + 1, n_lon)}
        left = {"lon": lax.rem(lon + n_lon - 1, n_lon)}
        owners = [lax.rem(owner + d, n_own) for d in range(1, n_own)]
        slabs = [lax.rem(lon + d, n_lon) for d in range(1, n_lon)]
        peers = (
            [partner]
            + [{"sample": 2 * other + core} for other in owners]
            + [{"lon": other} for other in slabs]
        )
        barrier = pltpu.get_barrier_semaphore()
        for peer in peers:
            pl.semaphore_signal(barrier, inc=1, device_id=peer, device_id_type=MESH)

        def copy(src, dst, slot, peer):
            return pltpu.make_async_remote_copy(
                src_ref=src,
                dst_ref=dst,
                send_sem=send.at[slot],
                recv_sem=recv.at[slot],
                device_id=peer,
                device_id_type=MESH,
            )

    def halo_copies(ref, slot):
        return (
            copy(ref.at[pl.ds(LON, HALO)], ref.at[pl.ds(0, HALO)], slot, right),
            copy(ref.at[pl.ds(HALO, HALO)], ref.at[pl.ds(LON + HALO, HALO)], slot + 1, left),
        )

    def local_halo(ref):
        ref[0:HALO] = ref[LON : LON + HALO]
        ref[LON + HALO : LON + 2 * HALO] = ref[HALO : 2 * HALO]

    x32[...] = state_ref[...].astype(F32).reshape(C * LON, LAT)
    for i in (0, 1, 2, 13, 14, 15):
        xa[HALO + i] = column(x32, i).astype(BF)
    if remote:
        pl.semaphore_wait(barrier, len(peers))
        x_right, x_left = halo_copies(xa, 0)
        x_left.start()
        x_right.start()
    for i in range(3, 13):
        xa[HALO + i] = column(x32, i).astype(BF)
    for fetch in fetches:
        fetch.wait()
    c32[...] = cot_ref[...].astype(F32).reshape(C * LON, LAT)

    flat_taps[...] = jnp.zeros_like(flat_taps)
    for a in range(TAPS):
        flat_taps[8 * a : 8 * a + TAPS, 0:C] = taps_ref[a]
    rest = flat_taps[...].T[0:C, :]
    high = rest.astype(BF)
    low = (rest - high.astype(F32)).astype(BF)
    kf[...] = matmul(
        jnp.concatenate([high[:, 0:64], low[:, 0:64], high[:, 0:64]], axis=1), spread[...]
    )
    gainb[...] = jnp.broadcast_to(gain_ref[...], (LAT, C)).T
    win_t[...] = (0.5 * win_ref[...].astype(F32)).astype(BF).T
    wout[...] = (0.5 * wout_t[...].astype(F32)).astype(BF).T
    acc_gain[...] = jnp.zeros_like(acc_gain)

    def doubled(columns):
        flat = columns.reshape(-1, LAT)
        return jnp.concatenate([flat, flat], axis=1)

    def field_spectrum(at, count):
        spectrum = matmul(doubled(xa[at : at + count]), field_f[...])
        xh[at : at + count] = spectrum.reshape(count, C, SPEC)

    def grad_spectrum(at, count):
        spectrum = matmul(doubled(ga[at : at + count]), field_g[:, SPEC:])
        gh[at : at + count] = spectrum.reshape(count, C, SPEC)

    def filtered(field, col, flip, inverse):
        def one_tile(tile, carry):
            at = pl.multiple_of(tile * TILE, TILE)
            for half in range(0, SPEC, LAT):
                window = field[pl.ds(col, GROUP + 2 * HALO), pl.ds(at, TILE), half : half + LAT]
                terms = []
                for a in range(TAPS):
                    first = 2 * HALO - a if flip else a
                    lane = a * SPEC + half
                    weight = kf[pl.ds(at, TILE), lane : lane + LAT]
                    terms.append(weight[None] * window[first : first + GROUP])
                total = tree_sum(terms)
                high = total.astype(BF)
                sum_high[:, pl.ds(at, TILE), half : half + LAT] = high
                sum_low[:, pl.ds(at, TILE), half : half + LAT] = (
                    total - high.astype(F32)
                ).astype(BF)
            return carry

        lax.fori_loop(0, C // TILE, one_tile, 0, unroll=2)
        main = matmul(sum_high[...].reshape(GROUP * C, SPEC), inverse[...])
        rest = matmul(sum_low[...].reshape(GROUP * C, SPEC), inverse[:, 0:LAT])
        return (main[:, 0:LAT] + main[:, LAT:] + rest).reshape(GROUP, C, LAT)

    def masks(col):
        return [sea_ref[pl.ds(col + k, 1), :].astype(F32) for k in range(GROUP)]

    def side_by_side(parts):
        return jnp.concatenate([parts[k] for k in range(GROUP)], axis=1)

    def lanes_of(col):
        return pl.ds(pl.multiple_of(col * LAT, GROUP * LAT), GROUP * LAT)

    def forward_group(col):
        mixed = filtered(xh, col, False, back_f)
        centred = mixed - jnp.mean(mixed, axis=1, keepdims=True)
        variance = jnp.mean(centred * centred, axis=1, keepdims=True)
        inv_scale = lax.rsqrt(variance + 1e-06)
        scaled = centred * inv_scale
        scaled_all[pl.ds(col, GROUP)] = scaled
        inv_all[pl.ds(col, GROUP), :] = inv_scale.reshape(GROUP, LAT)
        normed = side_by_side((scaled * gainb[...][None]).astype(BF))
        mask = masks(col)
        grad_out = side_by_side([(column(c32, col + k) * mask[k]).astype(BF) for k in range(GROUP)])
        where = lanes_of(col)
        norm_all[:, where] = normed
        cot_all[:, where] = grad_out
        for h in range(0, HID, HID_BLOCK):
            for n in range(0, GROUP * LAT, CELL_BLOCK):
                half = matmul(win_t[h : h + HID_BLOCK, :], normed[:, n : n + CELL_BLOCK])
                grad_half = matmul(wout[h : h + HID_BLOCK, :], grad_out[:, n : n + CELL_BLOCK])
                square = half * half
                bent = jnp.tanh(half * (1.5957691216057308 + 0.28541926509040104 * square))
                gate = 1.0 + bent
                hidden = half * gate
                slope = gate + hidden * (1.0 - bent) * (
                    1.5957691216057308 + 0.8562577952712031 * square
                )
                at = pl.ds(pl.multiple_of(col * LAT + n, CELL_BLOCK), CELL_BLOCK)
                hid_all[h : h + HID_BLOCK, at] = hidden.astype(BF)
                gp_all[h : h + HID_BLOCK, at] = (grad_half * slope).astype(BF)

    def finish_state(col):
        mask = masks(col)
        branch = matmul(wout_t[...], hid_all[:, lanes_of(col)])
        for k in range(GROUP):
            lane = slice(k * LAT, (k + 1) * LAT)
            at = pl.ds(col + k, C, stride=LON)
            x32[at, :] = mask[k] * (x32[at, :] + branch[:, lane])

    def backward_mlp(col):
        where = lanes_of(col)
        gain = gainb[...]
        grad_normed = matmul(win_ref[...], gp_all[:, where])
        for k in range(GROUP):
            lane = slice(k * LAT, (k + 1) * LAT)
            scaled = scaled_all[col + k]
            grad = grad_normed[:, lane]
            product = grad * scaled
            acc_gain[...] += product
            grad_scaled = grad * gain
            first = jnp.mean(grad_scaled, axis=0, keepdims=True)
            second = jnp.mean(product * gain, axis=0, keepdims=True)
            inv_scale = inv_all[pl.ds(col + k, 1), :]
            grad_conv = (inv_scale * (grad_scaled - first - scaled * second)).astype(BF)
            ga[HALO + col + k] = grad_conv
            spectrum = matmul(doubled(grad_conv), field_g[...])
            gw[col + k] = spectrum[:, 0:SPEC]
            gh[HALO + col + k] = spectrum[:, SPEC:]

    def in_groups(first, last, work):
        def one_group(step, carry):
            work(lax.rem(GROUP + step * GROUP, LON))
            return carry

        lax.fori_loop(first, last, one_group, 0)

    def start(copies):
        for one in copies:
            one.start()

    def wait(copies):
        for one in copies:
            one.wait()

    for at in range(HALO, LON + HALO, GROUP):
        field_spectrum(at, GROUP)
    def filter_grads(first, last):
        def one_tile(tile, carry):
            at = pl.multiple_of(tile * 8, 8)
            for half in range(0, SPEC, LAT):
                totals = [None] * TAPS
                for col in range(0, LON, 8):
                    grads = gw[col : col + 8, pl.ds(at, 8), half : half + LAT]
                    for a in range(TAPS):
                        field = xh[col + a : col + a + 8, pl.ds(at, 8), half : half + LAT]
                        part = jnp.sum(grads * field, axis=0)
                        totals[a] = part if totals[a] is None else totals[a] + part
                for a in range(TAPS):
                    dkf[pl.ds(at, 8), a * SPEC + half : a * SPEC + half + LAT] = totals[a]
            return carry

        lax.fori_loop(first, last, one_tile, 0, unroll=2)

    in_groups(0, 2, forward_group)
    in_groups(0, 2, backward_mlp)
    cells = slice(GROUP * LAT, 3 * GROUP * LAT)
    acc_out[...] = matmul_nt(cot_all[:, cells], hid_all[:, cells])
    acc_in[...] = matmul_nt(norm_all[:, cells], gp_all[:, cells])
    if remote:
        g_right, g_left = halo_copies(ga, 2)
        x_left.wait()
    else:
        local_halo(xa)
    field_spectrum(LON + HALO, HALO)
    forward_group(LON - GROUP)
    backward_mlp(LON - GROUP)
    if remote:
        g_right.start()
        x_right.wait()
    field_spectrum(0, HALO)
    forward_group(0)
    backward_mlp(0)
    if remote:
        g_left.start()

    for cells in (slice(0, GROUP * LAT), slice(3 * GROUP * LAT, LON * LAT)):
        acc_out[...] += matmul_nt(cot_all[:, cells], hid_all[:, cells])
        acc_in[...] += matmul_nt(norm_all[:, cells], gp_all[:, cells])
    wide = HID // 2
    for o in range(16):
        at = OWN * o
        stage[o, 0:12, 0:HID] = acc_in[at : at + 12, :]
        stage[o, 12:16, 0:HID] = acc_out[at : at + 4, :]
        stage[o, 0:8, HID:PACKED] = acc_out[at + 4 : at + 12, 0:wide]
        stage[o, 8:16, HID:PACKED] = acc_out[at + 4 : at + 12, wide:HID]
    for o in range(16):
        wsend[o % 2, o // 2] = stage[o].astype(BF)

    if remote:

        def to_slabs(slab, base):
            return [
                copy(slab.at[lon], slab.at[lon], base + d, {"lon": other})
                for d, other in enumerate(slabs)
            ]

        def to_owners(source, target, base):
            return [
                copy(source.at[other], target.at[d], base + d, {"sample": 2 * other + core})
                for d, other in enumerate(owners)
            ]

        def w_core():
            return [copy(wsend.at[1 - core], wcore, 4, partner)]

        def w_own():
            return to_owners(wmid, wparts, 5)

        def w_all():
            return to_slabs(wslab, 12)

        def k_core():
            return [copy(ksend.at[1 - core], kcore, 19, partner)]

        def k_own():
            return to_owners(kmid, kparts, 20)

        def k_all():
            return to_slabs(kslab, 27)

        start(w_core())
    filter_grads(0, C // 16)
    if remote:
        wait(w_core())
        wmid[...] = (wsend[core].astype(F32) + wcore[...].astype(F32)).astype(BF)
        start(w_own())
    filter_grads(C // 16, C // 8)

    lanes = lax.broadcasted_iota(jnp.int32, (C, LAT), 1)
    total = jnp.where(lanes == TAPS * TAPS, jnp.sum(acc_gain[...], axis=1, keepdims=True), 0.0)
    for a in range(TAPS):
        part = dkf[:, a * SPEC : (a + 1) * SPEC]
        high = part.astype(BF)
        low = (part - high.astype(F32)).astype(BF)
        both = matmul(high, gather[...])
        found = both[:, 0:LAT] + both[:, LAT:] + matmul(low, gather[:, 0:LAT])
        total = total + (pltpu.roll(found, a * TAPS, axis=1) if a else found)
    dks[0, 0:C, :] = total
    dks[1, 0:C, :] = pltpu.roll(total, LAT // 2, axis=1)
    for side in range(2):
        dks[side, C : C + 16, :] = jnp.zeros((16, LAT), F32)
    for o in range(16):
        at = OWN * o
        ksend[o % 2, o // 2] = dks[0, at : at + 8, :] + dks[1, at + 6 : at + 14, :]
    if remote:
        start(k_core())
    in_groups(0, 4, finish_state)
    sout_buf[...] = x32[...].reshape(C, LON, LAT).astype(BF)
    leave = [
        pltpu.make_async_copy(sout_buf, sout_ref, near.at[9]),
        pltpu.make_async_copy(gin_buf, gin_ref, near.at[10]),
    ]
    leave[0].start()
    if remote:
        wait(k_core())
        kmid[...] = ksend[core] + kcore[...]
        start(k_own())

    def backward_group(col):
        moved = filtered(gh, col, True, back_b)
        mask = masks(col)
        for k in range(GROUP):
            at = pl.ds(col + k, C, stride=LON)
            c32[at, :] = c32[at, :] * mask[k] + moved[k]

    in_groups(0, 2, backward_group)
    if remote:
        g_right.wait()
    else:
        local_halo(ga)
    grad_spectrum(0, HALO)
    backward_group(0)
    if remote:
        wait(w_own())
        held = wmid[owner].astype(F32)
        for d in range(len(owners)):
            held = held + wparts[d].astype(F32)
        wslab[lon] = held.astype(BF)
        start(w_all())
        wait(k_own())
        held = kmid[owner]
        for d in range(len(owners)):
            held = held + kparts[d]
        kslab[lon] = held
        start(k_all())
        g_left.wait()
    grad_spectrum(LON + HALO, HALO)
    backward_group(LON - GROUP)
    gin_buf[...] = c32[...].reshape(C, LON, LAT).astype(BF)
    leave[1].start()
    if remote:
        wait(w_all())
        weights = wslab[0].astype(F32)
        for other in range(1, n_lon):
            weights = weights + wslab[other].astype(F32)
        wait(k_all())
        small = kslab[0]
        for other in range(1, n_lon):
            small = small + kslab[other]
    else:
        weights = wsend[0, 0].astype(F32)
        small = ksend[0, 0]
    weights = weights * factor
    small = small * factor
    gwin_ref[...] = weights[0:12, 0:HID]
    gwout_ref[0:4, :] = weights[12:16, 0:HID]
    gwout_ref[4:12, 0:wide] = weights[0:8, HID:PACKED]
    gwout_ref[4:12, wide:HID] = weights[8:16, HID:PACKED]
    kout[0:6, :] = small[0:6, :]
    kout[6:12, :] = pltpu.roll(small, LAT // 2, axis=1)[0:6, :]
    small_t = kout[...].T
    for a in range(TAPS):
        gk_ref[a] = small_t[a * TAPS : (a + 1) * TAPS, 0:OWN]
    gg_ref[...] = small_t[TAPS * TAPS : TAPS * TAPS + 1, 0:OWN]
    for one in leave:
        one.wait()


def deliver(*refs):
    count = len(refs) // 3
    sems = refs[-1]
    sources, targets, held = refs[:count], refs[count : 2 * count], refs[2 * count : 3 * count]
    arrive = [pltpu.make_async_copy(sources[k], held[k], sems.at[0, k]) for k in range(count)]
    leave = [pltpu.make_async_copy(held[k], targets[k], sems.at[1, k]) for k in range(count)]
    for one in arrive:
        one.start()
    for k in range(count):
        arrive[k].wait()
        leave[k].start()
    for one in leave:
        one.wait()


def block(n_lon, n_sample, factor, state, cot, sea, taps, gain, win, wout):
    vmem = pl.BlockSpec(memory_space=pltpu.VMEM)
    far = pl.BlockSpec(memory_space=pltpu.HBM)
    shape = jax.ShapeDtypeStruct
    outs = (
        shape((C, LON, LAT), BF),
        shape((C, LON, LAT), BF),
        shape((OWN, HID), F32),
        shape((OWN, HID), F32),
        shape((TAPS, TAPS, OWN), F32),
        shape((1, OWN), F32),
    )
    scratch = [
        pltpu.VMEM((C, LON, LAT), BF),
        pltpu.VMEM((C, HID), BF),
        pltpu.VMEM((C, HID), BF),
        pltpu.VMEM((3 * 64, TAPS * SPEC), BF),
        pltpu.VMEM((2 * LAT, SPEC), BF),
        pltpu.VMEM((SPEC, 2 * LAT), BF),
        pltpu.VMEM((2 * LAT, 2 * SPEC), BF),
        pltpu.VMEM((SPEC, 2 * LAT), BF),
        pltpu.VMEM((SPEC, 2 * LAT), BF),
        pltpu.VMEM((C * LON, LAT), F32),
        pltpu.VMEM((C * LON, LAT), F32),
        pltpu.VMEM((LON + 2 * HALO, C, LAT), BF),
        pltpu.VMEM((LON + 2 * HALO, C, LAT), BF),
        pltpu.VMEM((LON + 2 * HALO, C, SPEC), F32),
        pltpu.VMEM((LON + 2 * HALO, C, SPEC), F32),
        pltpu.VMEM((LON, C, SPEC), F32),
        pltpu.VMEM((C, TAPS * SPEC), F32),
        pltpu.VMEM((C, TAPS * SPEC), F32),
        pltpu.VMEM((LAT, 2 * LAT), F32),
        pltpu.VMEM((GROUP, C, SPEC), BF),
        pltpu.VMEM((GROUP, C, SPEC), BF),
        pltpu.VMEM((C, LAT), F32),
        pltpu.VMEM((HID, C), BF),
        pltpu.VMEM((HID, C), BF),
        pltpu.VMEM((C, LON * LAT), BF),
        pltpu.VMEM((C, LON * LAT), BF),
        pltpu.VMEM((HID, LON * LAT), BF),
        pltpu.VMEM((HID, LON * LAT), BF),
        pltpu.VMEM((LON, C, LAT), F32),
        pltpu.VMEM((LON, LAT), F32),
        pltpu.VMEM((C, HID), F32),
        pltpu.VMEM((C, HID), F32),
        pltpu.VMEM((C, LAT), F32),
        pltpu.VMEM((2, C + 16, LAT), F32),
        pltpu.VMEM((16, 16, PACKED), F32),
        pltpu.VMEM((2, 8, 16, PACKED), BF),
        pltpu.VMEM((8, 16, PACKED), BF),
        pltpu.VMEM((8, 16, PACKED), BF),
        pltpu.VMEM((7, 16, PACKED), BF),
        pltpu.VMEM((8, 16, PACKED), BF),
        pltpu.VMEM((2, 8, 8, LAT), F32),
        pltpu.VMEM((8, 8, LAT), F32),
        pltpu.VMEM((8, 8, LAT), F32),
        pltpu.VMEM((7, 8, LAT), F32),
        pltpu.VMEM((8, 8, LAT), F32),
        pltpu.VMEM((16, LAT), F32),
        pltpu.VMEM((C, LON, LAT), BF),
        pltpu.VMEM((C, LON, LAT), BF),
        pltpu.SemaphoreType.DMA((34,)),
        pltpu.SemaphoreType.DMA((34,)),
        pltpu.SemaphoreType.DMA((11,)),
    ]
    extra = dict(collective_id=0, has_side_effects=True) if n_lon > 1 else {}
    results = pl.pallas_call(
        functools.partial(kernel_body, n_lon, n_sample, factor),
        out_shape=outs,
        in_specs=[vmem] * 4 + [far] * 9,
        out_specs=(far, far) + (vmem,) * 4,
        scratch_shapes=scratch,
        compiler_params=pltpu.CompilerParams(vmem_limit_bytes=62 * 1024 * 1024, **extra),
    )(
        state.reshape(C, LON, LAT),
        sea,
        taps.transpose(1, 2, 0),
        gain.reshape(1, C),
        cot.reshape(C, LON, LAT),
        win,
        wout.T,
        *spectral_constants(),
    )
    anywhere = pl.BlockSpec(memory_space=pl.ANY)
    return pl.pallas_call(
        deliver,
        out_shape=outs,
        in_specs=[anywhere] * 6,
        out_specs=(anywhere,) * 6,
        scratch_shapes=[pltpu.VMEM(out.shape, out.dtype) for out in outs]
        + [pltpu.SemaphoreType.DMA((2, 6))],
    )(*results)


def solution(mesh):
    n_lon, n_sample = mesh.shape["lon"], mesh.shape["sample"]
    factor = 1.0 / math.sqrt(n_sample * n_lon * LON * LAT)

    def on_device(state, cot, sea, taps, gain, win, wout):
        out = block(n_lon, n_sample, factor, state, cot, sea, taps, gain, win, wout)
        shape = state.shape
        return (
            out[0].reshape(shape),
            out[1].reshape(shape),
            out[2],
            out[3].T,
            out[4].transpose(2, 0, 1),
            out[5].reshape(OWN),
        )

    slab = P("sample", None, "lon", None)
    return jax.shard_map(
        on_device,
        mesh=mesh,
        in_specs=(slab, slab, P("lon", None), P(), P(), P(), P()),
        out_specs=(
            slab,
            slab,
            P("sample", None),
            P(None, "sample"),
            P("sample", None, None),
            P("sample"),
        ),
        check_vma=False,
    )
```

```python
import functools
import math

import jax
import jax.numpy as jnp
import numpy as np
from jax import lax
from jax.experimental import pallas as pl
from jax.experimental.pallas import tpu as pltpu
from jax.sharding import PartitionSpec as P

C = 192
HID = 768
LON = 16
LAT = 128
PERIOD = 131
SPEC = 256
TAPS = 7
HALO = 3
GROUP = 4
HID_BLOCK = 256
CELL_BLOCK = 256
TILE = 16
OWN = 12
PACKED = 1152
BF = jnp.bfloat16
F32 = jnp.float32
MESH = pl.DeviceIdType.MESH


def tree_sum(terms):
    while len(terms) > 1:
        paired = [terms[k] + terms[k + 1] for k in range(0, len(terms) - 1, 2)]
        if len(terms) % 2:
            paired.append(terms[-1])
        terms = paired
    return terms[0]


def matmul(left, right):
    return jnp.dot(left, right, preferred_element_type=F32)


def matmul_nt(left, right):
    return lax.dot_general(left, right, (((1,), (1,)), ((), ())), preferred_element_type=F32)


def split_constant(values):
    high = values.astype(BF)
    low = (values - high.astype(np.float64)).astype(BF)
    return high, low


def spectral_constants():
    angle = 2.0 * math.pi / PERIOD
    row = np.arange(LAT)
    field_f, field_b = np.zeros((LAT, SPEC)), np.zeros((LAT, SPEC))
    back_f, back_b = np.zeros((SPEC, LAT)), np.zeros((SPEC, LAT))
    taps = np.zeros((8, SPEC))
    shift = np.arange(TAPS) - HALO
    field_f[:, 0] = field_b[:, 0] = 1.0
    back_f[0] = back_b[0] = 1.0 / PERIOD
    taps[:TAPS, 0] = 1.0
    half = PERIOD // 2
    for f in range(1, half + 1):
        one, two, three = f, half + f, 2 * half + f
        cos, sin = np.cos(angle * f * row), np.sin(angle * f * row)
        c, d = np.cos(angle * f * shift), np.sin(angle * f * shift)
        taps[:TAPS, one], taps[:TAPS, two], taps[:TAPS, three] = c, d - c, c + d
        field_f[:, one], field_f[:, two], field_f[:, three] = cos - sin, cos, -sin
        field_b[:, one], field_b[:, two], field_b[:, three] = cos + sin, cos, sin
        scale = 2.0 / PERIOD
        back_f[one], back_f[two], back_f[three] = scale * (cos - sin), -scale * sin, -scale * cos
        back_b[one], back_b[two], back_b[three] = scale * (cos + sin), scale * sin, -scale * cos

    def stacked(values):
        return np.concatenate(split_constant(values), axis=0)

    def beside(values):
        return np.concatenate(split_constant(values), axis=1)

    spread_high, spread_low = np.zeros((64, TAPS * SPEC)), np.zeros((64, TAPS * SPEC))
    high, low = split_constant(taps)
    for a in range(TAPS):
        spread_high[8 * a : 8 * a + 8, a * SPEC : (a + 1) * SPEC] = high
        spread_low[8 * a : 8 * a + 8, a * SPEC : (a + 1) * SPEC] = low
    spread = np.concatenate([spread_high, spread_high, spread_low]).astype(BF)
    gather = np.zeros((SPEC, LAT))
    gather[:, :8] = taps.T
    return (
        spread,
        stacked(field_f),
        beside(back_f),
        np.concatenate([stacked(back_f.T), stacked(field_b)], axis=1),
        beside(back_b),
        beside(gather),
    )


def column(ref, at):
    return ref[pl.ds(at, C, stride=LON), :]


def kernel_body(
    n_lon,
    n_sample,
    factor,
    sea_ref,
    taps_ref,
    gain_ref,
    state_far,
    cot_far,
    win_far,
    wout_far,
    spread_far,
    field_f_far,
    back_f_far,
    field_g_far,
    back_b_far,
    gather_far,
    sout_ref,
    gin_ref,
    gwin_ref,
    gwout_ref,
    gk_ref,
    gg_ref,
    state_ref,
    cot_ref,
    win_ref,
    wout_t,
    spread,
    field_f,
    back_f,
    field_g,
    back_b,
    gather,
    x32,
    c32,
    xa,
    ga,
    xh,
    gh,
    gw,
    kf,
    dkf,
    flat_taps,
    sum_high,
    sum_low,
    gainb,
    win_t,
    wout,
    norm_all,
    cot_all,
    hid_all,
    gp_all,
    scaled_all,
    inv_all,
    acc_in,
    acc_out,
    acc_gain,
    dks,
    stage,
    wsend,
    wcore,
    wmid,
    wparts,
    wslab,
    ksend,
    kcore,
    kmid,
    kparts,
    kslab,
    kout,
    sout_buf,
    gin_buf,
    send,
    recv,
    near,
):
    fetches = [
        pltpu.make_async_copy(far, here, near.at[k])
        for k, (far, here) in enumerate(
            (
                (spread_far, spread),
                (field_f_far, field_f),
                (back_f_far, back_f),
                (win_far, win_ref),
                (wout_far, wout_t),
                (cot_far, cot_ref),
                (field_g_far, field_g),
                (back_b_far, back_b),
                (gather_far, gather),
            )
        )
    ]
    remote = n_lon > 1
    if remote:
        lon = lax.axis_index("lon")
        sample = lax.axis_index("sample")
        core = lax.rem(sample, 2)
        owner = sample // 2
        n_own = n_sample // 2
        partner = {"sample": sample + 1 - 2 * core}
        right = {"lon": lax.rem(lon + 1, n_lon)}
        left = {"lon": lax.rem(lon + n_lon - 1, n_lon)}
        owners = [lax.rem(owner + d, n_own) for d in range(1, n_own)]
        slabs = [lax.rem(lon + d, n_lon) for d in range(1, n_lon)]
        peers = (
            [partner]
            + [{"sample": 2 * other + core} for other in owners]
            + [{"lon": other} for other in slabs]
        )
        barrier = pltpu.get_barrier_semaphore()
        for peer in peers:
            pl.semaphore_signal(barrier, inc=1, device_id=peer, device_id_type=MESH)

        def copy(src, dst, slot, peer):
            return pltpu.make_async_remote_copy(
                src_ref=src,
                dst_ref=dst,
                send_sem=send.at[slot],
                recv_sem=recv.at[slot],
                device_id=peer,
                device_id_type=MESH,
            )

    def halo_copies(ref, slot):
        return (
            copy(ref.at[pl.ds(LON, HALO)], ref.at[pl.ds(0, HALO)], slot, right),
            copy(ref.at[pl.ds(HALO, HALO)], ref.at[pl.ds(LON + HALO, HALO)], slot + 1, left),
        )

    def local_halo(ref):
        ref[0:HALO] = ref[LON : LON + HALO]
        ref[LON + HALO : LON + 2 * HALO] = ref[HALO : 2 * HALO]

    arrive = pltpu.make_async_copy(state_far, state_ref, near.at[11])
    arrive.start()
    for fetch in fetches:
        fetch.start()
    arrive.wait()
    x32[...] = state_ref[...].astype(F32).reshape(C * LON, LAT)
    for i in (0, 1, 2, 13, 14, 15):
        xa[HALO + i] = column(x32, i).astype(BF)
    if remote:
        pl.semaphore_wait(barrier, len(peers))
        x_right, x_left = halo_copies(xa, 0)
        x_left.start()
        x_right.start()
    for i in range(3, 13):
        xa[HALO + i] = column(x32, i).astype(BF)
    for fetch in fetches:
        fetch.wait()
    c32[...] = cot_ref[...].astype(F32).reshape(C * LON, LAT)

    flat_taps[...] = jnp.zeros_like(flat_taps)
    for a in range(TAPS):
        flat_taps[8 * a : 8 * a + TAPS, 0:C] = taps_ref[a]
    rest = flat_taps[...].T[0:C, :]
    high = rest.astype(BF)
    low = (rest - high.astype(F32)).astype(BF)
    kf[...] = matmul(
        jnp.concatenate([high[:, 0:64], low[:, 0:64], high[:, 0:64]], axis=1), spread[...]
    )
    gainb[...] = jnp.broadcast_to(gain_ref[...], (LAT, C)).T
    win_t[...] = (0.5 * win_ref[...].astype(F32)).astype(BF).T
    wout[...] = (0.5 * wout_t[...].astype(F32)).astype(BF).T
    acc_gain[...] = jnp.zeros_like(acc_gain)

    def doubled(columns):
        flat = columns.reshape(-1, LAT)
        return jnp.concatenate([flat, flat], axis=1)

    def field_spectrum(at, count):
        spectrum = matmul(doubled(xa[at : at + count]), field_f[...])
        xh[at : at + count] = spectrum.reshape(count, C, SPEC)

    def grad_spectrum(at, count):
        spectrum = matmul(doubled(ga[at : at + count]), field_g[:, SPEC:])
        gh[at : at + count] = spectrum.reshape(count, C, SPEC)

    def filtered(field, col, flip, inverse):
        def one_tile(tile, carry):
            at = pl.multiple_of(tile * TILE, TILE)
            for half in range(0, SPEC, LAT):
                window = field[pl.ds(col, GROUP + 2 * HALO), pl.ds(at, TILE), half : half + LAT]
                terms = []
                for a in range(TAPS):
                    first = 2 * HALO - a if flip else a
                    lane = a * SPEC + half
                    weight = kf[pl.ds(at, TILE), lane : lane + LAT]
                    terms.append(weight[None] * window[first : first + GROUP])
                total = tree_sum(terms)
                high = total.astype(BF)
                sum_high[:, pl.ds(at, TILE), half : half + LAT] = high
                sum_low[:, pl.ds(at, TILE), half : half + LAT] = (
                    total - high.astype(F32)
                ).astype(BF)
            return carry

        lax.fori_loop(0, C // TILE, one_tile, 0, unroll=2)
        main = matmul(sum_high[...].reshape(GROUP * C, SPEC), inverse[...])
        rest = matmul(sum_low[...].reshape(GROUP * C, SPEC), inverse[:, 0:LAT])
        return (main[:, 0:LAT] + main[:, LAT:] + rest).reshape(GROUP, C, LAT)

    def masks(col):
        return [sea_ref[pl.ds(col + k, 1), :].astype(F32) for k in range(GROUP)]

    def side_by_side(parts):
        return jnp.concatenate([parts[k] for k in range(GROUP)], axis=1)

    def first_cell(col):
        turned = col + LON - GROUP
        return (turned % LON if isinstance(col, int) else lax.rem(turned, LON)) * LAT

    def lanes_of(col):
        return pl.ds(pl.multiple_of(first_cell(col), GROUP * LAT), GROUP * LAT)

    def forward_group(col):
        mixed = filtered(xh, col, False, back_f)
        centred = mixed - jnp.mean(mixed, axis=1, keepdims=True)
        variance = jnp.mean(centred * centred, axis=1, keepdims=True)
        inv_scale = lax.rsqrt(variance + 1e-06)
        scaled = centred * inv_scale
        scaled_all[pl.ds(col, GROUP)] = scaled
        inv_all[pl.ds(col, GROUP), :] = inv_scale.reshape(GROUP, LAT)
        normed = side_by_side((scaled * gainb[...][None]).astype(BF))
        mask = masks(col)
        grad_out = side_by_side([(column(c32, col + k) * mask[k]).astype(BF) for k in range(GROUP)])
        where = lanes_of(col)
        norm_all[:, where] = normed
        cot_all[:, where] = grad_out
        for h in range(0, HID, HID_BLOCK):
            for n in range(0, GROUP * LAT, CELL_BLOCK):
                half = matmul(win_t[h : h + HID_BLOCK, :], normed[:, n : n + CELL_BLOCK])
                grad_half = matmul(wout[h : h + HID_BLOCK, :], grad_out[:, n : n + CELL_BLOCK])
                square = half * half
                bent = jnp.tanh(half * (1.5957691216057308 + 0.28541926509040104 * square))
                gate = 1.0 + bent
                hidden = half * gate
                slope = gate + hidden * (1.0 - bent) * (
                    1.5957691216057308 + 0.8562577952712031 * square
                )
                at = pl.ds(pl.multiple_of(first_cell(col) + n, CELL_BLOCK), CELL_BLOCK)
                hid_all[h : h + HID_BLOCK, at] = hidden.astype(BF)
                gp_all[h : h + HID_BLOCK, at] = (grad_half * slope).astype(BF)

    def finish_state(col):
        mask = masks(col)
        branch = matmul(wout_t[...], hid_all[:, lanes_of(col)])
        for k in range(GROUP):
            lane = slice(k * LAT, (k + 1) * LAT)
            at = pl.ds(col + k, C, stride=LON)
            x32[at, :] = mask[k] * (x32[at, :] + branch[:, lane])

    def backward_mlp(col):
        where = lanes_of(col)
        gain = gainb[...]
        grad_normed = matmul(win_ref[...], gp_all[:, where])
        for k in range(GROUP):
            lane = slice(k * LAT, (k + 1) * LAT)
            scaled = scaled_all[col + k]
            grad = grad_normed[:, lane]
            product = grad * scaled
            acc_gain[...] += product
            grad_scaled = grad * gain
            first = jnp.mean(grad_scaled, axis=0, keepdims=True)
            second = jnp.mean(product * gain, axis=0, keepdims=True)
            inv_scale = inv_all[pl.ds(col + k, 1), :]
            grad_conv = (inv_scale * (grad_scaled - first - scaled * second)).astype(BF)
            ga[HALO + col + k] = grad_conv
            spectrum = matmul(doubled(grad_conv), field_g[...])
            gw[col + k] = spectrum[:, 0:SPEC]
            gh[HALO + col + k] = spectrum[:, SPEC:]

    def in_groups(first, last, work):
        def one_group(step, carry):
            work(lax.rem(GROUP + step * GROUP, LON))
            return carry

        lax.fori_loop(first, last, one_group, 0)

    def start(copies):
        for one in copies:
            one.start()

    def wait(copies):
        for one in copies:
            one.wait()

    for at in range(HALO, LON + HALO, GROUP):
        field_spectrum(at, GROUP)
    def filter_grads(first, last):
        def one_tile(tile, carry):
            at = pl.multiple_of(tile * 8, 8)
            for half in range(0, SPEC, LAT):
                totals = [None] * TAPS
                for col in range(0, LON, 8):
                    grads = gw[col : col + 8, pl.ds(at, 8), half : half + LAT]
                    for a in range(TAPS):
                        field = xh[col + a : col + a + 8, pl.ds(at, 8), half : half + LAT]
                        part = jnp.sum(grads * field, axis=0)
                        totals[a] = part if totals[a] is None else totals[a] + part
                for a in range(TAPS):
                    dkf[pl.ds(at, 8), a * SPEC + half : a * SPEC + half + LAT] = totals[a]
            return carry

        lax.fori_loop(first, last, one_tile, 0, unroll=2)

    in_groups(0, 2, forward_group)
    cells = slice(0, LON * LAT // 2)
    acc_out[...] = matmul_nt(cot_all[:, cells], hid_all[:, cells])
    acc_in[...] = matmul_nt(norm_all[:, cells], gp_all[:, cells])
    if remote:
        g_right, g_left = halo_copies(ga, 2)
        x_left.wait()
    else:
        local_halo(xa)
    field_spectrum(LON + HALO, HALO)
    forward_group(LON - GROUP)
    backward_mlp(LON - GROUP)
    if remote:
        g_right.start()
        x_right.wait()
    field_spectrum(0, HALO)
    forward_group(0)

    cells = slice(LON * LAT // 2, LON * LAT)
    acc_out[...] += matmul_nt(cot_all[:, cells], hid_all[:, cells])
    acc_in[...] += matmul_nt(norm_all[:, cells], gp_all[:, cells])
    wide = HID // 2
    for o in range(16):
        at = OWN * o
        stage[o, 0:12, 0:HID] = acc_in[at : at + 12, :]
        stage[o, 12:16, 0:HID] = acc_out[at : at + 4, :]
        stage[o, 0:8, HID:PACKED] = acc_out[at + 4 : at + 12, 0:wide]
        stage[o, 8:16, HID:PACKED] = acc_out[at + 4 : at + 12, wide:HID]
    for o in range(16):
        wsend[o % 2, o // 2] = stage[o].astype(BF)

    if remote:

        def to_slabs(slab, base):
            return [
                copy(slab.at[lon], slab.at[lon], base + d, {"lon": other})
                for d, other in enumerate(slabs)
            ]

        def to_owners(source, target, base):
            return [
                copy(source.at[other], target.at[d], base + d, {"sample": 2 * other + core})
                for d, other in enumerate(owners)
            ]

        def w_core():
            return [copy(wsend.at[1 - core], wcore, 4, partner)]

        def w_own():
            return to_owners(wmid, wparts, 5)

        def w_all():
            return to_slabs(wslab, 12)

        def k_core():
            return [copy(ksend.at[1 - core], kcore, 19, partner)]

        def k_own():
            return to_owners(kmid, kparts, 20)

        def k_all():
            return to_slabs(kslab, 27)

        start(w_core())
    backward_mlp(0)
    if remote:
        g_left.start()
    in_groups(0, 1, backward_mlp)
    if remote:
        wait(w_core())
        wmid[...] = (wsend[core].astype(F32) + wcore[...].astype(F32)).astype(BF)
        start(w_own())
    in_groups(1, 2, backward_mlp)
    filter_grads(0, C // 8)

    lanes = lax.broadcasted_iota(jnp.int32, (C, LAT), 1)
    total = jnp.where(lanes == TAPS * TAPS, jnp.sum(acc_gain[...], axis=1, keepdims=True), 0.0)
    for a in range(TAPS):
        part = dkf[:, a * SPEC : (a + 1) * SPEC]
        high = part.astype(BF)
        low = (part - high.astype(F32)).astype(BF)
        both = matmul(high, gather[...])
        found = both[:, 0:LAT] + both[:, LAT:] + matmul(low, gather[:, 0:LAT])
        total = total + (pltpu.roll(found, a * TAPS, axis=1) if a else found)
    dks[0, 0:C, :] = total
    dks[1, 0:C, :] = pltpu.roll(total, LAT // 2, axis=1)
    for side in range(2):
        dks[side, C : C + 16, :] = jnp.zeros((16, LAT), F32)
    for o in range(16):
        at = OWN * o
        ksend[o % 2, o // 2] = dks[0, at : at + 8, :] + dks[1, at + 6 : at + 14, :]
    if remote:
        start(k_core())
    in_groups(0, 2, finish_state)
    if remote:
        wait(k_core())
        kmid[...] = ksend[core] + kcore[...]
        start(k_own())
    in_groups(2, 4, finish_state)
    sout_buf[...] = x32[...].reshape(C, LON, LAT).astype(BF)
    leave = [
        pltpu.make_async_copy(sout_buf, sout_ref, near.at[9]),
        pltpu.make_async_copy(gin_buf, gin_ref, near.at[10]),
    ]
    leave[0].start()

    def backward_group(col):
        moved = filtered(gh, col, True, back_b)
        mask = masks(col)
        for k in range(GROUP):
            at = pl.ds(col + k, C, stride=LON)
            c32[at, :] = c32[at, :] * mask[k] + moved[k]

    in_groups(0, 1, backward_group)
    if remote:
        wait(w_own())
        held = wmid[owner].astype(F32)
        for d in range(len(owners)):
            held = held + wparts[d].astype(F32)
        wslab[lon] = held.astype(BF)
        start(w_all())
    in_groups(1, 2, backward_group)
    if remote:
        g_right.wait()
    else:
        local_halo(ga)
    grad_spectrum(0, HALO)
    backward_group(0)
    if remote:
        wait(k_own())
        held = kmid[owner]
        for d in range(len(owners)):
            held = held + kparts[d]
        kslab[lon] = held
        start(k_all())
        g_left.wait()
    grad_spectrum(LON + HALO, HALO)
    backward_group(LON - GROUP)
    gin_buf[...] = c32[...].reshape(C, LON, LAT).astype(BF)
    leave[1].start()
    if remote:
        wait(w_all())
        weights = wslab[0].astype(F32)
        for other in range(1, n_lon):
            weights = weights + wslab[other].astype(F32)
        wait(k_all())
        small = kslab[0]
        for other in range(1, n_lon):
            small = small + kslab[other]
    else:
        weights = wsend[0, 0].astype(F32)
        small = ksend[0, 0]
    weights = weights * factor
    small = small * factor
    gwin_ref[...] = weights[0:12, 0:HID]
    gwout_ref[0:4, :] = weights[12:16, 0:HID]
    gwout_ref[4:12, 0:wide] = weights[0:8, HID:PACKED]
    gwout_ref[4:12, wide:HID] = weights[8:16, HID:PACKED]
    kout[0:6, :] = small[0:6, :]
    kout[6:12, :] = pltpu.roll(small, LAT // 2, axis=1)[0:6, :]
    small_t = kout[...].T
    for a in range(TAPS):
        gk_ref[a] = small_t[a * TAPS : (a + 1) * TAPS, 0:OWN]
    gg_ref[...] = small_t[TAPS * TAPS : TAPS * TAPS + 1, 0:OWN]
    for one in leave:
        one.wait()


def deliver(*refs):
    count = len(refs) // 3
    sems = refs[-1]
    sources, targets, held = refs[:count], refs[count : 2 * count], refs[2 * count : 3 * count]
    arrive = [pltpu.make_async_copy(sources[k], held[k], sems.at[0, k]) for k in range(count)]
    leave = [pltpu.make_async_copy(held[k], targets[k], sems.at[1, k]) for k in range(count)]
    for one in arrive:
        one.start()
    for k in range(count):
        arrive[k].wait()
        leave[k].start()
    for one in leave:
        one.wait()


def block(n_lon, n_sample, factor, state, cot, sea, taps, gain, win, wout):
    vmem = pl.BlockSpec(memory_space=pltpu.VMEM)
    far = pl.BlockSpec(memory_space=pltpu.HBM)
    shape = jax.ShapeDtypeStruct
    outs = (
        shape((C, LON, LAT), BF),
        shape((C, LON, LAT), BF),
        shape((OWN, HID), F32),
        shape((OWN, HID), F32),
        shape((TAPS, TAPS, OWN), F32),
        shape((1, OWN), F32),
    )
    scratch = [
        pltpu.VMEM((C, LON, LAT), BF),
        pltpu.VMEM((C, LON, LAT), BF),
        pltpu.VMEM((C, HID), BF),
        pltpu.VMEM((C, HID), BF),
        pltpu.VMEM((3 * 64, TAPS * SPEC), BF),
        pltpu.VMEM((2 * LAT, SPEC), BF),
        pltpu.VMEM((SPEC, 2 * LAT), BF),
        pltpu.VMEM((2 * LAT, 2 * SPEC), BF),
        pltpu.VMEM((SPEC, 2 * LAT), BF),
        pltpu.VMEM((SPEC, 2 * LAT), BF),
        pltpu.VMEM((C * LON, LAT), F32),
        pltpu.VMEM((C * LON, LAT), F32),
        pltpu.VMEM((LON + 2 * HALO, C, LAT), BF),
        pltpu.VMEM((LON + 2 * HALO, C, LAT), BF),
        pltpu.VMEM((LON + 2 * HALO, C, SPEC), F32),
        pltpu.VMEM((LON + 2 * HALO, C, SPEC), F32),
        pltpu.VMEM((LON, C, SPEC), F32),
        pltpu.VMEM((C, TAPS * SPEC), F32),
        pltpu.VMEM((C, TAPS * SPEC), F32),
        pltpu.VMEM((LAT, 2 * LAT), F32),
        pltpu.VMEM((GROUP, C, SPEC), BF),
        pltpu.VMEM((GROUP, C, SPEC), BF),
        pltpu.VMEM((C, LAT), F32),
        pltpu.VMEM((HID, C), BF),
        pltpu.VMEM((HID, C), BF),
        pltpu.VMEM((C, LON * LAT), BF),
        pltpu.VMEM((C, LON * LAT), BF),
        pltpu.VMEM((HID, LON * LAT), BF),
        pltpu.VMEM((HID, LON * LAT), BF),
        pltpu.VMEM((LON, C, LAT), F32),
        pltpu.VMEM((LON, LAT), F32),
        pltpu.VMEM((C, HID), F32),
        pltpu.VMEM((C, HID), F32),
        pltpu.VMEM((C, LAT), F32),
        pltpu.VMEM((2, C + 16, LAT), F32),
        pltpu.VMEM((16, 16, PACKED), F32),
        pltpu.VMEM((2, 8, 16, PACKED), BF),
        pltpu.VMEM((8, 16, PACKED), BF),
        pltpu.VMEM((8, 16, PACKED), BF),
        pltpu.VMEM((7, 16, PACKED), BF),
        pltpu.VMEM((8, 16, PACKED), BF),
        pltpu.VMEM((2, 8, 8, LAT), F32),
        pltpu.VMEM((8, 8, LAT), F32),
        pltpu.VMEM((8, 8, LAT), F32),
        pltpu.VMEM((7, 8, LAT), F32),
        pltpu.VMEM((8, 8, LAT), F32),
        pltpu.VMEM((16, LAT), F32),
        pltpu.VMEM((C, LON, LAT), BF),
        pltpu.VMEM((C, LON, LAT), BF),
        pltpu.SemaphoreType.DMA((34,)),
        pltpu.SemaphoreType.DMA((34,)),
        pltpu.SemaphoreType.DMA((12,)),
    ]
    extra = dict(collective_id=0, has_side_effects=True) if n_lon > 1 else {}
    results = pl.pallas_call(
        functools.partial(kernel_body, n_lon, n_sample, factor),
        out_shape=outs,
        in_specs=[vmem] * 3 + [far] * 10,
        out_specs=(far, far) + (vmem,) * 4,
        scratch_shapes=scratch,
        compiler_params=pltpu.CompilerParams(vmem_limit_bytes=62 * 1024 * 1024, **extra),
    )(
        sea,
        taps.transpose(1, 2, 0),
        gain.reshape(1, C),
        state.reshape(C, LON, LAT),
        cot.reshape(C, LON, LAT),
        win,
        wout.T,
        *spectral_constants(),
    )
    anywhere = pl.BlockSpec(memory_space=pl.ANY)
    return pl.pallas_call(
        deliver,
        out_shape=outs,
        in_specs=[anywhere] * 6,
        out_specs=(anywhere,) * 6,
        scratch_shapes=[pltpu.VMEM(out.shape, out.dtype) for out in outs]
        + [pltpu.SemaphoreType.DMA((2, 6))],
    )(*results)


def solution(mesh):
    n_lon, n_sample = mesh.shape["lon"], mesh.shape["sample"]
    factor = 1.0 / math.sqrt(n_sample * n_lon * LON * LAT)

    def on_device(state, cot, sea, taps, gain, win, wout):
        out = block(n_lon, n_sample, factor, state, cot, sea, taps, gain, win, wout)
        shape = state.shape
        return (
            out[0].reshape(shape),
            out[1].reshape(shape),
            out[2],
            out[3].T,
            out[4].transpose(2, 0, 1),
            out[5].reshape(OWN),
        )

    slab = P("sample", None, "lon", None)
    return jax.shard_map(
        on_device,
        mesh=mesh,
        in_specs=(slab, slab, P("lon", None), P(), P(), P(), P()),
        out_specs=(
            slab,
            slab,
            P("sample", None),
            P(None, "sample"),
            P("sample", None, None),
            P("sample"),
        ),
        check_vma=False,
    )
```

```python
import functools
import math

import jax
import jax.numpy as jnp
import numpy as np
from jax import lax
from jax.experimental import pallas as pl
from jax.experimental.pallas import tpu as pltpu
from jax.sharding import PartitionSpec as P

C = 192
HID = 768
LON = 16
LAT = 128
PERIOD = 131
SPEC = 256
TAPS = 7
HALO = 3
GROUP = 4
HID_BLOCK = 256
CELL_BLOCK = 256
TILE = 16
OWN = 12
PACKED = 1152
BF = jnp.bfloat16
F32 = jnp.float32
MESH = pl.DeviceIdType.MESH


def tree_sum(terms):
    while len(terms) > 1:
        paired = [terms[k] + terms[k + 1] for k in range(0, len(terms) - 1, 2)]
        if len(terms) % 2:
            paired.append(terms[-1])
        terms = paired
    return terms[0]


def matmul(left, right):
    return jnp.dot(left, right, preferred_element_type=F32)


def matmul_nt(left, right):
    return lax.dot_general(left, right, (((1,), (1,)), ((), ())), preferred_element_type=F32)


def split_constant(values):
    high = values.astype(BF)
    low = (values - high.astype(np.float64)).astype(BF)
    return high, low


def spectral_constants():
    angle = 2.0 * math.pi / PERIOD
    row = np.arange(LAT)
    field_f, field_b = np.zeros((LAT, SPEC)), np.zeros((LAT, SPEC))
    back_f, back_b = np.zeros((SPEC, LAT)), np.zeros((SPEC, LAT))
    taps = np.zeros((8, SPEC))
    shift = np.arange(TAPS) - HALO
    field_f[:, 0] = field_b[:, 0] = 1.0
    back_f[0] = back_b[0] = 1.0 / PERIOD
    taps[:TAPS, 0] = 1.0
    half = PERIOD // 2
    for f in range(1, half + 1):
        one, two, three = f, half + f, 2 * half + f
        cos, sin = np.cos(angle * f * row), np.sin(angle * f * row)
        c, d = np.cos(angle * f * shift), np.sin(angle * f * shift)
        taps[:TAPS, one], taps[:TAPS, two], taps[:TAPS, three] = c, d - c, c + d
        field_f[:, one], field_f[:, two], field_f[:, three] = cos - sin, cos, -sin
        field_b[:, one], field_b[:, two], field_b[:, three] = cos + sin, cos, sin
        scale = 2.0 / PERIOD
        back_f[one], back_f[two], back_f[three] = scale * (cos - sin), -scale * sin, -scale * cos
        back_b[one], back_b[two], back_b[three] = scale * (cos + sin), scale * sin, -scale * cos

    def stacked(values):
        return np.concatenate(split_constant(values), axis=0)

    def beside(values):
        return np.concatenate(split_constant(values), axis=1)

    spread_high, spread_low = np.zeros((64, TAPS * SPEC)), np.zeros((64, TAPS * SPEC))
    high, low = split_constant(taps)
    for a in range(TAPS):
        spread_high[8 * a : 8 * a + 8, a * SPEC : (a + 1) * SPEC] = high
        spread_low[8 * a : 8 * a + 8, a * SPEC : (a + 1) * SPEC] = low
    spread = np.concatenate([spread_high, spread_high, spread_low]).astype(BF)
    gather = np.zeros((SPEC, LAT))
    gather[:, :8] = taps.T
    return (
        spread,
        stacked(field_f),
        beside(back_f),
        np.concatenate([stacked(back_f.T), stacked(field_b)], axis=1),
        beside(back_b),
        beside(gather),
    )


def column(ref, at):
    return ref[pl.ds(at, C, stride=LON), :]


def kernel_body(
    n_lon,
    n_sample,
    factor,
    sea_ref,
    taps_ref,
    gain_ref,
    state_far,
    cot_far,
    win_far,
    wout_far,
    spread_far,
    field_f_far,
    back_f_far,
    field_g_far,
    back_b_far,
    gather_far,
    sout_ref,
    gin_ref,
    gwin_ref,
    gwout_ref,
    gk_ref,
    gg_ref,
    state_ref,
    cot_ref,
    win_ref,
    wout_t,
    spread,
    field_f,
    back_f,
    field_g,
    back_b,
    gather,
    x32,
    c32,
    xa,
    ga,
    xh,
    gh,
    gw,
    kf,
    dkf,
    flat_taps,
    sum_high,
    sum_low,
    gainb,
    win_t,
    wout,
    norm_all,
    cot_all,
    hid_all,
    gp_all,
    scaled_all,
    inv_all,
    acc_in,
    acc_out,
    acc_gain,
    dks,
    stage,
    wsend,
    wcore,
    wmid,
    wparts,
    wslab,
    ksend,
    kcore,
    kmid,
    kparts,
    kslab,
    kout,
    sout_buf,
    gin_buf,
    send,
    recv,
    near,
):
    fetches = [
        pltpu.make_async_copy(far, here, near.at[k])
        for k, (far, here) in enumerate(
            (
                (spread_far, spread),
                (field_f_far, field_f),
                (back_f_far, back_f),
                (win_far, win_ref),
                (wout_far, wout_t),
                (cot_far, cot_ref),
                (field_g_far, field_g),
                (back_b_far, back_b),
                (gather_far, gather),
            )
        )
    ]
    remote = n_lon > 1
    if remote:
        lon = lax.axis_index("lon")
        sample = lax.axis_index("sample")
        core = lax.rem(sample, 2)
        owner = sample // 2
        n_own = n_sample // 2
        partner = {"sample": sample + 1 - 2 * core}
        right = {"lon": lax.rem(lon + 1, n_lon)}
        left = {"lon": lax.rem(lon + n_lon - 1, n_lon)}
        deep = n_own // 2
        owners = [
            lax.rem(owner // deep + far, 2) * deep + lax.rem(owner + step, deep)
            for far, step in ((1, 2), (1, 1), (1, 3), (1, 0), (0, 2), (0, 1), (0, 3))
        ]
        slabs = [
            2 * lax.rem(lon // 2 + step, n_lon // 2) + lax.rem(lon + side, 2)
            for side, step in ((1, 2), (0, 2), (1, 1), (1, 3), (0, 1), (0, 3), (1, 0))
        ]
        peers = (
            [{"sample": 2 * other + core} for other in owners]
            + [{"lon": other} for other in slabs]
            + [partner]
        )
        barrier = pltpu.get_barrier_semaphore()
        for peer in peers:
            pl.semaphore_signal(barrier, inc=1, device_id=peer, device_id_type=MESH)

        def copy(src, dst, slot, peer):
            return pltpu.make_async_remote_copy(
                src_ref=src,
                dst_ref=dst,
                send_sem=send.at[slot],
                recv_sem=recv.at[slot],
                device_id=peer,
                device_id_type=MESH,
            )

    def halo_copies(ref, slot):
        return (
            copy(ref.at[pl.ds(LON, HALO)], ref.at[pl.ds(0, HALO)], slot, right),
            copy(ref.at[pl.ds(HALO, HALO)], ref.at[pl.ds(LON + HALO, HALO)], slot + 1, left),
        )

    def local_halo(ref):
        ref[0:HALO] = ref[LON : LON + HALO]
        ref[LON + HALO : LON + 2 * HALO] = ref[HALO : 2 * HALO]

    arrive = pltpu.make_async_copy(state_far, state_ref, near.at[11])
    arrive.start()
    for fetch in fetches:
        fetch.start()
    arrive.wait()
    x32[...] = state_ref[...].astype(F32).reshape(C * LON, LAT)
    for i in (0, 1, 2, 13, 14, 15):
        xa[HALO + i] = column(x32, i).astype(BF)
    if remote:
        pl.semaphore_wait(barrier, len(peers))
        x_right, x_left = halo_copies(xa, 0)
        x_left.start()
        x_right.start()
    for i in range(3, 13):
        xa[HALO + i] = column(x32, i).astype(BF)
    for fetch in fetches:
        fetch.wait()
    c32[...] = cot_ref[...].astype(F32).reshape(C * LON, LAT)

    flat_taps[...] = jnp.zeros_like(flat_taps)
    for a in range(TAPS):
        flat_taps[8 * a : 8 * a + TAPS, 0:C] = taps_ref[a]
    rest = flat_taps[...].T[0:C, :]
    high = rest.astype(BF)
    low = (rest - high.astype(F32)).astype(BF)
    kf[...] = matmul(
        jnp.concatenate([high[:, 0:64], low[:, 0:64], high[:, 0:64]], axis=1), spread[...]
    )
    gainb[...] = jnp.broadcast_to(gain_ref[...], (LAT, C)).T
    win_t[...] = (0.5 * win_ref[...].astype(F32)).astype(BF).T
    wout[...] = (0.5 * wout_t[...].astype(F32)).astype(BF).T
    acc_gain[...] = jnp.zeros_like(acc_gain)

    def doubled(columns):
        flat = columns.reshape(-1, LAT)
        return jnp.concatenate([flat, flat], axis=1)

    def field_spectrum(at, count):
        spectrum = matmul(doubled(xa[at : at + count]), field_f[...])
        xh[at : at + count] = spectrum.reshape(count, C, SPEC)

    def grad_spectrum(at, count):
        spectrum = matmul(doubled(ga[at : at + count]), field_g[:, SPEC:])
        gh[at : at + count] = spectrum.reshape(count, C, SPEC)

    def filtered(field, col, flip, inverse):
        def one_tile(tile, carry):
            at = pl.multiple_of(tile * TILE, TILE)
            for half in range(0, SPEC, LAT):
                window = field[pl.ds(col, GROUP + 2 * HALO), pl.ds(at, TILE), half : half + LAT]
                terms = []
                for a in range(TAPS):
                    first = 2 * HALO - a if flip else a
                    lane = a * SPEC + half
                    weight = kf[pl.ds(at, TILE), lane : lane + LAT]
                    terms.append(weight[None] * window[first : first + GROUP])
                total = tree_sum(terms)
                high = total.astype(BF)
                sum_high[:, pl.ds(at, TILE), half : half + LAT] = high
                sum_low[:, pl.ds(at, TILE), half : half + LAT] = (
                    total - high.astype(F32)
                ).astype(BF)
            return carry

        lax.fori_loop(0, C // TILE, one_tile, 0, unroll=2)
        main = matmul(sum_high[...].reshape(GROUP * C, SPEC), inverse[...])
        rest = matmul(sum_low[...].reshape(GROUP * C, SPEC), inverse[:, 0:LAT])
        return (main[:, 0:LAT] + main[:, LAT:] + rest).reshape(GROUP, C, LAT)

    def masks(col):
        return [sea_ref[pl.ds(col + k, 1), :].astype(F32) for k in range(GROUP)]

    def side_by_side(parts):
        return jnp.concatenate([parts[k] for k in range(GROUP)], axis=1)

    def first_cell(col):
        turned = col + LON - GROUP
        return (turned % LON if isinstance(col, int) else lax.rem(turned, LON)) * LAT

    def lanes_of(col):
        return pl.ds(pl.multiple_of(first_cell(col), GROUP * LAT), GROUP * LAT)

    def forward_group(col):
        mixed = filtered(xh, col, False, back_f)
        centred = mixed - jnp.mean(mixed, axis=1, keepdims=True)
        variance = jnp.mean(centred * centred, axis=1, keepdims=True)
        inv_scale = lax.rsqrt(variance + 1e-06)
        scaled = centred * inv_scale
        scaled_all[pl.ds(col, GROUP)] = scaled
        inv_all[pl.ds(col, GROUP), :] = inv_scale.reshape(GROUP, LAT)
        normed = side_by_side((scaled * gainb[...][None]).astype(BF))
        mask = masks(col)
        grad_out = side_by_side([(column(c32, col + k) * mask[k]).astype(BF) for k in range(GROUP)])
        where = lanes_of(col)
        norm_all[:, where] = normed
        cot_all[:, where] = grad_out
        for h in range(0, HID, HID_BLOCK):
            for n in range(0, GROUP * LAT, CELL_BLOCK):
                half = matmul(win_t[h : h + HID_BLOCK, :], normed[:, n : n + CELL_BLOCK])
                grad_half = matmul(wout[h : h + HID_BLOCK, :], grad_out[:, n : n + CELL_BLOCK])
                square = half * half
                bent = jnp.tanh(half * (1.5957691216057308 + 0.28541926509040104 * square))
                gate = 1.0 + bent
                hidden = half * gate
                slope = gate + hidden * (1.0 - bent) * (
                    1.5957691216057308 + 0.8562577952712031 * square
                )
                at = pl.ds(pl.multiple_of(first_cell(col) + n, CELL_BLOCK), CELL_BLOCK)
                hid_all[h : h + HID_BLOCK, at] = hidden.astype(BF)
                gp_all[h : h + HID_BLOCK, at] = (grad_half * slope).astype(BF)

    def finish_state(col):
        mask = masks(col)
        branch = matmul(wout_t[...], hid_all[:, lanes_of(col)])
        for k in range(GROUP):
            lane = slice(k * LAT, (k + 1) * LAT)
            at = pl.ds(col + k, C, stride=LON)
            x32[at, :] = mask[k] * (x32[at, :] + branch[:, lane])

    def backward_mlp(col):
        where = lanes_of(col)
        gain = gainb[...]
        grad_normed = matmul(win_ref[...], gp_all[:, where])
        for k in range(GROUP):
            lane = slice(k * LAT, (k + 1) * LAT)
            scaled = scaled_all[col + k]
            grad = grad_normed[:, lane]
            product = grad * scaled
            acc_gain[...] += product
            grad_scaled = grad * gain
            first = jnp.mean(grad_scaled, axis=0, keepdims=True)
            second = jnp.mean(product * gain, axis=0, keepdims=True)
            inv_scale = inv_all[pl.ds(col + k, 1), :]
            grad_conv = (inv_scale * (grad_scaled - first - scaled * second)).astype(BF)
            ga[HALO + col + k] = grad_conv
            spectrum = matmul(doubled(grad_conv), field_g[...])
            gw[col + k] = spectrum[:, 0:SPEC]
            gh[HALO + col + k] = spectrum[:, SPEC:]

    def in_groups(first, last, work):
        def one_group(step, carry):
            work(lax.rem(GROUP + step * GROUP, LON))
            return carry

        lax.fori_loop(first, last, one_group, 0)

    def start(copies):
        for one in copies:
            one.start()

    def wait(copies):
        for one in copies:
            one.wait()

    for at in range(HALO, LON + HALO, GROUP):
        field_spectrum(at, GROUP)
    def filter_grads(first, last):
        def one_tile(tile, carry):
            at = pl.multiple_of(tile * 8, 8)
            for half in range(0, SPEC, LAT):
                totals = [None] * TAPS
                for col in range(0, LON, 8):
                    grads = gw[col : col + 8, pl.ds(at, 8), half : half + LAT]
                    for a in range(TAPS):
                        field = xh[col + a : col + a + 8, pl.ds(at, 8), half : half + LAT]
                        part = jnp.sum(grads * field, axis=0)
                        totals[a] = part if totals[a] is None else totals[a] + part
                for a in range(TAPS):
                    dkf[pl.ds(at, 8), a * SPEC + half : a * SPEC + half + LAT] = totals[a]
            return carry

        lax.fori_loop(first, last, one_tile, 0, unroll=2)

    in_groups(0, 2, forward_group)
    cells = slice(0, LON * LAT // 2)
    acc_out[...] = matmul_nt(cot_all[:, cells], hid_all[:, cells])
    acc_in[...] = matmul_nt(norm_all[:, cells], gp_all[:, cells])
    if remote:
        g_right, g_left = halo_copies(ga, 2)
        x_left.wait()
    else:
        local_halo(xa)
    field_spectrum(LON + HALO, HALO)
    forward_group(LON - GROUP)
    backward_mlp(LON - GROUP)
    if remote:
        g_right.start()
        x_right.wait()
    field_spectrum(0, HALO)
    forward_group(0)

    cells = slice(LON * LAT // 2, LON * LAT)
    acc_out[...] += matmul_nt(cot_all[:, cells], hid_all[:, cells])
    acc_in[...] += matmul_nt(norm_all[:, cells], gp_all[:, cells])
    wide = HID // 2
    for o in range(16):
        at = OWN * o
        stage[o, 0:12, 0:HID] = acc_in[at : at + 12, :]
        stage[o, 12:16, 0:HID] = acc_out[at : at + 4, :]
        stage[o, 0:8, HID:PACKED] = acc_out[at + 4 : at + 12, 0:wide]
        stage[o, 8:16, HID:PACKED] = acc_out[at + 4 : at + 12, wide:HID]
    for o in range(16):
        wsend[o % 2, o // 2] = stage[o].astype(BF)

    if remote:

        def to_slabs(slab, base):
            return [
                copy(slab.at[lon], slab.at[lon], base + d, {"lon": other})
                for d, other in enumerate(slabs)
            ]

        def to_owners(source, target, base):
            return [
                copy(source.at[other], target.at[d], base + d, {"sample": 2 * other + core})
                for d, other in enumerate(owners)
            ]

        def w_core():
            return [copy(wsend.at[1 - core], wcore, 4, partner)]

        def w_own():
            return to_owners(wmid, wparts, 5)

        def w_all():
            return to_slabs(wslab, 12)

        def k_core():
            return [copy(ksend.at[1 - core], kcore, 19, partner)]

        def k_own():
            return to_owners(kmid, kparts, 20)

        def k_all():
            return to_slabs(kslab, 27)

        start(w_core())
    backward_mlp(0)
    if remote:
        g_left.start()
    in_groups(0, 1, backward_mlp)
    if remote:
        wait(w_core())
        wmid[...] = (wsend[core].astype(F32) + wcore[...].astype(F32)).astype(BF)
        start(w_own())
    in_groups(1, 2, backward_mlp)
    filter_grads(0, C // 8)

    lanes = lax.broadcasted_iota(jnp.int32, (C, LAT), 1)
    total = jnp.where(lanes == TAPS * TAPS, jnp.sum(acc_gain[...], axis=1, keepdims=True), 0.0)
    for a in range(TAPS):
        part = dkf[:, a * SPEC : (a + 1) * SPEC]
        high = part.astype(BF)
        low = (part - high.astype(F32)).astype(BF)
        both = matmul(high, gather[...])
        found = both[:, 0:LAT] + both[:, LAT:] + matmul(low, gather[:, 0:LAT])
        total = total + (pltpu.roll(found, a * TAPS, axis=1) if a else found)
    dks[0, 0:C, :] = total
    dks[1, 0:C, :] = pltpu.roll(total, LAT // 2, axis=1)
    for side in range(2):
        dks[side, C : C + 16, :] = jnp.zeros((16, LAT), F32)
    for o in range(16):
        at = OWN * o
        ksend[o % 2, o // 2] = dks[0, at : at + 8, :] + dks[1, at + 6 : at + 14, :]
    if remote:
        start(k_core())
    in_groups(0, 2, finish_state)
    if remote:
        wait(k_core())
        kmid[...] = ksend[core] + kcore[...]
        start(k_own())
    in_groups(2, 4, finish_state)
    sout_buf[...] = x32[...].reshape(C, LON, LAT).astype(BF)
    leave = [
        pltpu.make_async_copy(sout_buf, sout_ref, near.at[9]),
        pltpu.make_async_copy(gin_buf, gin_ref, near.at[10]),
    ]
    leave[0].start()

    def backward_group(col):
        moved = filtered(gh, col, True, back_b)
        mask = masks(col)
        for k in range(GROUP):
            at = pl.ds(col + k, C, stride=LON)
            c32[at, :] = c32[at, :] * mask[k] + moved[k]

    in_groups(0, 1, backward_group)
    if remote:
        wait(w_own())
        held = wmid[owner].astype(F32)
        for d in range(len(owners)):
            held = held + wparts[d].astype(F32)
        wslab[lon] = held.astype(BF)
        start(w_all())
    in_groups(1, 2, backward_group)
    if remote:
        g_right.wait()
    else:
        local_halo(ga)
    grad_spectrum(0, HALO)
    backward_group(0)
    if remote:
        wait(k_own())
        held = kmid[owner]
        for d in range(len(owners)):
            held = held + kparts[d]
        kslab[lon] = held
        start(k_all())
        g_left.wait()
    grad_spectrum(LON + HALO, HALO)
    backward_group(LON - GROUP)
    gin_buf[...] = c32[...].reshape(C, LON, LAT).astype(BF)
    leave[1].start()
    if remote:
        wait(w_all())
        weights = wslab[0].astype(F32)
        for other in range(1, n_lon):
            weights = weights + wslab[other].astype(F32)
        wait(k_all())
        small = kslab[0]
        for other in range(1, n_lon):
            small = small + kslab[other]
    else:
        weights = wsend[0, 0].astype(F32)
        small = ksend[0, 0]
    weights = weights * factor
    small = small * factor
    gwin_ref[...] = weights[0:12, 0:HID]
    gwout_ref[0:4, :] = weights[12:16, 0:HID]
    gwout_ref[4:12, 0:wide] = weights[0:8, HID:PACKED]
    gwout_ref[4:12, wide:HID] = weights[8:16, HID:PACKED]
    kout[0:6, :] = small[0:6, :]
    kout[6:12, :] = pltpu.roll(small, LAT // 2, axis=1)[0:6, :]
    small_t = kout[...].T
    for a in range(TAPS):
        gk_ref[a] = small_t[a * TAPS : (a + 1) * TAPS, 0:OWN]
    gg_ref[...] = small_t[TAPS * TAPS : TAPS * TAPS + 1, 0:OWN]
    for one in leave:
        one.wait()


def deliver(*refs):
    count = len(refs) // 3
    sems = refs[-1]
    sources, targets, held = refs[:count], refs[count : 2 * count], refs[2 * count : 3 * count]
    arrive = [pltpu.make_async_copy(sources[k], held[k], sems.at[0, k]) for k in range(count)]
    leave = [pltpu.make_async_copy(held[k], targets[k], sems.at[1, k]) for k in range(count)]
    for one in arrive:
        one.start()
    for k in range(count):
        arrive[k].wait()
        leave[k].start()
    for one in leave:
        one.wait()


def block(n_lon, n_sample, factor, state, cot, sea, taps, gain, win, wout):
    vmem = pl.BlockSpec(memory_space=pltpu.VMEM)
    far = pl.BlockSpec(memory_space=pltpu.HBM)
    shape = jax.ShapeDtypeStruct
    outs = (
        shape((C, LON, LAT), BF),
        shape((C, LON, LAT), BF),
        shape((OWN, HID), F32),
        shape((OWN, HID), F32),
        shape((TAPS, TAPS, OWN), F32),
        shape((1, OWN), F32),
    )
    scratch = [
        pltpu.VMEM((C, LON, LAT), BF),
        pltpu.VMEM((C, LON, LAT), BF),
        pltpu.VMEM((C, HID), BF),
        pltpu.VMEM((C, HID), BF),
        pltpu.VMEM((3 * 64, TAPS * SPEC), BF),
        pltpu.VMEM((2 * LAT, SPEC), BF),
        pltpu.VMEM((SPEC, 2 * LAT), BF),
        pltpu.VMEM((2 * LAT, 2 * SPEC), BF),
        pltpu.VMEM((SPEC, 2 * LAT), BF),
        pltpu.VMEM((SPEC, 2 * LAT), BF),
        pltpu.VMEM((C * LON, LAT), F32),
        pltpu.VMEM((C * LON, LAT), F32),
        pltpu.VMEM((LON + 2 * HALO, C, LAT), BF),
        pltpu.VMEM((LON + 2 * HALO, C, LAT), BF),
        pltpu.VMEM((LON + 2 * HALO, C, SPEC), F32),
        pltpu.VMEM((LON + 2 * HALO, C, SPEC), F32),
        pltpu.VMEM((LON, C, SPEC), F32),
        pltpu.VMEM((C, TAPS * SPEC), F32),
        pltpu.VMEM((C, TAPS * SPEC), F32),
        pltpu.VMEM((LAT, 2 * LAT), F32),
        pltpu.VMEM((GROUP, C, SPEC), BF),
        pltpu.VMEM((GROUP, C, SPEC), BF),
        pltpu.VMEM((C, LAT), F32),
        pltpu.VMEM((HID, C), BF),
        pltpu.VMEM((HID, C), BF),
        pltpu.VMEM((C, LON * LAT), BF),
        pltpu.VMEM((C, LON * LAT), BF),
        pltpu.VMEM((HID, LON * LAT), BF),
        pltpu.VMEM((HID, LON * LAT), BF),
        pltpu.VMEM((LON, C, LAT), F32),
        pltpu.VMEM((LON, LAT), F32),
        pltpu.VMEM((C, HID), F32),
        pltpu.VMEM((C, HID), F32),
        pltpu.VMEM((C, LAT), F32),
        pltpu.VMEM((2, C + 16, LAT), F32),
        pltpu.VMEM((16, 16, PACKED), F32),
        pltpu.VMEM((2, 8, 16, PACKED), BF),
        pltpu.VMEM((8, 16, PACKED), BF),
        pltpu.VMEM((8, 16, PACKED), BF),
        pltpu.VMEM((7, 16, PACKED), BF),
        pltpu.VMEM((8, 16, PACKED), BF),
        pltpu.VMEM((2, 8, 8, LAT), F32),
        pltpu.VMEM((8, 8, LAT), F32),
        pltpu.VMEM((8, 8, LAT), F32),
        pltpu.VMEM((7, 8, LAT), F32),
        pltpu.VMEM((8, 8, LAT), F32),
        pltpu.VMEM((16, LAT), F32),
        pltpu.VMEM((C, LON, LAT), BF),
        pltpu.VMEM((C, LON, LAT), BF),
        pltpu.SemaphoreType.DMA((34,)),
        pltpu.SemaphoreType.DMA((34,)),
        pltpu.SemaphoreType.DMA((12,)),
    ]
    extra = dict(collective_id=0, has_side_effects=True) if n_lon > 1 else {}
    results = pl.pallas_call(
        functools.partial(kernel_body, n_lon, n_sample, factor),
        out_shape=outs,
        in_specs=[vmem] * 3 + [far] * 10,
        out_specs=(far, far) + (vmem,) * 4,
        scratch_shapes=scratch,
        compiler_params=pltpu.CompilerParams(vmem_limit_bytes=62 * 1024 * 1024, **extra),
    )(
        sea,
        taps.transpose(1, 2, 0),
        gain.reshape(1, C),
        state.reshape(C, LON, LAT),
        cot.reshape(C, LON, LAT),
        win,
        wout.T,
        *spectral_constants(),
    )
    anywhere = pl.BlockSpec(memory_space=pl.ANY)
    return pl.pallas_call(
        deliver,
        out_shape=outs,
        in_specs=[anywhere] * 6,
        out_specs=(anywhere,) * 6,
        scratch_shapes=[pltpu.VMEM(out.shape, out.dtype) for out in outs]
        + [pltpu.SemaphoreType.DMA((2, 6))],
    )(*results)


def solution(mesh):
    n_lon, n_sample = mesh.shape["lon"], mesh.shape["sample"]
    factor = 1.0 / math.sqrt(n_sample * n_lon * LON * LAT)

    def on_device(state, cot, sea, taps, gain, win, wout):
        out = block(n_lon, n_sample, factor, state, cot, sea, taps, gain, win, wout)
        shape = state.shape
        return (
            out[0].reshape(shape),
            out[1].reshape(shape),
            out[2],
            out[3].T,
            out[4].transpose(2, 0, 1),
            out[5].reshape(OWN),
        )

    slab = P("sample", None, "lon", None)
    return jax.shard_map(
        on_device,
        mesh=mesh,
        in_specs=(slab, slab, P("lon", None), P(), P(), P(), P()),
        out_specs=(
            slab,
            slab,
            P("sample", None),
            P(None, "sample"),
            P("sample", None, None),
            P("sample"),
        ),
        check_vma=False,
    )
```

```python
import functools
import math

import jax
import jax.numpy as jnp
import numpy as np
from jax import lax
from jax.experimental import pallas as pl
from jax.experimental.pallas import tpu as pltpu
from jax.sharding import PartitionSpec as P

C = 192
HID = 768
LON = 16
LAT = 128
PERIOD = 131
SPEC = 256
TAPS = 7
HALO = 3
GROUP = 4
HID_BLOCK = 256
CELL_BLOCK = 256
TILE = 16
OWN = 12
PACKED = 1152
BF = jnp.bfloat16
F32 = jnp.float32
MESH = pl.DeviceIdType.MESH


def tree_sum(terms):
    while len(terms) > 1:
        paired = [terms[k] + terms[k + 1] for k in range(0, len(terms) - 1, 2)]
        if len(terms) % 2:
            paired.append(terms[-1])
        terms = paired
    return terms[0]


def matmul(left, right):
    return jnp.dot(left, right, preferred_element_type=F32)


def matmul_nt(left, right):
    return lax.dot_general(left, right, (((1,), (1,)), ((), ())), preferred_element_type=F32)


def split_constant(values):
    high = values.astype(BF)
    low = (values - high.astype(np.float64)).astype(BF)
    return high, low


def spectral_constants():
    angle = 2.0 * math.pi / PERIOD
    row = np.arange(LAT)
    field_f, field_b = np.zeros((LAT, SPEC)), np.zeros((LAT, SPEC))
    back_f, back_b = np.zeros((SPEC, LAT)), np.zeros((SPEC, LAT))
    taps = np.zeros((8, SPEC))
    shift = np.arange(TAPS) - HALO
    field_f[:, 0] = field_b[:, 0] = 1.0
    back_f[0] = back_b[0] = 1.0 / PERIOD
    taps[:TAPS, 0] = 1.0
    half = PERIOD // 2
    for f in range(1, half + 1):
        one, two, three = f, half + f, 2 * half + f
        cos, sin = np.cos(angle * f * row), np.sin(angle * f * row)
        c, d = np.cos(angle * f * shift), np.sin(angle * f * shift)
        taps[:TAPS, one], taps[:TAPS, two], taps[:TAPS, three] = c, d - c, c + d
        field_f[:, one], field_f[:, two], field_f[:, three] = cos - sin, cos, -sin
        field_b[:, one], field_b[:, two], field_b[:, three] = cos + sin, cos, sin
        scale = 2.0 / PERIOD
        back_f[one], back_f[two], back_f[three] = scale * (cos - sin), -scale * sin, -scale * cos
        back_b[one], back_b[two], back_b[three] = scale * (cos + sin), scale * sin, -scale * cos

    def stacked(values):
        return np.concatenate(split_constant(values), axis=0)

    def beside(values):
        return np.concatenate(split_constant(values), axis=1)

    spread_high, spread_low = np.zeros((64, TAPS * SPEC)), np.zeros((64, TAPS * SPEC))
    high, low = split_constant(taps)
    for a in range(TAPS):
        spread_high[8 * a : 8 * a + 8, a * SPEC : (a + 1) * SPEC] = high
        spread_low[8 * a : 8 * a + 8, a * SPEC : (a + 1) * SPEC] = low
    spread = np.concatenate([spread_high, spread_high, spread_low]).astype(BF)
    gather = np.zeros((SPEC, LAT))
    gather[:, :8] = taps.T
    return (
        spread,
        stacked(field_f),
        beside(back_f),
        np.concatenate([stacked(back_f.T), stacked(field_b)], axis=1),
        beside(back_b),
        beside(gather),
    )


def column(ref, at):
    return ref[pl.ds(at, C, stride=LON), :]


def kernel_body(
    n_lon,
    n_sample,
    factor,
    sea_ref,
    taps_ref,
    gain_ref,
    state_far,
    cot_far,
    win_far,
    wout_far,
    spread_far,
    field_f_far,
    back_f_far,
    field_g_far,
    back_b_far,
    gather_far,
    sout_ref,
    gin_ref,
    gwin_ref,
    gwout_ref,
    gk_ref,
    gg_ref,
    state_ref,
    cot_ref,
    win_ref,
    wout_t,
    spread,
    field_f,
    back_f,
    field_g,
    back_b,
    gather,
    x32,
    c32,
    xa,
    ga,
    xh,
    gh,
    gw,
    kf,
    dkf,
    flat_taps,
    sum_high,
    sum_low,
    gainb,
    win_t,
    wout,
    norm_all,
    cot_all,
    hid_all,
    gp_all,
    scaled_all,
    inv_all,
    acc_in,
    acc_out,
    acc_gain,
    dks,
    stage,
    wsend,
    wcore,
    wmid,
    wparts,
    wslab,
    ksend,
    kcore,
    kmid,
    kparts,
    kslab,
    kout,
    sout_buf,
    gin_buf,
    send,
    recv,
    near,
):
    fetches = [
        pltpu.make_async_copy(far, here, near.at[k])
        for k, (far, here) in enumerate(
            (
                (spread_far, spread),
                (field_f_far, field_f),
                (back_f_far, back_f),
                (win_far, win_ref),
                (wout_far, wout_t),
                (cot_far, cot_ref),
                (field_g_far, field_g),
                (back_b_far, back_b),
                (gather_far, gather),
            )
        )
    ]
    remote = n_lon > 1
    if remote:
        lon = lax.axis_index("lon")
        sample = lax.axis_index("sample")
        core = lax.rem(sample, 2)
        owner = sample // 2
        n_own = n_sample // 2
        partner = {"sample": sample + 1 - 2 * core}
        right = {"lon": lax.rem(lon + 1, n_lon)}
        left = {"lon": lax.rem(lon + n_lon - 1, n_lon)}
        owners = [lax.rem(owner + d, n_own) for d in range(1, n_own)]
        slabs = [lax.rem(lon + d, n_lon) for d in range(1, n_lon)]
        peers = (
            [partner]
            + [{"sample": 2 * other + core} for other in owners]
            + [{"lon": other} for other in slabs]
        )
        barrier = pltpu.get_barrier_semaphore()
        for peer in peers:
            pl.semaphore_signal(barrier, inc=1, device_id=peer, device_id_type=MESH)

        def copy(src, dst, slot, peer):
            return pltpu.make_async_remote_copy(
                src_ref=src,
                dst_ref=dst,
                send_sem=send.at[slot],
                recv_sem=recv.at[slot],
                device_id=peer,
                device_id_type=MESH,
            )

    def halo_copies(ref, slot):
        return (
            copy(ref.at[pl.ds(LON, HALO)], ref.at[pl.ds(0, HALO)], slot, right),
            copy(ref.at[pl.ds(HALO, HALO)], ref.at[pl.ds(LON + HALO, HALO)], slot + 1, left),
        )

    def local_halo(ref):
        ref[0:HALO] = ref[LON : LON + HALO]
        ref[LON + HALO : LON + 2 * HALO] = ref[HALO : 2 * HALO]

    arrive = pltpu.make_async_copy(state_far, state_ref, near.at[11])
    arrive.start()
    for fetch in fetches:
        fetch.start()
    arrive.wait()
    x32[...] = state_ref[...].astype(F32).reshape(C * LON, LAT)
    for i in (0, 1, 2, 13, 14, 15):
        xa[HALO + i] = column(x32, i).astype(BF)
    if remote:
        pl.semaphore_wait(barrier, len(peers))
        x_right, x_left = halo_copies(xa, 0)
        x_left.start()
        x_right.start()
    for i in range(3, 13):
        xa[HALO + i] = column(x32, i).astype(BF)
    for fetch in fetches:
        fetch.wait()
    c32[...] = cot_ref[...].astype(F32).reshape(C * LON, LAT)

    flat_taps[...] = jnp.zeros_like(flat_taps)
    for a in range(TAPS):
        flat_taps[8 * a : 8 * a + TAPS, 0:C] = taps_ref[a]
    rest = flat_taps[...].T[0:C, :]
    high = rest.astype(BF)
    low = (rest - high.astype(F32)).astype(BF)
    kf[...] = matmul(
        jnp.concatenate([high[:, 0:64], low[:, 0:64], high[:, 0:64]], axis=1), spread[...]
    )
    gainb[...] = jnp.broadcast_to(gain_ref[...], (LAT, C)).T
    win_t[...] = (0.5 * win_ref[...].astype(F32)).astype(BF).T
    wout[...] = (0.5 * wout_t[...].astype(F32)).astype(BF).T
    acc_gain[...] = jnp.zeros_like(acc_gain)

    def doubled(columns):
        flat = columns.reshape(-1, LAT)
        return jnp.concatenate([flat, flat], axis=1)

    def field_spectrum(at, count):
        spectrum = matmul(doubled(xa[at : at + count]), field_f[...])
        xh[at : at + count] = spectrum.reshape(count, C, SPEC)

    def grad_spectrum(at, count):
        spectrum = matmul(doubled(ga[at : at + count]), field_g[:, SPEC:])
        gh[at : at + count] = spectrum.reshape(count, C, SPEC)

    def filtered(field, col, flip, inverse):
        def one_tile(tile, carry):
            at = pl.multiple_of(tile * TILE, TILE)
            for half in range(0, SPEC, LAT):
                window = field[pl.ds(col, GROUP + 2 * HALO), pl.ds(at, TILE), half : half + LAT]
                terms = []
                for a in range(TAPS):
                    first = 2 * HALO - a if flip else a
                    lane = a * SPEC + half
                    weight = kf[pl.ds(at, TILE), lane : lane + LAT]
                    terms.append(weight[None] * window[first : first + GROUP])
                total = tree_sum(terms)
                high = total.astype(BF)
                sum_high[:, pl.ds(at, TILE), half : half + LAT] = high
                sum_low[:, pl.ds(at, TILE), half : half + LAT] = (
                    total - high.astype(F32)
                ).astype(BF)
            return carry

        lax.fori_loop(0, C // TILE, one_tile, 0, unroll=2)
        main = matmul(sum_high[...].reshape(GROUP * C, SPEC), inverse[...])
        rest = matmul(sum_low[...].reshape(GROUP * C, SPEC), inverse[:, 0:LAT])
        return (main[:, 0:LAT] + main[:, LAT:] + rest).reshape(GROUP, C, LAT)

    def masks(col):
        return [sea_ref[pl.ds(col + k, 1), :].astype(F32) for k in range(GROUP)]

    def side_by_side(parts):
        return jnp.concatenate([parts[k] for k in range(GROUP)], axis=1)

    def first_cell(col):
        turned = col + LON - GROUP
        return (turned % LON if isinstance(col, int) else lax.rem(turned, LON)) * LAT

    def lanes_of(col):
        return pl.ds(pl.multiple_of(first_cell(col), GROUP * LAT), GROUP * LAT)

    def forward_group(col):
        mixed = filtered(xh, col, False, back_f)
        centred = mixed - jnp.mean(mixed, axis=1, keepdims=True)
        variance = jnp.mean(centred * centred, axis=1, keepdims=True)
        inv_scale = lax.rsqrt(variance + 1e-06)
        scaled = centred * inv_scale
        scaled_all[pl.ds(col, GROUP)] = scaled
        inv_all[pl.ds(col, GROUP), :] = inv_scale.reshape(GROUP, LAT)
        normed = side_by_side((scaled * gainb[...][None]).astype(BF))
        mask = masks(col)
        grad_out = side_by_side([(column(c32, col + k) * mask[k]).astype(BF) for k in range(GROUP)])
        where = lanes_of(col)
        norm_all[:, where] = normed
        cot_all[:, where] = grad_out
        for h in range(0, HID, HID_BLOCK):
            for n in range(0, GROUP * LAT, CELL_BLOCK):
                half = matmul(win_t[h : h + HID_BLOCK, :], normed[:, n : n + CELL_BLOCK])
                grad_half = matmul(wout[h : h + HID_BLOCK, :], grad_out[:, n : n + CELL_BLOCK])
                square = half * half
                bent = jnp.tanh(half * (1.5957691216057308 + 0.28541926509040104 * square))
                gate = 1.0 + bent
                hidden = half * gate
                slope = gate + hidden * (1.0 - bent) * (
                    1.5957691216057308 + 0.8562577952712031 * square
                )
                at = pl.ds(pl.multiple_of(first_cell(col) + n, CELL_BLOCK), CELL_BLOCK)
                hid_all[h : h + HID_BLOCK, at] = hidden.astype(BF)
                gp_all[h : h + HID_BLOCK, at] = (grad_half * slope).astype(BF)

    def finish_state(col):
        mask = masks(col)
        branch = matmul(wout_t[...], hid_all[:, lanes_of(col)])
        for k in range(GROUP):
            lane = slice(k * LAT, (k + 1) * LAT)
            at = pl.ds(col + k, C, stride=LON)
            x32[at, :] = mask[k] * (x32[at, :] + branch[:, lane])

    def backward_mlp(col):
        where = lanes_of(col)
        gain = gainb[...]
        grad_normed = matmul(win_ref[...], gp_all[:, where])
        for k in range(GROUP):
            lane = slice(k * LAT, (k + 1) * LAT)
            scaled = scaled_all[col + k]
            grad = grad_normed[:, lane]
            product = grad * scaled
            acc_gain[...] += product
            grad_scaled = grad * gain
            first = jnp.mean(grad_scaled, axis=0, keepdims=True)
            second = jnp.mean(product * gain, axis=0, keepdims=True)
            inv_scale = inv_all[pl.ds(col + k, 1), :]
            grad_conv = (inv_scale * (grad_scaled - first - scaled * second)).astype(BF)
            ga[HALO + col + k] = grad_conv
            spectrum = matmul(doubled(grad_conv), field_g[...])
            gw[col + k] = spectrum[:, 0:SPEC]
            gh[HALO + col + k] = spectrum[:, SPEC:]

    def in_groups(first, last, work):
        def one_group(step, carry):
            work(lax.rem(GROUP + step * GROUP, LON))
            return carry

        lax.fori_loop(first, last, one_group, 0)

    def start(copies):
        for one in copies:
            one.start()

    def wait(copies):
        for one in copies:
            one.wait()

    for at in range(HALO, LON + HALO, GROUP):
        field_spectrum(at, GROUP)
    def filter_grads(first, last):
        def one_tile(tile, carry):
            at = pl.multiple_of(tile * 8, 8)
            for half in range(0, SPEC, LAT):
                totals = [None] * TAPS
                for col in range(0, LON, 8):
                    grads = gw[col : col + 8, pl.ds(at, 8), half : half + LAT]
                    for a in range(TAPS):
                        field = xh[col + a : col + a + 8, pl.ds(at, 8), half : half + LAT]
                        part = jnp.sum(grads * field, axis=0)
                        totals[a] = part if totals[a] is None else totals[a] + part
                for a in range(TAPS):
                    dkf[pl.ds(at, 8), a * SPEC + half : a * SPEC + half + LAT] = totals[a]
            return carry

        lax.fori_loop(first, last, one_tile, 0, unroll=2)

    in_groups(0, 2, forward_group)
    cells = slice(0, LON * LAT // 2)
    acc_out[...] = matmul_nt(cot_all[:, cells], hid_all[:, cells])
    acc_in[...] = matmul_nt(norm_all[:, cells], gp_all[:, cells])
    if remote:
        g_right, g_left = halo_copies(ga, 2)
        x_left.wait()
    else:
        local_halo(xa)
    field_spectrum(LON + HALO, HALO)
    forward_group(LON - GROUP)
    backward_mlp(LON - GROUP)
    if remote:
        g_right.start()
        x_right.wait()
    field_spectrum(0, HALO)
    forward_group(0)

    cells = slice(LON * LAT // 2, LON * LAT)
    acc_out[...] += matmul_nt(cot_all[:, cells], hid_all[:, cells])
    acc_in[...] += matmul_nt(norm_all[:, cells], gp_all[:, cells])
    wide = HID // 2
    for o in range(16):
        at = OWN * o
        stage[o, 0:12, 0:HID] = acc_in[at : at + 12, :]
        stage[o, 12:16, 0:HID] = acc_out[at : at + 4, :]
        stage[o, 0:8, HID:PACKED] = acc_out[at + 4 : at + 12, 0:wide]
        stage[o, 8:16, HID:PACKED] = acc_out[at + 4 : at + 12, wide:HID]
    for o in range(16):
        wsend[o % 2, o // 2] = stage[o].astype(BF)

    if remote:

        def to_slabs(slab, base):
            return [
                copy(slab.at[lon], slab.at[lon], base + d, {"lon": other})
                for d, other in enumerate(slabs)
            ]

        def to_owners(source, target, base):
            return [
                copy(source.at[other], target.at[d], base + d, {"sample": 2 * other + core})
                for d, other in enumerate(owners)
            ]

        def w_core():
            return [copy(wsend.at[1 - core], wcore, 4, partner)]

        def w_own():
            return to_owners(wmid, wparts, 5)

        def w_all():
            return to_slabs(wslab, 12)

        def k_core():
            return [copy(ksend.at[1 - core], kcore, 19, partner)]

        def k_own():
            return to_owners(kmid, kparts, 20)

        def k_all():
            return to_slabs(kslab, 27)

        start(w_core())
    backward_mlp(0)
    in_groups(0, 1, backward_mlp)
    if remote:
        wait(w_core())
        wmid[...] = (wsend[core].astype(F32) + wcore[...].astype(F32)).astype(BF)
        start(w_own())
        g_left.start()
    in_groups(1, 2, backward_mlp)
    filter_grads(0, C // 8)

    lanes = lax.broadcasted_iota(jnp.int32, (C, LAT), 1)
    total = jnp.where(lanes == TAPS * TAPS, jnp.sum(acc_gain[...], axis=1, keepdims=True), 0.0)
    for a in range(TAPS):
        part = dkf[:, a * SPEC : (a + 1) * SPEC]
        high = part.astype(BF)
        low = (part - high.astype(F32)).astype(BF)
        both = matmul(high, gather[...])
        found = both[:, 0:LAT] + both[:, LAT:] + matmul(low, gather[:, 0:LAT])
        total = total + (pltpu.roll(found, a * TAPS, axis=1) if a else found)
    dks[0, 0:C, :] = total
    dks[1, 0:C, :] = pltpu.roll(total, LAT // 2, axis=1)
    for side in range(2):
        dks[side, C : C + 16, :] = jnp.zeros((16, LAT), F32)
    for o in range(16):
        at = OWN * o
        ksend[o % 2, o // 2] = dks[0, at : at + 8, :] + dks[1, at + 6 : at + 14, :]
    if remote:
        start(k_core())
    in_groups(0, 2, finish_state)
    if remote:
        wait(k_core())
        kmid[...] = ksend[core] + kcore[...]
        start(k_own())
    in_groups(2, 4, finish_state)
    sout_buf[...] = x32[...].reshape(C, LON, LAT).astype(BF)
    leave = [
        pltpu.make_async_copy(sout_buf, sout_ref, near.at[9]),
        pltpu.make_async_copy(gin_buf, gin_ref, near.at[10]),
    ]
    leave[0].start()

    def backward_group(col):
        moved = filtered(gh, col, True, back_b)
        mask = masks(col)
        for k in range(GROUP):
            at = pl.ds(col + k, C, stride=LON)
            c32[at, :] = c32[at, :] * mask[k] + moved[k]

    in_groups(0, 1, backward_group)
    if remote:
        wait(w_own())
        held = wmid[owner].astype(F32)
        for d in range(len(owners)):
            held = held + wparts[d].astype(F32)
        wslab[lon] = held.astype(BF)
        start(w_all())
    in_groups(1, 2, backward_group)
    if remote:
        g_right.wait()
    else:
        local_halo(ga)
    grad_spectrum(0, HALO)
    backward_group(0)
    if remote:
        wait(k_own())
        held = kmid[owner]
        for d in range(len(owners)):
            held = held + kparts[d]
        kslab[lon] = held
        start(k_all())
        g_left.wait()
    grad_spectrum(LON + HALO, HALO)
    backward_group(LON - GROUP)
    gin_buf[...] = c32[...].reshape(C, LON, LAT).astype(BF)
    leave[1].start()
    if remote:
        wait(w_all())
        weights = wslab[0].astype(F32)
        for other in range(1, n_lon):
            weights = weights + wslab[other].astype(F32)
        wait(k_all())
        small = kslab[0]
        for other in range(1, n_lon):
            small = small + kslab[other]
    else:
        weights = wsend[0, 0].astype(F32)
        small = ksend[0, 0]
    weights = weights * factor
    small = small * factor
    gwin_ref[...] = weights[0:12, 0:HID]
    gwout_ref[0:4, :] = weights[12:16, 0:HID]
    gwout_ref[4:12, 0:wide] = weights[0:8, HID:PACKED]
    gwout_ref[4:12, wide:HID] = weights[8:16, HID:PACKED]
    kout[0:6, :] = small[0:6, :]
    kout[6:12, :] = pltpu.roll(small, LAT // 2, axis=1)[0:6, :]
    small_t = kout[...].T
    for a in range(TAPS):
        gk_ref[a] = small_t[a * TAPS : (a + 1) * TAPS, 0:OWN]
    gg_ref[...] = small_t[TAPS * TAPS : TAPS * TAPS + 1, 0:OWN]
    for one in leave:
        one.wait()


def deliver(*refs):
    count = len(refs) // 3
    sems = refs[-1]
    sources, targets, held = refs[:count], refs[count : 2 * count], refs[2 * count : 3 * count]
    arrive = [pltpu.make_async_copy(sources[k], held[k], sems.at[0, k]) for k in range(count)]
    leave = [pltpu.make_async_copy(held[k], targets[k], sems.at[1, k]) for k in range(count)]
    for one in arrive:
        one.start()
    for k in range(count):
        arrive[k].wait()
        leave[k].start()
    for one in leave:
        one.wait()


def block(n_lon, n_sample, factor, state, cot, sea, taps, gain, win, wout):
    vmem = pl.BlockSpec(memory_space=pltpu.VMEM)
    far = pl.BlockSpec(memory_space=pltpu.HBM)
    shape = jax.ShapeDtypeStruct
    outs = (
        shape((C, LON, LAT), BF),
        shape((C, LON, LAT), BF),
        shape((OWN, HID), F32),
        shape((OWN, HID), F32),
        shape((TAPS, TAPS, OWN), F32),
        shape((1, OWN), F32),
    )
    scratch = [
        pltpu.VMEM((C, LON, LAT), BF),
        pltpu.VMEM((C, LON, LAT), BF),
        pltpu.VMEM((C, HID), BF),
        pltpu.VMEM((C, HID), BF),
        pltpu.VMEM((3 * 64, TAPS * SPEC), BF),
        pltpu.VMEM((2 * LAT, SPEC), BF),
        pltpu.VMEM((SPEC, 2 * LAT), BF),
        pltpu.VMEM((2 * LAT, 2 * SPEC), BF),
        pltpu.VMEM((SPEC, 2 * LAT), BF),
        pltpu.VMEM((SPEC, 2 * LAT), BF),
        pltpu.VMEM((C * LON, LAT), F32),
        pltpu.VMEM((C * LON, LAT), F32),
        pltpu.VMEM((LON + 2 * HALO, C, LAT), BF),
        pltpu.VMEM((LON + 2 * HALO, C, LAT), BF),
        pltpu.VMEM((LON + 2 * HALO, C, SPEC), F32),
        pltpu.VMEM((LON + 2 * HALO, C, SPEC), F32),
        pltpu.VMEM((LON, C, SPEC), F32),
        pltpu.VMEM((C, TAPS * SPEC), F32),
        pltpu.VMEM((C, TAPS * SPEC), F32),
        pltpu.VMEM((LAT, 2 * LAT), F32),
        pltpu.VMEM((GROUP, C, SPEC), BF),
        pltpu.VMEM((GROUP, C, SPEC), BF),
        pltpu.VMEM((C, LAT), F32),
        pltpu.VMEM((HID, C), BF),
        pltpu.VMEM((HID, C), BF),
        pltpu.VMEM((C, LON * LAT), BF),
        pltpu.VMEM((C, LON * LAT), BF),
        pltpu.VMEM((HID, LON * LAT), BF),
        pltpu.VMEM((HID, LON * LAT), BF),
        pltpu.VMEM((LON, C, LAT), F32),
        pltpu.VMEM((LON, LAT), F32),
        pltpu.VMEM((C, HID), F32),
        pltpu.VMEM((C, HID), F32),
        pltpu.VMEM((C, LAT), F32),
        pltpu.VMEM((2, C + 16, LAT), F32),
        pltpu.VMEM((16, 16, PACKED), F32),
        pltpu.VMEM((2, 8, 16, PACKED), BF),
        pltpu.VMEM((8, 16, PACKED), BF),
        pltpu.VMEM((8, 16, PACKED), BF),
        pltpu.VMEM((7, 16, PACKED), BF),
        pltpu.VMEM((8, 16, PACKED), BF),
        pltpu.VMEM((2, 8, 8, LAT), F32),
        pltpu.VMEM((8, 8, LAT), F32),
        pltpu.VMEM((8, 8, LAT), F32),
        pltpu.VMEM((7, 8, LAT), F32),
        pltpu.VMEM((8, 8, LAT), F32),
        pltpu.VMEM((16, LAT), F32),
        pltpu.VMEM((C, LON, LAT), BF),
        pltpu.VMEM((C, LON, LAT), BF),
        pltpu.SemaphoreType.DMA((34,)),
        pltpu.SemaphoreType.DMA((34,)),
        pltpu.SemaphoreType.DMA((12,)),
    ]
    extra = dict(collective_id=0, has_side_effects=True) if n_lon > 1 else {}
    results = pl.pallas_call(
        functools.partial(kernel_body, n_lon, n_sample, factor),
        out_shape=outs,
        in_specs=[vmem] * 3 + [far] * 10,
        out_specs=(far, far) + (vmem,) * 4,
        scratch_shapes=scratch,
        compiler_params=pltpu.CompilerParams(vmem_limit_bytes=62 * 1024 * 1024, **extra),
    )(
        sea,
        taps.transpose(1, 2, 0),
        gain.reshape(1, C),
        state.reshape(C, LON, LAT),
        cot.reshape(C, LON, LAT),
        win,
        wout.T,
        *spectral_constants(),
    )
    anywhere = pl.BlockSpec(memory_space=pl.ANY)
    return pl.pallas_call(
        deliver,
        out_shape=outs,
        in_specs=[anywhere] * 6,
        out_specs=(anywhere,) * 6,
        scratch_shapes=[pltpu.VMEM(out.shape, out.dtype) for out in outs]
        + [pltpu.SemaphoreType.DMA((2, 6))],
    )(*results)


def solution(mesh):
    n_lon, n_sample = mesh.shape["lon"], mesh.shape["sample"]
    factor = 1.0 / math.sqrt(n_sample * n_lon * LON * LAT)

    def on_device(state, cot, sea, taps, gain, win, wout):
        out = block(n_lon, n_sample, factor, state, cot, sea, taps, gain, win, wout)
        shape = state.shape
        return (
            out[0].reshape(shape),
            out[1].reshape(shape),
            out[2],
            out[3].T,
            out[4].transpose(2, 0, 1),
            out[5].reshape(OWN),
        )

    slab = P("sample", None, "lon", None)
    return jax.shard_map(
        on_device,
        mesh=mesh,
        in_specs=(slab, slab, P("lon", None), P(), P(), P(), P()),
        out_specs=(
            slab,
            slab,
            P("sample", None),
            P(None, "sample"),
            P("sample", None, None),
            P("sample"),
        ),
        check_vma=False,
    )
```

```python
import functools
import math

import jax
import jax.numpy as jnp
import numpy as np
from jax import lax
from jax.experimental import pallas as pl
from jax.experimental.pallas import tpu as pltpu
from jax.sharding import PartitionSpec as P

C = 192
HID = 768
LON = 16
LAT = 128
PERIOD = 131
SPEC = 256
TAPS = 7
HALO = 3
GROUP = 4
HID_BLOCK = 256
CELL_BLOCK = 256
TILE = 16
OWN = 12
PACKED = 1152
BF = jnp.bfloat16
F32 = jnp.float32
MESH = pl.DeviceIdType.MESH


def tree_sum(terms):
    while len(terms) > 1:
        paired = [terms[k] + terms[k + 1] for k in range(0, len(terms) - 1, 2)]
        if len(terms) % 2:
            paired.append(terms[-1])
        terms = paired
    return terms[0]


def matmul(left, right):
    return jnp.dot(left, right, preferred_element_type=F32)


def matmul_nt(left, right):
    return lax.dot_general(left, right, (((1,), (1,)), ((), ())), preferred_element_type=F32)


def split_constant(values):
    high = values.astype(BF)
    low = (values - high.astype(np.float64)).astype(BF)
    return high, low


def spectral_constants():
    angle = 2.0 * math.pi / PERIOD
    row = np.arange(LAT)
    field_f, field_b = np.zeros((LAT, SPEC)), np.zeros((LAT, SPEC))
    back_f, back_b = np.zeros((SPEC, LAT)), np.zeros((SPEC, LAT))
    taps = np.zeros((8, SPEC))
    shift = np.arange(TAPS) - HALO
    field_f[:, 0] = field_b[:, 0] = 1.0
    back_f[0] = back_b[0] = 1.0 / PERIOD
    taps[:TAPS, 0] = 1.0
    half = PERIOD // 2
    for f in range(1, half + 1):
        one, two, three = f, half + f, 2 * half + f
        cos, sin = np.cos(angle * f * row), np.sin(angle * f * row)
        c, d = np.cos(angle * f * shift), np.sin(angle * f * shift)
        taps[:TAPS, one], taps[:TAPS, two], taps[:TAPS, three] = c, d - c, c + d
        field_f[:, one], field_f[:, two], field_f[:, three] = cos - sin, cos, -sin
        field_b[:, one], field_b[:, two], field_b[:, three] = cos + sin, cos, sin
        scale = 2.0 / PERIOD
        back_f[one], back_f[two], back_f[three] = scale * (cos - sin), -scale * sin, -scale * cos
        back_b[one], back_b[two], back_b[three] = scale * (cos + sin), scale * sin, -scale * cos

    def stacked(values):
        return np.concatenate(split_constant(values), axis=0)

    def beside(values):
        return np.concatenate(split_constant(values), axis=1)

    spread_high, spread_low = np.zeros((64, TAPS * SPEC)), np.zeros((64, TAPS * SPEC))
    high, low = split_constant(taps)
    for a in range(TAPS):
        spread_high[8 * a : 8 * a + 8, a * SPEC : (a + 1) * SPEC] = high
        spread_low[8 * a : 8 * a + 8, a * SPEC : (a + 1) * SPEC] = low
    spread = np.concatenate([spread_high, spread_high, spread_low]).astype(BF)
    gather = np.zeros((SPEC, LAT))
    gather[:, :8] = taps.T
    return (
        spread,
        stacked(field_f),
        beside(back_f),
        np.concatenate([stacked(back_f.T), stacked(field_b)], axis=1),
        beside(back_b),
        beside(gather),
    )


def column(ref, at):
    return ref[pl.ds(at, C, stride=LON), :]


def kernel_body(
    n_lon,
    n_sample,
    factor,
    sea_ref,
    taps_ref,
    gain_ref,
    state_far,
    cot_far,
    win_far,
    wout_far,
    spread_far,
    field_f_far,
    back_f_far,
    field_g_far,
    back_b_far,
    gather_far,
    sout_ref,
    gin_ref,
    gwin_ref,
    gwout_ref,
    gk_ref,
    gg_ref,
    state_ref,
    cot_ref,
    win_ref,
    wout_t,
    spread,
    field_f,
    back_f,
    field_g,
    back_b,
    gather,
    x32,
    c32,
    xa,
    ga,
    xh,
    gh,
    gw,
    kf,
    dkf,
    flat_taps,
    sum_high,
    sum_low,
    gainb,
    win_t,
    wout,
    norm_all,
    cot_all,
    hid_all,
    gp_all,
    scaled_all,
    inv_all,
    acc_in,
    acc_out,
    acc_gain,
    dks,
    stage,
    wsend,
    wcore,
    wmid,
    wparts,
    wslab,
    ksend,
    kcore,
    kmid,
    kparts,
    kslab,
    kout,
    sout_buf,
    gin_buf,
    send,
    recv,
    near,
):
    fetches = [
        pltpu.make_async_copy(far, here, near.at[k])
        for k, (far, here) in enumerate(
            (
                (spread_far, spread),
                (field_f_far, field_f),
                (back_f_far, back_f),
                (win_far, win_ref),
                (wout_far, wout_t),
                (cot_far, cot_ref),
                (field_g_far, field_g),
                (back_b_far, back_b),
                (gather_far, gather),
            )
        )
    ]
    remote = n_lon > 1
    if remote:
        lon = lax.axis_index("lon")
        sample = lax.axis_index("sample")
        core = lax.rem(sample, 2)
        owner = sample // 2
        n_own = n_sample // 2
        partner = {"sample": sample + 1 - 2 * core}
        right = {"lon": lax.rem(lon + 1, n_lon)}
        left = {"lon": lax.rem(lon + n_lon - 1, n_lon)}
        owners = [lax.rem(owner + d, n_own) for d in range(1, n_own)]
        slabs = [lax.rem(lon + d, n_lon) for d in range(1, n_lon)]
        peers = (
            [partner]
            + [{"sample": 2 * other + core} for other in owners]
            + [{"lon": other} for other in slabs]
        )
        barrier = pltpu.get_barrier_semaphore()
        for peer in peers:
            pl.semaphore_signal(barrier, inc=1, device_id=peer, device_id_type=MESH)

        def copy(src, dst, slot, peer):
            return pltpu.make_async_remote_copy(
                src_ref=src,
                dst_ref=dst,
                send_sem=send.at[slot],
                recv_sem=recv.at[slot],
                device_id=peer,
                device_id_type=MESH,
            )

    def halo_copies(ref, slot):
        return (
            copy(ref.at[pl.ds(LON, HALO)], ref.at[pl.ds(0, HALO)], slot, right),
            copy(ref.at[pl.ds(HALO, HALO)], ref.at[pl.ds(LON + HALO, HALO)], slot + 1, left),
        )

    def local_halo(ref):
        ref[0:HALO] = ref[LON : LON + HALO]
        ref[LON + HALO : LON + 2 * HALO] = ref[HALO : 2 * HALO]

    arrive = pltpu.make_async_copy(state_far, state_ref, near.at[11])
    arrive.start()
    for fetch in fetches:
        fetch.start()
    arrive.wait()
    x32[...] = state_ref[...].astype(F32).reshape(C * LON, LAT)
    for i in (0, 1, 2, 13, 14, 15):
        xa[HALO + i] = column(x32, i).astype(BF)
    if remote:
        pl.semaphore_wait(barrier, len(peers))
        x_right, x_left = halo_copies(xa, 0)
        x_left.start()
        x_right.start()
    for i in range(3, 13):
        xa[HALO + i] = column(x32, i).astype(BF)
    for fetch in fetches:
        fetch.wait()
    c32[...] = cot_ref[...].astype(F32).reshape(C * LON, LAT)

    flat_taps[...] = jnp.zeros_like(flat_taps)
    for a in range(TAPS):
        flat_taps[8 * a : 8 * a + TAPS, 0:C] = taps_ref[a]
    rest = flat_taps[...].T[0:C, :]
    high = rest.astype(BF)
    low = (rest - high.astype(F32)).astype(BF)
    kf[...] = matmul(
        jnp.concatenate([high[:, 0:64], low[:, 0:64], high[:, 0:64]], axis=1), spread[...]
    )
    gainb[...] = jnp.broadcast_to(gain_ref[...], (LAT, C)).T
    win_t[...] = (0.5 * win_ref[...].astype(F32)).astype(BF).T
    wout[...] = (0.5 * wout_t[...].astype(F32)).astype(BF).T
    acc_gain[...] = jnp.zeros_like(acc_gain)

    def doubled(columns):
        flat = columns.reshape(-1, LAT)
        return jnp.concatenate([flat, flat], axis=1)

    def field_spectrum(at, count):
        spectrum = matmul(doubled(xa[at : at + count]), field_f[...])
        xh[at : at + count] = spectrum.reshape(count, C, SPEC)

    def grad_spectrum(at, count):
        spectrum = matmul(doubled(ga[at : at + count]), field_g[:, SPEC:])
        gh[at : at + count] = spectrum.reshape(count, C, SPEC)

    def filtered(field, col, flip, inverse, exact):
        def one_tile(tile, carry):
            at = pl.multiple_of(tile * TILE, TILE)
            for half in range(0, SPEC, LAT):
                window = field[pl.ds(col, GROUP + 2 * HALO), pl.ds(at, TILE), half : half + LAT]
                terms = []
                for a in range(TAPS):
                    first = 2 * HALO - a if flip else a
                    lane = a * SPEC + half
                    weight = kf[pl.ds(at, TILE), lane : lane + LAT]
                    terms.append(weight[None] * window[first : first + GROUP])
                total = tree_sum(terms)
                high = total.astype(BF)
                sum_high[:, pl.ds(at, TILE), half : half + LAT] = high
                if exact:
                    low = (total - high.astype(F32)).astype(BF)
                    sum_low[:, pl.ds(at, TILE), half : half + LAT] = low
            return carry

        lax.fori_loop(0, C // TILE, one_tile, 0, unroll=2)
        main = matmul(sum_high[...].reshape(GROUP * C, SPEC), inverse[...])
        both = main[:, 0:LAT] + main[:, LAT:]
        if exact:
            both = both + matmul(sum_low[...].reshape(GROUP * C, SPEC), inverse[:, 0:LAT])
        return both.reshape(GROUP, C, LAT)

    def masks(col):
        return [sea_ref[pl.ds(col + k, 1), :].astype(F32) for k in range(GROUP)]

    def side_by_side(parts):
        return jnp.concatenate([parts[k] for k in range(GROUP)], axis=1)

    def first_cell(col):
        turned = col + LON - GROUP
        return (turned % LON if isinstance(col, int) else lax.rem(turned, LON)) * LAT

    def lanes_of(col):
        return pl.ds(pl.multiple_of(first_cell(col), GROUP * LAT), GROUP * LAT)

    def forward_group(col):
        mixed = filtered(xh, col, False, back_f, True)
        centred = mixed - jnp.mean(mixed, axis=1, keepdims=True)
        variance = jnp.mean(centred * centred, axis=1, keepdims=True)
        inv_scale = lax.rsqrt(variance + 1e-06)
        scaled = centred * inv_scale
        scaled_all[pl.ds(col, GROUP)] = scaled
        inv_all[pl.ds(col, GROUP), :] = inv_scale.reshape(GROUP, LAT)
        normed = side_by_side((scaled * gainb[...][None]).astype(BF))
        mask = masks(col)
        grad_out = side_by_side([(column(c32, col + k) * mask[k]).astype(BF) for k in range(GROUP)])
        where = lanes_of(col)
        norm_all[:, where] = normed
        cot_all[:, where] = grad_out
        for h in range(0, HID, HID_BLOCK):
            for n in range(0, GROUP * LAT, CELL_BLOCK):
                half = matmul(win_t[h : h + HID_BLOCK, :], normed[:, n : n + CELL_BLOCK])
                grad_half = matmul(wout[h : h + HID_BLOCK, :], grad_out[:, n : n + CELL_BLOCK])
                square = half * half
                bent = jnp.tanh(half * (1.5957691216057308 + 0.28541926509040104 * square))
                gate = 1.0 + bent
                hidden = half * gate
                slope = gate + hidden * (1.0 - bent) * (
                    1.5957691216057308 + 0.8562577952712031 * square
                )
                at = pl.ds(pl.multiple_of(first_cell(col) + n, CELL_BLOCK), CELL_BLOCK)
                hid_all[h : h + HID_BLOCK, at] = hidden.astype(BF)
                gp_all[h : h + HID_BLOCK, at] = (grad_half * slope).astype(BF)

    def finish_state(col):
        mask = masks(col)
        branch = matmul(wout_t[...], hid_all[:, lanes_of(col)])
        for k in range(GROUP):
            lane = slice(k * LAT, (k + 1) * LAT)
            at = pl.ds(col + k, C, stride=LON)
            x32[at, :] = mask[k] * (x32[at, :] + branch[:, lane])

    def backward_mlp(col):
        where = lanes_of(col)
        gain = gainb[...]
        grad_normed = matmul(win_ref[...], gp_all[:, where])
        for k in range(GROUP):
            lane = slice(k * LAT, (k + 1) * LAT)
            scaled = scaled_all[col + k]
            grad = grad_normed[:, lane]
            product = grad * scaled
            acc_gain[...] += product
            grad_scaled = grad * gain
            first = jnp.mean(grad_scaled, axis=0, keepdims=True)
            second = jnp.mean(product * gain, axis=0, keepdims=True)
            inv_scale = inv_all[pl.ds(col + k, 1), :]
            grad_conv = (inv_scale * (grad_scaled - first - scaled * second)).astype(BF)
            ga[HALO + col + k] = grad_conv
            spectrum = matmul(doubled(grad_conv), field_g[...])
            gw[col + k] = spectrum[:, 0:SPEC]
            gh[HALO + col + k] = spectrum[:, SPEC:]

    def in_groups(first, last, work):
        def one_group(step, carry):
            work(lax.rem(GROUP + step * GROUP, LON))
            return carry

        lax.fori_loop(first, last, one_group, 0)

    def start(copies):
        for one in copies:
            one.start()

    def wait(copies):
        for one in copies:
            one.wait()

    for at in range(HALO, LON + HALO, GROUP):
        field_spectrum(at, GROUP)
    def filter_grads(first, last):
        def one_tile(tile, carry):
            at = pl.multiple_of(tile * 8, 8)
            for half in range(0, SPEC, LAT):
                totals = [None] * TAPS
                for col in range(0, LON, 8):
                    grads = gw[col : col + 8, pl.ds(at, 8), half : half + LAT]
                    for a in range(TAPS):
                        field = xh[col + a : col + a + 8, pl.ds(at, 8), half : half + LAT]
                        part = jnp.sum(grads * field, axis=0)
                        totals[a] = part if totals[a] is None else totals[a] + part
                for a in range(TAPS):
                    dkf[pl.ds(at, 8), a * SPEC + half : a * SPEC + half + LAT] = totals[a]
            return carry

        lax.fori_loop(first, last, one_tile, 0, unroll=2)

    in_groups(0, 2, forward_group)
    cells = slice(0, LON * LAT // 2)
    acc_out[...] = matmul_nt(cot_all[:, cells], hid_all[:, cells])
    acc_in[...] = matmul_nt(norm_all[:, cells], gp_all[:, cells])
    if remote:
        g_right, g_left = halo_copies(ga, 2)
        x_left.wait()
    else:
        local_halo(xa)
    field_spectrum(LON + HALO, HALO)
    forward_group(LON - GROUP)
    backward_mlp(LON - GROUP)
    if remote:
        g_right.start()
        x_right.wait()
    field_spectrum(0, HALO)
    forward_group(0)

    cells = slice(LON * LAT // 2, LON * LAT)
    acc_out[...] += matmul_nt(cot_all[:, cells], hid_all[:, cells])
    acc_in[...] += matmul_nt(norm_all[:, cells], gp_all[:, cells])
    wide = HID // 2
    for o in range(16):
        at = OWN * o
        stage[o, 0:12, 0:HID] = acc_in[at : at + 12, :]
        stage[o, 12:16, 0:HID] = acc_out[at : at + 4, :]
        stage[o, 0:8, HID:PACKED] = acc_out[at + 4 : at + 12, 0:wide]
        stage[o, 8:16, HID:PACKED] = acc_out[at + 4 : at + 12, wide:HID]
    for o in range(16):
        wsend[o % 2, o // 2] = stage[o].astype(BF)

    if remote:

        def to_slabs(slab, base):
            return [
                copy(slab.at[lon], slab.at[lon], base + d, {"lon": other})
                for d, other in enumerate(slabs)
            ]

        def to_owners(source, target, base):
            return [
                copy(source.at[other], target.at[d], base + d, {"sample": 2 * other + core})
                for d, other in enumerate(owners)
            ]

        def w_core():
            return [copy(wsend.at[1 - core], wcore, 4, partner)]

        def w_own():
            return to_owners(wmid, wparts, 5)

        def w_all():
            return to_slabs(wslab, 12)

        def k_core():
            return [copy(ksend.at[1 - core], kcore, 19, partner)]

        def k_own():
            return to_owners(kmid, kparts, 20)

        def k_all():
            return to_slabs(kslab, 27)

        start(w_core())
    backward_mlp(0)
    if remote:
        g_left.start()
    in_groups(0, 1, backward_mlp)
    if remote:
        wait(w_core())
        wmid[...] = (wsend[core].astype(F32) + wcore[...].astype(F32)).astype(BF)
        start(w_own())
    in_groups(1, 2, backward_mlp)
    filter_grads(0, C // 8)

    lanes = lax.broadcasted_iota(jnp.int32, (C, LAT), 1)
    total = jnp.where(lanes == TAPS * TAPS, jnp.sum(acc_gain[...], axis=1, keepdims=True), 0.0)
    for a in range(TAPS):
        part = dkf[:, a * SPEC : (a + 1) * SPEC]
        high = part.astype(BF)
        low = (part - high.astype(F32)).astype(BF)
        both = matmul(high, gather[...])
        found = both[:, 0:LAT] + both[:, LAT:] + matmul(low, gather[:, 0:LAT])
        total = total + (pltpu.roll(found, a * TAPS, axis=1) if a else found)
    dks[0, 0:C, :] = total
    dks[1, 0:C, :] = pltpu.roll(total, LAT // 2, axis=1)
    for side in range(2):
        dks[side, C : C + 16, :] = jnp.zeros((16, LAT), F32)
    for o in range(16):
        at = OWN * o
        ksend[o % 2, o // 2] = dks[0, at : at + 8, :] + dks[1, at + 6 : at + 14, :]
    if remote:
        start(k_core())
    in_groups(0, 2, finish_state)
    if remote:
        wait(k_core())
        kmid[...] = ksend[core] + kcore[...]
        start(k_own())
    in_groups(2, 4, finish_state)
    sout_buf[...] = x32[...].reshape(C, LON, LAT).astype(BF)
    leave = [
        pltpu.make_async_copy(sout_buf, sout_ref, near.at[9]),
        pltpu.make_async_copy(gin_buf, gin_ref, near.at[10]),
    ]
    leave[0].start()

    def backward_group(col):
        moved = filtered(gh, col, True, back_b, False)
        mask = masks(col)
        for k in range(GROUP):
            at = pl.ds(col + k, C, stride=LON)
            c32[at, :] = c32[at, :] * mask[k] + moved[k]

    in_groups(0, 1, backward_group)
    if remote:
        wait(w_own())
        held = wmid[owner].astype(F32)
        for d in range(len(owners)):
            held = held + wparts[d].astype(F32)
        wslab[lon] = held.astype(BF)
        start(w_all())
    in_groups(1, 2, backward_group)
    if remote:
        g_right.wait()
    else:
        local_halo(ga)
    grad_spectrum(0, HALO)
    backward_group(0)
    if remote:
        wait(k_own())
        held = kmid[owner]
        for d in range(len(owners)):
            held = held + kparts[d]
        kslab[lon] = held
        start(k_all())
        g_left.wait()
    grad_spectrum(LON + HALO, HALO)
    backward_group(LON - GROUP)
    gin_buf[...] = c32[...].reshape(C, LON, LAT).astype(BF)
    leave[1].start()
    if remote:
        wait(w_all())
        weights = wslab[0].astype(F32)
        for other in range(1, n_lon):
            weights = weights + wslab[other].astype(F32)
        wait(k_all())
        small = kslab[0]
        for other in range(1, n_lon):
            small = small + kslab[other]
    else:
        weights = wsend[0, 0].astype(F32)
        small = ksend[0, 0]
    weights = weights * factor
    small = small * factor
    gwin_ref[...] = weights[0:12, 0:HID]
    gwout_ref[0:4, :] = weights[12:16, 0:HID]
    gwout_ref[4:12, 0:wide] = weights[0:8, HID:PACKED]
    gwout_ref[4:12, wide:HID] = weights[8:16, HID:PACKED]
    kout[0:6, :] = small[0:6, :]
    kout[6:12, :] = pltpu.roll(small, LAT // 2, axis=1)[0:6, :]
    small_t = kout[...].T
    for a in range(TAPS):
        gk_ref[a] = small_t[a * TAPS : (a + 1) * TAPS, 0:OWN]
    gg_ref[...] = small_t[TAPS * TAPS : TAPS * TAPS + 1, 0:OWN]
    for one in leave:
        one.wait()


def deliver(*refs):
    count = len(refs) // 3
    sems = refs[-1]
    sources, targets, held = refs[:count], refs[count : 2 * count], refs[2 * count : 3 * count]
    arrive = [pltpu.make_async_copy(sources[k], held[k], sems.at[0, k]) for k in range(count)]
    leave = [pltpu.make_async_copy(held[k], targets[k], sems.at[1, k]) for k in range(count)]
    for one in arrive:
        one.start()
    for k in range(count):
        arrive[k].wait()
        leave[k].start()
    for one in leave:
        one.wait()


def block(n_lon, n_sample, factor, state, cot, sea, taps, gain, win, wout):
    vmem = pl.BlockSpec(memory_space=pltpu.VMEM)
    far = pl.BlockSpec(memory_space=pltpu.HBM)
    shape = jax.ShapeDtypeStruct
    outs = (
        shape((C, LON, LAT), BF),
        shape((C, LON, LAT), BF),
        shape((OWN, HID), F32),
        shape((OWN, HID), F32),
        shape((TAPS, TAPS, OWN), F32),
        shape((1, OWN), F32),
    )
    scratch = [
        pltpu.VMEM((C, LON, LAT), BF),
        pltpu.VMEM((C, LON, LAT), BF),
        pltpu.VMEM((C, HID), BF),
        pltpu.VMEM((C, HID), BF),
        pltpu.VMEM((3 * 64, TAPS * SPEC), BF),
        pltpu.VMEM((2 * LAT, SPEC), BF),
        pltpu.VMEM((SPEC, 2 * LAT), BF),
        pltpu.VMEM((2 * LAT, 2 * SPEC), BF),
        pltpu.VMEM((SPEC, 2 * LAT), BF),
        pltpu.VMEM((SPEC, 2 * LAT), BF),
        pltpu.VMEM((C * LON, LAT), F32),
        pltpu.VMEM((C * LON, LAT), F32),
        pltpu.VMEM((LON + 2 * HALO, C, LAT), BF),
        pltpu.VMEM((LON + 2 * HALO, C, LAT), BF),
        pltpu.VMEM((LON + 2 * HALO, C, SPEC), F32),
        pltpu.VMEM((LON + 2 * HALO, C, SPEC), F32),
        pltpu.VMEM((LON, C, SPEC), F32),
        pltpu.VMEM((C, TAPS * SPEC), F32),
        pltpu.VMEM((C, TAPS * SPEC), F32),
        pltpu.VMEM((LAT, 2 * LAT), F32),
        pltpu.VMEM((GROUP, C, SPEC), BF),
        pltpu.VMEM((GROUP, C, SPEC), BF),
        pltpu.VMEM((C, LAT), F32),
        pltpu.VMEM((HID, C), BF),
        pltpu.VMEM((HID, C), BF),
        pltpu.VMEM((C, LON * LAT), BF),
        pltpu.VMEM((C, LON * LAT), BF),
        pltpu.VMEM((HID, LON * LAT), BF),
        pltpu.VMEM((HID, LON * LAT), BF),
        pltpu.VMEM((LON, C, LAT), F32),
        pltpu.VMEM((LON, LAT), F32),
        pltpu.VMEM((C, HID), F32),
        pltpu.VMEM((C, HID), F32),
        pltpu.VMEM((C, LAT), F32),
        pltpu.VMEM((2, C + 16, LAT), F32),
        pltpu.VMEM((16, 16, PACKED), F32),
        pltpu.VMEM((2, 8, 16, PACKED), BF),
        pltpu.VMEM((8, 16, PACKED), BF),
        pltpu.VMEM((8, 16, PACKED), BF),
        pltpu.VMEM((7, 16, PACKED), BF),
        pltpu.VMEM((8, 16, PACKED), BF),
        pltpu.VMEM((2, 8, 8, LAT), F32),
        pltpu.VMEM((8, 8, LAT), F32),
        pltpu.VMEM((8, 8, LAT), F32),
        pltpu.VMEM((7, 8, LAT), F32),
        pltpu.VMEM((8, 8, LAT), F32),
        pltpu.VMEM((16, LAT), F32),
        pltpu.VMEM((C, LON, LAT), BF),
        pltpu.VMEM((C, LON, LAT), BF),
        pltpu.SemaphoreType.DMA((34,)),
        pltpu.SemaphoreType.DMA((34,)),
        pltpu.SemaphoreType.DMA((12,)),
    ]
    extra = dict(collective_id=0, has_side_effects=True) if n_lon > 1 else {}
    results = pl.pallas_call(
        functools.partial(kernel_body, n_lon, n_sample, factor),
        out_shape=outs,
        in_specs=[vmem] * 3 + [far] * 10,
        out_specs=(far, far) + (vmem,) * 4,
        scratch_shapes=scratch,
        compiler_params=pltpu.CompilerParams(vmem_limit_bytes=62 * 1024 * 1024, **extra),
    )(
        sea,
        taps.transpose(1, 2, 0),
        gain.reshape(1, C),
        state.reshape(C, LON, LAT),
        cot.reshape(C, LON, LAT),
        win,
        wout.T,
        *spectral_constants(),
    )
    anywhere = pl.BlockSpec(memory_space=pl.ANY)
    return pl.pallas_call(
        deliver,
        out_shape=outs,
        in_specs=[anywhere] * 6,
        out_specs=(anywhere,) * 6,
        scratch_shapes=[pltpu.VMEM(out.shape, out.dtype) for out in outs]
        + [pltpu.SemaphoreType.DMA((2, 6))],
    )(*results)


def solution(mesh):
    n_lon, n_sample = mesh.shape["lon"], mesh.shape["sample"]
    factor = 1.0 / math.sqrt(n_sample * n_lon * LON * LAT)

    def on_device(state, cot, sea, taps, gain, win, wout):
        out = block(n_lon, n_sample, factor, state, cot, sea, taps, gain, win, wout)
        shape = state.shape
        return (
            out[0].reshape(shape),
            out[1].reshape(shape),
            out[2],
            out[3].T,
            out[4].transpose(2, 0, 1),
            out[5].reshape(OWN),
        )

    slab = P("sample", None, "lon", None)
    return jax.shard_map(
        on_device,
        mesh=mesh,
        in_specs=(slab, slab, P("lon", None), P(), P(), P(), P()),
        out_specs=(
            slab,
            slab,
            P("sample", None),
            P(None, "sample"),
            P("sample", None, None),
            P("sample"),
        ),
        check_vma=False,
    )
```
